512 devices in a mesh: lon: 32 (over z_hi, y, core), lat: 16 (over x, z_lo).
Axes of the slice: x: 4, y: 8, z: 8 (z_hi: 2, z_lo: 4; z = z_hi * 4 + z_lo), core: 2. Of those that a mesh axis runs over, the one named last changes fastest.
Arguments:
- potential_warmth_degrees: float32 [8, 1536, 4096], P(None, 'lat', 'lon'), may hold values from -1.8 to 28
- dissolved_salt_content: float32 [8, 1536, 4096], P(None, 'lat', 'lon'), may hold values from 18 to 37
- zonal_edge_current: float32 [8, 1536, 4096], P(None, 'lat', 'lon'), may hold values from -3 to 3
- meridional_edge_current: float32 [8, 1536, 4096], P(None, 'lat', 'lon'), may hold values from -3 to 3
- wet_grid_flag: int32 [8, 1536, 4096], P(None, 'lat', 'lon'), may hold values from 0 to 1, as said below
- zonal_wet_edge_flag: int32 [8, 1536, 4096], P(None, 'lat', 'lon'), may hold values from 0 to 1, as said below
- meridional_wet_edge_flag: int32 [8, 1536, 4096], P(None, 'lat', 'lon'), may hold values from 0 to 1, as said below
- bottom_tier_count: int32 [1536, 4096], P('lat', 'lon'), may hold values from 0 to 8, as said below
- zonal_grid_spacing: float32 [1536, 4096], P('lat', 'lon'), may hold values from 1800 to 7000
- meridional_grid_spacing: float32 [1536, 4096], P('lat', 'lon'), may hold values from 1800 to 7000
Outputs:
- temperature_after: float32 [8, 1536, 4096], P(None, 'lat', 'lon')
- salinity_after: float32 [8, 1536, 4096], P(None, 'lat', 'lon')
- zonal_after: float32 [8, 1536, 4096], P(None, 'lat', 'lon')
- meridional_after: float32 [8, 1536, 4096], P(None, 'lat', 'lon')
The draws below stay inside these ranges and needn't reach their ends.
Inputs may be any that keep to these rules, and one draw needn't show every extreme that they name: wet_grid_flag[k, j, i] is 1 exactly where k < bottom_tier_count[j, i]. zonal_wet_edge_flag is wet_grid_flag times wet_grid_flag of the cell to the east (east of column 4095 is column 0). meridional_wet_edge_flag is wet_grid_flag times wet_grid_flag of the cell to the north; north of row 1535 at column i lies row 1535 at column 4095 - i. `bottom_tier_count`: some column is all land and some column is sea at every level.
All inputs are finite; a program needn't handle non-finite values.
Results may differ from the reference program's by a relative error of at most 0.00002.
Values sent between devices are 32-bit elements; how exact they have to be, the bound alone decides.
No kernel may reach another device: no remote copies, remote signals or barrier semaphores. Data moves between devices by JAX's collectives and lax.ppermute only.
A program may use at most 64 MiB of HBM per device.

```python
import math
import jax
import jax.numpy as jnp

K = 8
NJ = 1536
NI = 4096


def column_levels(key):
    tier_pile = jax.random.randint(key, (NJ, NI), 0, K + 1).astype(jnp.int32)
    tier_pile = tier_pile.at[0, 0].set(0)
    return tier_pile.at[NJ - 1, NI - 1].set(K)


def sea_from_levels(tier_pile):
    level_index = jnp.arange(K).astype(jnp.int32)
    return (level_index[:, None, None] < tier_pile[None]).astype(jnp.int32)


def rough_field(key):
    rough = jax.random.uniform(key, (K, NJ, NI), jnp.float32)
    return rough


def draw_potential_warmth_degrees(key, part):
    key = jax.random.fold_in(key, 11)
    return -1.8 + 29.8 * rough_field(key)


def draw_dissolved_salt_content(key, part):
    key = jax.random.fold_in(key, 12)
    return 18.0 + 19.0 * rough_field(key)


def draw_bottom_tier_count(key, part):
    tier_pile = column_levels(key)
    return tier_pile


def draw_wet_grid_flag(key, part):
    tier_pile = column_levels(key)
    return sea_from_levels(tier_pile)


def draw_zonal_wet_edge_flag(key, part):
    tier_pile = column_levels(key)
    sea_cells = sea_from_levels(tier_pile)
    return sea_cells * jnp.roll(sea_cells, -1, axis=2)


def draw_meridional_wet_edge_flag(key, part):
    tier_pile = column_levels(key)
    sea_cells = sea_from_levels(tier_pile)
    northern = jnp.concatenate([sea_cells[:, 1:, :], sea_cells[:, -1:, ::-1]], axis=1)
    return sea_cells * northern


def shard_levels(own_key, shape, shards, least, largest):
    def one(axis_at, shards_of):
        steps = jax.random.uniform(jax.random.fold_in(jax.random.fold_in(own_key, 6), axis_at), (shards_of,), jnp.float32, least / len(shards), largest / len(shards))
        return jnp.repeat(jnp.exp(steps), shape[axis_at] // shards_of).reshape((-1,) + (1,) * (len(shape) - axis_at - 1))

    level = one(*shards[0])
    for cut in shards[1:]:
        level = level * one(*cut)
    return level


def bell_draw(own_key, extent, spread, limit, shards=(), kind=jnp.bfloat16):
    result = jax.random.normal(own_key, extent, jnp.float32) * spread
    if len(shards) > 0:
        result = shard_levels(own_key, extent, shards, -0.22, 0.18) * result
    return jnp.clip(result, min=-limit, max=limit).astype(kind)


def setup_inputs(seed: int = 0) -> dict:
    arg_keys = jax.random.split(jax.random.key(seed), 11)
    potential_warmth_degrees = draw_potential_warmth_degrees(jax.random.fold_in(arg_keys[10], 71), 0)
    dissolved_salt_content = draw_dissolved_salt_content(jax.random.fold_in(arg_keys[10], 71), 0)
    zonal_edge_current = bell_draw(arg_keys[2], (K, NJ, NI), 0.3, 3.0, ((1, 16), (2, 32)), jnp.float32)
    meridional_edge_current = bell_draw(arg_keys[3], (K, NJ, NI), 0.3, 3.0, ((1, 16), (2, 32)), jnp.float32)
    wet_grid_flag = draw_wet_grid_flag(jax.random.fold_in(arg_keys[10], 71), 0)
    zonal_wet_edge_flag = draw_zonal_wet_edge_flag(jax.random.fold_in(arg_keys[10], 71), 0)
    meridional_wet_edge_flag = draw_meridional_wet_edge_flag(jax.random.fold_in(arg_keys[10], 71), 0)
    bottom_tier_count = draw_bottom_tier_count(jax.random.fold_in(arg_keys[10], 71), 0)
    zonal_grid_spacing = jnp.clip(1800.0 + 5200.0 * jax.random.uniform(arg_keys[8], (NJ, NI), jnp.float32) ** shard_levels(arg_keys[8], (NJ, NI), ((0, 16), (1, 32)), -0.2, 0.2), 1800.0, 7000.0)
    meridional_grid_spacing = jnp.clip(1800.0 + 5200.0 * jax.random.uniform(arg_keys[9], (NJ, NI), jnp.float32) ** shard_levels(arg_keys[9], (NJ, NI), ((0, 16), (1, 32)), -0.2, 0.2), 1800.0, 7000.0)
    return {"potential_warmth_degrees": potential_warmth_degrees, "dissolved_salt_content": dissolved_salt_content, "zonal_edge_current": zonal_edge_current, "meridional_edge_current": meridional_edge_current, "wet_grid_flag": wet_grid_flag, "zonal_wet_edge_flag": zonal_wet_edge_flag, "meridional_wet_edge_flag": meridional_wet_edge_flag, "bottom_tier_count": bottom_tier_count, "zonal_grid_spacing": zonal_grid_spacing, "meridional_grid_spacing": meridional_grid_spacing}


GRAVITY = 9.81
REFERENCE_DENSITY = 1026.0
TIME_STEP = 360.0
LATERAL = 300.0
VERTICAL = 0.001
ROTATION = 7.292e-5


def tier_dimensions(tier_pile):
    index = jnp.arange(tier_pile).astype(jnp.float32)
    tier_depth_extent = 6.0 + 4.0 * index
    depths = 2.0 * index * index + 6.0 * index + 3.0
    spacing = 4.0 * index + 4.0
    return tier_depth_extent, depths, spacing


def sea_density(heat, salt, depths):
    anom_t = heat - 10.0
    anom_s = salt - 35.0
    first = -0.1655 * (1.0 + 0.5 * 0.05952 * anom_t + 1.497e-4 * depths) * anom_t
    second = 0.76554 * (1.0 - 0.5 * 0.00054914 * anom_s - 1.109e-5 * depths) * anom_s
    return first + second - 0.0024341 * anom_t * anom_s


def edge_amounts(potential_warmth_degrees, dissolved_salt_content, zonal_edge_current, meridional_edge_current, zonal_edge_amount, meridional_edge_amount, zonal_grid_spacing, meridional_grid_spacing):
    tier_depth_extent = tier_dimensions(potential_warmth_degrees.shape[0])[0][:, None, None]
    zonal_water_flux = meridional_grid_spacing * tier_depth_extent * zonal_edge_current * zonal_edge_amount
    meridional_water_flux = zonal_grid_spacing * tier_depth_extent * meridional_edge_current * meridional_edge_amount
    zonal_diffusive_coefficient = LATERAL * meridional_grid_spacing * tier_depth_extent / zonal_grid_spacing * zonal_edge_amount
    meridional_diffusive_coefficient = LATERAL * zonal_grid_spacing * tier_depth_extent / meridional_grid_spacing * meridional_edge_amount
    return jnp.concatenate([potential_warmth_degrees, dissolved_salt_content, zonal_water_flux, meridional_water_flux, zonal_diffusive_coefficient, meridional_diffusive_coefficient], axis=0)


def fold_signs(tier_pile):
    base = jnp.array([1.0, 1.0, -1.0, -1.0, 1.0, 1.0], dtype=jnp.float32)
    return jnp.repeat(base, tier_pile)


def centre(field):
    return field[:, 1:-1, 1:-1]


def to_east(field):
    return field[:, 1:-1, 2:]


def to_west(field):
    return field[:, 1:-1, :-2]


def to_north(field):
    return field[:, 2:, 1:-1]


def to_south(field):
    return field[:, :-2, 1:-1]


def south_east(field):
    return field[:, :-2, 2:]


def north_west(field):
    return field[:, 2:, :-2]


def advance(extended, zonal_edge_current, meridional_edge_current, sea_cells, zonal_edge_amount, meridional_edge_amount, bottom_tier_count, zonal_grid_spacing, meridional_grid_spacing, coriolis):
    tier_pile = zonal_edge_current.shape[0]
    tier_depth_extent, depths, spacing = tier_dimensions(tier_pile)
    thick_col = tier_depth_extent[:, None, None]
    spacing_col = spacing[1:, None, None]
    heat_ext, salt_ext, utr_ext, vtr_ext, gx_ext, gy_ext = [extended[number] for number in range(6)]
    density = sea_density(heat_ext, salt_ext, depths[:, None, None])
    weighted = density * thick_col
    pressure = GRAVITY / REFERENCE_DENSITY * (jnp.cumsum(weighted, axis=0) - 0.5 * weighted)
    press_x = -(to_east(pressure) - centre(pressure)) / zonal_grid_spacing
    press_y = -(to_north(pressure) - centre(pressure)) / meridional_grid_spacing
    east_tr = centre(utr_ext)
    north_tr = centre(vtr_ext)
    converge = east_tr - to_west(utr_ext) + north_tr - to_south(vtr_ext)
    upward = -jnp.cumsum(converge[::-1], axis=0)[::-1]
    cell_area = zonal_grid_spacing * meridional_grid_spacing
    level_index = jnp.arange(tier_pile).astype(jnp.int32)
    wet_face = (level_index[:, None, None] < bottom_tier_count[None]).astype(jnp.float32)
    no_flux = jnp.zeros_like(upward[:1])

    def tracer(field_ext):
        field = centre(field_ext)
        flux_east = east_tr * (field + to_east(field_ext)) * 0.5 - centre(gx_ext) * (to_east(field_ext) - field)
        flux_west = to_west(utr_ext) * (to_west(field_ext) + field) * 0.5 - to_west(gx_ext) * (field - to_west(field_ext))
        flux_north = north_tr * (field + to_north(field_ext)) * 0.5 - centre(gy_ext) * (to_north(field_ext) - field)
        flux_south = to_south(vtr_ext) * (to_south(field_ext) + field) * 0.5 - to_south(gy_ext) * (field - to_south(field_ext))
        interior = upward[1:] * (field[:-1] + field[1:]) * 0.5 - VERTICAL * cell_area * (field[:-1] - field[1:]) / spacing_col * wet_face[1:]
        vertical = jnp.concatenate([upward[:1] * field[:1], interior, no_flux], axis=0)
        net_flux = flux_east - flux_west + flux_north - flux_south + vertical[:-1] - vertical[1:]
        return (field - TIME_STEP * net_flux / (cell_area * thick_col)) * sea_cells

    def viscous(velocity, face):
        interior = VERTICAL * (velocity[:-1] - velocity[1:]) / spacing_col * face[:-1] * face[1:]
        stress = jnp.concatenate([no_flux, interior, no_flux], axis=0)
        return (stress[:-1] - stress[1:]) / thick_col

    coriolis_col = coriolis[:, None]
    cor_u = coriolis_col * (north_tr + to_east(vtr_ext) + to_south(vtr_ext) + south_east(vtr_ext)) / (4.0 * zonal_grid_spacing * thick_col)
    cor_v = -coriolis_col * (east_tr + to_west(utr_ext) + to_north(utr_ext) + north_west(utr_ext)) / (4.0 * meridional_grid_spacing * thick_col)
    zonal_after = (zonal_edge_current + TIME_STEP * (press_x + cor_u + viscous(zonal_edge_current, zonal_edge_amount))) * zonal_edge_amount
    meridional_after = (meridional_edge_current + TIME_STEP * (press_y + cor_v + viscous(meridional_edge_current, meridional_edge_amount))) * meridional_edge_amount
    return tracer(heat_ext), tracer(salt_ext), zonal_after, meridional_after


def coriolis_rows(first_row, meridional_lines, total_rows):
    global_row = first_row + jnp.arange(meridional_lines).astype(jnp.float32)
    latitude = 10.0 + 78.0 * (global_row + 0.5) / total_rows
    return 2.0 * ROTATION * jnp.sin(latitude * (math.pi / 180.0))


def extend(piled_tiers, signs):
    mirror = signs[:, None, None] * piled_tiers[:, -1:, ::-1]
    meridional_lines = jnp.concatenate([jnp.zeros_like(piled_tiers[:, :1, :]), piled_tiers, mirror], axis=1)
    return jnp.concatenate([meridional_lines[:, :, -1:], meridional_lines, meridional_lines[:, :, :1]], axis=2)


def reference(potential_warmth_degrees, dissolved_salt_content, zonal_edge_current, meridional_edge_current, wet_grid_flag, zonal_wet_edge_flag, meridional_wet_edge_flag, bottom_tier_count, zonal_grid_spacing, meridional_grid_spacing):
    tier_pile = potential_warmth_degrees.shape[0]
    sea_cells = wet_grid_flag.astype(jnp.float32)
    zonal_edge_amount = zonal_wet_edge_flag.astype(jnp.float32)
    meridional_edge_amount = meridional_wet_edge_flag.astype(jnp.float32)
    piled_tiers = edge_amounts(potential_warmth_degrees, dissolved_salt_content, zonal_edge_current, meridional_edge_current, zonal_edge_amount, meridional_edge_amount, zonal_grid_spacing, meridional_grid_spacing)
    extended = extend(piled_tiers, fold_signs(tier_pile))
    extended = extended.reshape(6, tier_pile, extended.shape[1], extended.shape[2])
    coriolis = coriolis_rows(jnp.float32(0.0), NJ, NJ * 1.0)
    return advance(extended, zonal_edge_current, meridional_edge_current, sea_cells, zonal_edge_amount, meridional_edge_amount, bottom_tier_count, zonal_grid_spacing, meridional_grid_spacing, coriolis)
```

```python
import functools
import math

import jax
import jax.numpy as jnp
from jax import lax
from jax.experimental import pallas as pl
from jax.experimental.pallas import tpu as pltpu
from jax.sharding import PartitionSpec as P

GRAVITY = 9.81
REFERENCE_DENSITY = 1026.0
TIME_STEP = 360.0
LATERAL = 300.0
VERTICAL = 0.001
ROTATION = 7.292e-05

LEVELS = 8
LANES = 128
TILE = 8
PACKET = 4 * LEVELS
VMEM = pltpu.MemorySpace.VMEM

THICK = [6.0 + 4.0 * k for k in range(LEVELS)]
DEPTH = [2.0 * k * k + 6.0 * k + 3.0 for k in range(LEVELS)]
SPACING = [4.0 * k + 4.0 for k in range(LEVELS)]


def lane_index(shape):
    return lax.broadcasted_iota(jnp.int32, shape, len(shape) - 1)


def roll_lanes(x, shift):
    return pltpu.roll(x, shift % LANES, x.ndim - 1)


def density(heat, salt, k):
    anom_t = heat - 10.0
    anom_s = salt - 35.0
    by_t = -0.1655 * (1.0 + 0.0001497 * DEPTH[k])
    by_s = 0.76554 * (1.0 - 1.109e-05 * DEPTH[k])
    along_t = by_t + (-0.1655 * 0.5 * 0.05952) * anom_t - 0.0024341 * anom_s
    along_s = by_s - (0.76554 * 0.5 * 0.00054914) * anom_s
    return along_t * anom_t + along_s * anom_s


def row_pack(
    t_low, t_top, s_low, s_top, u_low, u_top, v_top, zf_low, zf_top, mf_top, e1_top, e2_low, e2_top, to_a, to_b
):
    j = lax.axis_index("lat")
    even = j % 2 == 0
    top = j == lax.axis_size("lat") - 1
    last = TILE - 1

    def put(out, fields):
        for number, field in enumerate(fields):
            out[number * LEVELS : (number + 1) * LEVELS, :] = field

    def upward():
        spacing_x, spacing_y = e1_top[last:, :], e2_top[last:, :]
        face = mf_top[:, last, :].astype(jnp.float32)
        return [
            t_top[:, last, :],
            s_top[:, last, :],
            spacing_x * v_top[:, last, :] * face,
            LATERAL * spacing_x / spacing_y * face,
        ]

    def downward():
        flux = e2_low[:1, :] * u_low[:, 0, :] * zf_low[:, 0, :].astype(jnp.float32)
        return [t_low[:, 0, :], s_low[:, 0, :], flux, jnp.zeros_like(flux)]

    @pl.when(even)
    def _():
        put(to_a, upward())
        put(to_b, downward())

    @pl.when(jnp.logical_not(even))
    def _():
        put(to_a, downward())

    @pl.when(jnp.logical_not(even) & jnp.logical_not(top))
    def _():
        put(to_b, upward())

    @pl.when(top)
    def _():
        flux = e2_top[last:, :] * u_top[:, last, :] * zf_top[:, last, :].astype(jnp.float32)
        rows = jnp.concatenate([t_top[:, last, :], s_top[:, last, :], -flux], axis=0)
        shape = (LANES, LANES)
        mirror = lane_index(shape) + lax.broadcasted_iota(jnp.int32, shape, 0) == LANES - 1
        to_b[: 3 * LEVELS, :] = lax.dot(
            rows, mirror.astype(jnp.float32), precision=lax.Precision.HIGHEST, preferred_element_type=jnp.float32
        )
        to_b[3 * LEVELS :, :] = jnp.zeros((LEVELS, LANES), jnp.float32)


def column_pack(t, s, u, v, zf, mf, e1, e2, to_east, to_west, coriolis, packed):
    lines = t.shape[1]
    lane = lane_index((TILE, LANES))
    first_row = lax.axis_index("lat") * lines
    total_rows = lines * lax.axis_size("lat")
    packed[...] = jnp.zeros_like(packed)

    def tile(r, _):
        rows = pl.ds(pl.multiple_of(r * TILE, TILE), TILE)
        spacing_x, spacing_y = e1[rows, :], e2[rows, :]
        ratio = LATERAL * spacing_y / spacing_x
        fields = [jnp.zeros((TILE, LANES), jnp.float32) for _ in range(7)]

        def keep(number, k, x, source):
            target = number * LEVELS + k
            fields[number] = jnp.where(lane == target, roll_lanes(x, target - source), fields[number])

        for k in range(LEVELS):
            heat, salt = t[k, rows, :], s[k, rows, :]
            face = zf[k, rows, :].astype(jnp.float32)
            keep(0, k, heat, LANES - 1)
            keep(1, k, salt, LANES - 1)
            keep(2, k, spacing_y * u[k, rows, :] * face, LANES - 1)
            keep(3, k, ratio * face, LANES - 1)
            keep(4, k, heat, 0)
            keep(5, k, salt, 0)
            keep(6, k, spacing_x * v[k, rows, :] * mf[k, rows, :].astype(jnp.float32), 0)
        total = fields[0]
        for field in fields[1:]:
            total = total + field
        packed[rows, :] = total
        row = (first_row + r * TILE + lax.broadcasted_iota(jnp.int32, (TILE, LANES), 0)).astype(jnp.float32)
        latitude = 10.0 + 78.0 * (row + 0.5) / total_rows
        coriolis[rows, :] = 2.0 * ROTATION * jnp.sin(latitude * (math.pi / 180.0))
        return 0

    lax.fori_loop(0, lines // TILE, tile, 0)
    turned = packed[...].T
    to_east[...] = turned[:PACKET]
    to_west[...] = turned[PACKET : 2 * PACKET]


def corner_pack(from_a, from_b, to_east, to_west, to_a, to_b):
    even_j = lax.axis_index("lat") % 2 == 0
    even_i = lax.axis_index("lon") % 2 == 0
    shape = (PACKET, LANES)
    row = lax.broadcasted_iota(jnp.int32, shape, 0)
    corner = (lane_index(shape) == 96) & (row >= 2 * LEVELS) & (row < 3 * LEVELS)
    first, second = from_a[...], from_b[...]
    north = jnp.where(even_j, first, second)
    south = jnp.where(even_j, second, first)
    east = jnp.where(corner, roll_lanes(north, 96 - (LANES - 1)), to_east[...])
    west = jnp.where(corner, roll_lanes(south, 96), to_west[...])
    to_a[...] = jnp.where(even_i, east, west)
    to_b[...] = jnp.where(even_i, west, east)


def step(
    t, s, u, v, zf, mf, count, e1, e2, coriolis, own_west, lat_a, lat_b, lon_a, lon_b,
    t_out, s_out, u_out, v_out,
    t_ext, s_ext, p_ext, a_ext, b_ext, u_ext, v_ext, ft_ext, fs_ext, turned, sides,
):
    lines = t.shape[1]
    tiles = lines // TILE
    south_row, north_row = TILE - 1, TILE + lines
    even_j = lax.axis_index("lat") % 2 == 0
    even_i = lax.axis_index("lon") % 2 == 0

    def pick(ref_true, ref_false, flag, number):
        rows = slice(number * LEVELS, (number + 1) * LEVELS)
        return jnp.where(flag, ref_true[rows, :], ref_false[rows, :])

    north = [pick(lat_a, lat_b, even_j, n) for n in range(3)]
    south = [pick(lat_b, lat_a, even_j, n) for n in range(4)]
    east = [pick(lon_a, lon_b, even_i, n) for n in range(3)]
    west = [pick(lon_b, lon_a, even_i, n) for n in range(4)]
    lane = lane_index((TILE, LANES))
    at_first, at_last = lane == 0, lane == LANES - 1

    t_ext[:, north_row, :] = north[0]
    s_ext[:, north_row, :] = north[1]
    a_ext[:, north_row, :] = north[2] + jnp.where(at_first, roll_lanes(west[2], -96), roll_lanes(north[2], 1))
    b_ext[:, south_row, :] = south[2] + jnp.where(at_last, roll_lanes(east[2], 127 - 96), roll_lanes(south[2], -1))
    v_ext[:, south_row, :] = south[2]
    here, there = 0.5 * south[2] + south[3], 0.5 * south[2] - south[3]
    ft_ext[:, south_row, :] = here * south[0] + there * t[:, 0, :]
    fs_ext[:, south_row, :] = here * south[1] + there * s[:, 0, :]

    here, there = 0.5 * west[2] + west[3], 0.5 * west[2] - west[3]
    turned[...] = jnp.zeros_like(turned)
    turned[0:8, :] = here * west[0] + there * own_west[0:8, :]
    turned[8:16, :] = here * west[1] + there * own_west[8:16, :]
    turned[16:24, :] = west[2]
    for n in range(3):
        turned[24 + 8 * n : 32 + 8 * n, :] = east[n]
    head = jnp.zeros((1, LANES), jnp.float32)
    for k in range(LEVELS):
        half = (0.5 * THICK[k]) * density(turned[24 + k : 25 + k, :], turned[32 + k : 33 + k, :], k)
        turned[48 + k : 49 + k, :] = head + half
        head = head + 2.0 * half
    sides[...] = turned[...].T

    def extend(r, _):
        source = pl.ds(pl.multiple_of(r * TILE, TILE), TILE)
        target = pl.ds(pl.multiple_of(r * TILE + TILE, TILE), TILE)
        for k in range(LEVELS):
            t_ext[k, target, :] = t[k, source, :]
            s_ext[k, target, :] = s[k, source, :]
        return 0

    lax.fori_loop(0, tiles, extend, 0)

    def heads(r, _):
        rows = pl.ds(pl.multiple_of(r * TILE + TILE, TILE), TILE)
        head = jnp.zeros((TILE, LANES), jnp.float32)
        for k in range(LEVELS):
            half = (0.5 * THICK[k]) * density(t_ext[k, rows, :], s_ext[k, rows, :], k)
            p_ext[k, rows, :] = head + half
            head = head + 2.0 * half
        return 0

    lax.fori_loop(0, tiles + 1, heads, 0)

    def from_west(x, side, number):
        return jnp.where(at_first, roll_lanes(side, -number), roll_lanes(x, 1))

    def from_east(x, side, number):
        return jnp.where(at_last, roll_lanes(side, LANES - 1 - number), roll_lanes(x, -1))

    def faces(r, _):
        source = pl.ds(pl.multiple_of(r * TILE, TILE), TILE)
        rows = pl.ds(pl.multiple_of(r * TILE + TILE, TILE), TILE)
        above = pl.ds(r * TILE + TILE + 1, TILE)
        spacing_x, spacing_y = e1[source, :], e2[source, :]
        ratio = LATERAL * spacing_x / spacing_y
        side = sides[source, :]
        for k in range(LEVELS):
            flux_x = spacing_y * u[k, source, :] * zf[k, source, :].astype(jnp.float32)
            u_ext[k, rows, :] = flux_x
            a_ext[k, rows, :] = flux_x + from_west(flux_x, side, 16 + k)
            face = mf[k, source, :].astype(jnp.float32)
            flux_y = spacing_x * v[k, source, :] * face
            v_ext[k, rows, :] = flux_y
            b_ext[k, rows, :] = flux_y + from_east(flux_y, side, 40 + k)
            here, there = 0.5 * flux_y + ratio * face, 0.5 * flux_y - ratio * face
            ft_ext[k, rows, :] = here * t_ext[k, rows, :] + there * t_ext[k, above, :]
            fs_ext[k, rows, :] = here * s_ext[k, rows, :] + there * s_ext[k, above, :]
        return 0

    lax.fori_loop(0, tiles, faces, 0)

    def update(r, _):
        source = pl.ds(pl.multiple_of(r * TILE, TILE), TILE)
        rows = pl.ds(pl.multiple_of(r * TILE + TILE, TILE), TILE)
        above = pl.ds(r * TILE + TILE + 1, TILE)
        below = pl.ds(r * TILE + TILE - 1, TILE)
        spacing_x, spacing_y = e1[source, :], e2[source, :]
        side = sides[source, :]
        levels = count[source, :]
        inverse_x, inverse_y = 1.0 / spacing_x, 1.0 / spacing_y
        ratio = LATERAL * spacing_y * inverse_x
        area = spacing_x * spacing_y
        per_area = TIME_STEP * inverse_x * inverse_y
        turn = (0.25 * TIME_STEP) * coriolis[source, :]
        turn_x, turn_y = turn * inverse_x, turn * inverse_y
        push = -TIME_STEP * GRAVITY / REFERENCE_DENSITY
        push_x, push_y = push * inverse_x, push * inverse_y
        zero = jnp.zeros((TILE, LANES), jnp.float32)
        upward, t_below, s_below, u_below, v_below = zero, zero, zero, zero, zero
        for k in reversed(range(LEVELS)):
            heat, salt = t[k, source, :], s[k, source, :]
            flux_x, flux_y = u_ext[k, rows, :], v_ext[k, rows, :]
            face_x, face_y = zf[k, source, :].astype(jnp.float32), mf[k, source, :].astype(jnp.float32)
            both_x, both_y = a_ext[k, rows, :], b_ext[k, rows, :]
            wet = levels > k
            spread = ratio * face_x
            here, there = 0.5 * flux_x + spread, 0.5 * flux_x - spread
            t_east = here * heat + there * from_east(heat, side, 24 + k)
            s_east = here * salt + there * from_east(salt, side, 32 + k)
            t_net = t_east - from_west(t_east, side, k) + ft_ext[k, rows, :] - ft_ext[k, below, :]
            s_net = s_east - from_west(s_east, side, 8 + k) + fs_ext[k, rows, :] - fs_ext[k, below, :]
            converge = 2.0 * flux_x - both_x + flux_y - v_ext[k, below, :]
            upward = upward - THICK[k] * converge
            if k > 0:
                mix = jnp.where(wet, (VERTICAL / SPACING[k]) * area, 0.0)
                upper, lower = 0.5 * upward - mix, 0.5 * upward + mix
                t_above = upper * t[k - 1, source, :] + lower * heat
                s_above = upper * s[k - 1, source, :] + lower * salt
            else:
                t_above, s_above = upward * heat, upward * salt
            t_net = t_net + (t_above - t_below) * (1.0 / THICK[k])
            s_net = s_net + (s_above - s_below) * (1.0 / THICK[k])
            t_below, s_below = t_above, s_above
            t_out[k, source, :] = jnp.where(wet, heat - per_area * t_net, 0.0)
            s_out[k, source, :] = jnp.where(wet, salt - per_area * s_net, 0.0)
            zonal, meridional = u[k, source, :], v[k, source, :]
            if k > 0:
                scale = VERTICAL / SPACING[k]
                u_above = scale * (u[k - 1, source, :] - zonal) * (face_x * zf[k - 1, source, :].astype(jnp.float32))
                v_above = scale * (v[k - 1, source, :] - meridional) * (face_y * mf[k - 1, source, :].astype(jnp.float32))
            else:
                u_above, v_above = zero, zero
            head = p_ext[k, rows, :]
            slope_x = from_east(head, side, 48 + k) - head
            slope_y = p_ext[k, above, :] - head
            share = TIME_STEP / THICK[k]
            u_out[k, source, :] = (
                zonal + push_x * slope_x + turn_x * (both_y + b_ext[k, below, :]) + share * (u_above - u_below)
            ) * face_x
            v_out[k, source, :] = (
                meridional + push_y * slope_y - turn_y * (both_x + a_ext[k, above, :]) + share * (v_above - v_below)
            ) * face_y
            u_below, v_below = u_above, v_above
        return 0

    lax.fori_loop(0, tiles, update, 0)


def whole(n):
    return [pl.BlockSpec(memory_space=VMEM)] * n


def per_device(
    potential_warmth_degrees,
    dissolved_salt_content,
    zonal_edge_current,
    meridional_edge_current,
    wet_grid_flag,
    zonal_wet_edge_flag,
    meridional_wet_edge_flag,
    bottom_tier_count,
    zonal_grid_spacing,
    meridional_grid_spacing,
):
    t, s, u, v = potential_warmth_degrees, dissolved_salt_content, zonal_edge_current, meridional_edge_current
    zf, mf, e1, e2 = zonal_wet_edge_flag, meridional_wet_edge_flag, zonal_grid_spacing, meridional_grid_spacing
    lines = t.shape[1]
    lons, lats = lax.axis_size("lon"), lax.axis_size("lat")
    f32 = jnp.float32
    params = pltpu.CompilerParams(vmem_limit_bytes=24 * 1024 * 1024)
    packet = jax.ShapeDtypeStruct((PACKET, LANES), f32)
    field = jax.ShapeDtypeStruct(t.shape, f32)

    low3 = pl.BlockSpec((LEVELS, TILE, LANES), lambda g: (0, 0, 0))
    top3 = pl.BlockSpec((LEVELS, TILE, LANES), lambda g: (0, lines // TILE - 1, 0))
    low2 = pl.BlockSpec((TILE, LANES), lambda g: (0, 0))
    top2 = pl.BlockSpec((TILE, LANES), lambda g: (lines // TILE - 1, 0))
    out2 = pl.BlockSpec((PACKET, LANES), lambda g: (0, 0))
    lat_to_a, lat_to_b = pl.pallas_call(
        row_pack,
        grid=(1,),
        in_specs=[low3, top3, low3, top3, low3, top3, top3, low3, top3, top3, top2, low2, top2],
        out_specs=[out2, out2],
        out_shape=[packet, packet],
        compiler_params=params,
        name="row_pack",
    )(t, t, s, s, u, u, v, zf, zf, mf, e1, e2, e2)

    pairs_a = [(j, j ^ 1) for j in range(lats)]
    pairs_b = []
    for i in range(lons):
        for j in range(1, lats):
            other = (lons - 1 - i) * lats + j if j == lats - 1 else i * lats + (j + 1 if j % 2 else j - 1)
            pairs_b.append((i * lats + j, other))
    lat_a = lax.ppermute(lat_to_a, "lat", pairs_a)
    lat_b = lax.ppermute(lat_to_b, ("lon", "lat"), pairs_b)

    to_east, to_west, coriolis = pl.pallas_call(
        column_pack,
        in_specs=whole(8),
        out_specs=whole(3),
        out_shape=[packet, packet, jax.ShapeDtypeStruct(e1.shape, f32)],
        scratch_shapes=[VMEM((LANES, LANES), f32)],
        compiler_params=params,
        name="column_pack",
    )(t, s, u, v, zf, mf, e1, e2)

    lon_to_a, lon_to_b = pl.pallas_call(
        corner_pack,
        in_specs=whole(4),
        out_specs=whole(2),
        out_shape=[packet, packet],
        compiler_params=params,
        name="corner_pack",
    )(lat_a, lat_b, to_east, to_west)
    lon_b = lax.ppermute(lon_to_b, "lon", [(i, (i + 1 if i % 2 else i - 1) % lons) for i in range(lons)])
    lon_a = lax.ppermute(lon_to_a, "lon", [(i, i ^ 1) for i in range(lons)])

    extended = VMEM((LEVELS, lines + 2 * TILE, LANES), f32)
    square = VMEM((LANES, LANES), f32)
    return pl.pallas_call(
        step,
        in_specs=whole(15),
        out_specs=whole(4),
        out_shape=[field] * 4,
        scratch_shapes=[extended] * 9 + [square] * 2,
        compiler_params=params,
        name="step",
    )(t, s, u, v, zf, mf, bottom_tier_count, e1, e2, coriolis, to_west, lat_a, lat_b, lon_a, lon_b)


def solution(mesh):
    deep, flat = P(None, "lat", "lon"), P("lat", "lon")
    return jax.shard_map(
        per_device,
        mesh=mesh,
        in_specs=(deep,) * 7 + (flat,) * 3,
        out_specs=(deep,) * 4,
        check_vma=False,
    )
```

```python
import functools
import math

import jax
import jax.numpy as jnp
from jax import lax
from jax.experimental import pallas as pl
from jax.experimental.pallas import tpu as pltpu
from jax.sharding import PartitionSpec as P

GRAVITY = 9.81
REFERENCE_DENSITY = 1026.0
TIME_STEP = 360.0
LATERAL = 300.0
VERTICAL = 0.001
ROTATION = 7.292e-05

LEVELS = 8
LANES = 128
TILE = 8
PACKET = 4 * LEVELS
VMEM = pltpu.MemorySpace.VMEM

THICK = [6.0 + 4.0 * k for k in range(LEVELS)]
DEPTH = [2.0 * k * k + 6.0 * k + 3.0 for k in range(LEVELS)]
SPACING = [4.0 * k + 4.0 for k in range(LEVELS)]


def lane_index(shape):
    return lax.broadcasted_iota(jnp.int32, shape, len(shape) - 1)


def roll_lanes(x, shift):
    return pltpu.roll(x, shift % LANES, x.ndim - 1)


def density(heat, salt, k):
    anom_t = heat - 10.0
    anom_s = salt - 35.0
    by_t = -0.1655 * (1.0 + 0.0001497 * DEPTH[k])
    by_s = 0.76554 * (1.0 - 1.109e-05 * DEPTH[k])
    along_t = by_t + (-0.1655 * 0.5 * 0.05952) * anom_t - 0.0024341 * anom_s
    along_s = by_s - (0.76554 * 0.5 * 0.00054914) * anom_s
    return along_t * anom_t + along_s * anom_s


def row_pack(t, s, u, v, zf, mf, e1, e2, to_a, to_b, deep, flags, flat, arrived):
    j = lax.axis_index("lat")
    even = j % 2 == 0
    top = j == lax.axis_size("lat") - 1
    last = TILE - 1
    low, high = pl.ds(0, TILE), pl.ds(t.shape[1] - TILE, TILE)
    wanted = [(t, low), (t, high), (s, low), (s, high), (u, low), (u, high), (v, high)]
    marks = [(zf, low), (zf, high), (mf, high)]
    sizes = [(e1, high), (e2, high), (e2, low)]
    copies = [pltpu.make_async_copy(ref.at[:, rows, :], deep.at[n], arrived.at[n]) for n, (ref, rows) in enumerate(wanted)]
    copies += [pltpu.make_async_copy(ref.at[:, rows, :], flags.at[n], arrived.at[7 + n]) for n, (ref, rows) in enumerate(marks)]
    copies += [pltpu.make_async_copy(ref.at[rows, :], flat.at[n], arrived.at[10 + n]) for n, (ref, rows) in enumerate(sizes)]
    for copy in copies:
        copy.start()
    for copy in copies:
        copy.wait()

    def put(out, fields):
        for number, field in enumerate(fields):
            out[number * LEVELS : (number + 1) * LEVELS, :] = field

    def upward():
        spacing_x, spacing_y = flat[0, last:, :], flat[1, last:, :]
        face = flags[2, :, last, :].astype(jnp.float32)
        return [
            deep[1, :, last, :],
            deep[3, :, last, :],
            spacing_x * deep[6, :, last, :] * face,
            LATERAL * spacing_x / spacing_y * face,
        ]

    def downward():
        flux = flat[2, :1, :] * deep[4, :, 0, :] * flags[0, :, 0, :].astype(jnp.float32)
        return [deep[0, :, 0, :], deep[2, :, 0, :], flux, jnp.zeros_like(flux)]

    @pl.when(even)
    def _():
        put(to_a, upward())
        put(to_b, downward())

    @pl.when(jnp.logical_not(even))
    def _():
        put(to_a, downward())

    @pl.when(jnp.logical_not(even) & jnp.logical_not(top))
    def _():
        put(to_b, upward())

    @pl.when(top)
    def _():
        flux = flat[1, last:, :] * deep[5, :, last, :] * flags[1, :, last, :].astype(jnp.float32)
        rows = jnp.concatenate([deep[1, :, last, :], deep[3, :, last, :], -flux], axis=0)
        shape = (LANES, LANES)
        mirror = lane_index(shape) + lax.broadcasted_iota(jnp.int32, shape, 0) == LANES - 1
        to_b[: 3 * LEVELS, :] = lax.dot(
            rows, mirror.astype(jnp.float32), precision=lax.Precision.HIGHEST, preferred_element_type=jnp.float32
        )
        to_b[3 * LEVELS :, :] = jnp.zeros((LEVELS, LANES), jnp.float32)


def column_pack(t, s, u, v, zf, mf, e1, e2, to_east, to_west, coriolis, packed):
    lines = t.shape[1]
    lane = lane_index((TILE, LANES))
    first_row = lax.axis_index("lat") * lines
    total_rows = lines * lax.axis_size("lat")
    packed[...] = jnp.zeros_like(packed)

    def tile(r, _):
        rows = pl.ds(pl.multiple_of(r * TILE, TILE), TILE)
        spacing_x, spacing_y = e1[rows, :], e2[rows, :]
        ratio = LATERAL * spacing_y / spacing_x
        fields = [jnp.zeros((TILE, LANES), jnp.float32) for _ in range(7)]

        def keep(number, k, x, source):
            target = number * LEVELS + k
            fields[number] = jnp.where(lane == target, roll_lanes(x, target - source), fields[number])

        for k in range(LEVELS):
            heat, salt = t[k, rows, :], s[k, rows, :]
            face = zf[k, rows, :].astype(jnp.float32)
            keep(0, k, heat, LANES - 1)
            keep(1, k, salt, LANES - 1)
            keep(2, k, spacing_y * u[k, rows, :] * face, LANES - 1)
            keep(3, k, ratio * face, LANES - 1)
            keep(4, k, heat, 0)
            keep(5, k, salt, 0)
            keep(6, k, spacing_x * v[k, rows, :] * mf[k, rows, :].astype(jnp.float32), 0)
        total = fields[0]
        for field in fields[1:]:
            total = total + field
        packed[rows, :] = total
        row = (first_row + r * TILE + lax.broadcasted_iota(jnp.int32, (TILE, LANES), 0)).astype(jnp.float32)
        latitude = 10.0 + 78.0 * (row + 0.5) / total_rows
        coriolis[rows, :] = 2.0 * ROTATION * jnp.sin(latitude * (math.pi / 180.0))
        return 0

    lax.fori_loop(0, lines // TILE, tile, 0)
    turned = packed[...].T
    to_east[...] = turned[:PACKET]
    to_west[...] = turned[PACKET : 2 * PACKET]


def corner_pack(from_a, from_b, to_east, to_west, to_a, to_b):
    even_j = lax.axis_index("lat") % 2 == 0
    even_i = lax.axis_index("lon") % 2 == 0
    shape = (PACKET, LANES)
    row = lax.broadcasted_iota(jnp.int32, shape, 0)
    corner = (lane_index(shape) == 96) & (row >= 2 * LEVELS) & (row < 3 * LEVELS)
    first, second = from_a[...], from_b[...]
    north = jnp.where(even_j, first, second)
    south = jnp.where(even_j, second, first)
    east = jnp.where(corner, roll_lanes(north, 96 - (LANES - 1)), to_east[...])
    west = jnp.where(corner, roll_lanes(south, 96), to_west[...])
    to_a[...] = jnp.where(even_i, east, west)
    to_b[...] = jnp.where(even_i, west, east)


def step(
    t, s, u, v, zf, mf, count, e1, e2, coriolis, own_west, lat_a, lat_b, lon_a, lon_b,
    t_out, s_out, u_out, v_out,
    t_ext, s_ext, p_ext, a_ext, b_ext, u_ext, v_ext, ft_ext, fs_ext, turned, sides,
):
    lines = t.shape[1]
    tiles = lines // TILE
    south_row, north_row = TILE - 1, TILE + lines
    even_j = lax.axis_index("lat") % 2 == 0
    even_i = lax.axis_index("lon") % 2 == 0

    def pick(ref_true, ref_false, flag, number):
        rows = slice(number * LEVELS, (number + 1) * LEVELS)
        return jnp.where(flag, ref_true[rows, :], ref_false[rows, :])

    north = [pick(lat_a, lat_b, even_j, n) for n in range(3)]
    south = [pick(lat_b, lat_a, even_j, n) for n in range(4)]
    east = [pick(lon_a, lon_b, even_i, n) for n in range(3)]
    west = [pick(lon_b, lon_a, even_i, n) for n in range(4)]
    lane = lane_index((TILE, LANES))
    at_first, at_last = lane == 0, lane == LANES - 1

    t_ext[:, north_row, :] = north[0]
    s_ext[:, north_row, :] = north[1]
    a_ext[:, north_row, :] = north[2] + jnp.where(at_first, roll_lanes(west[2], -96), roll_lanes(north[2], 1))
    b_ext[:, south_row, :] = south[2] + jnp.where(at_last, roll_lanes(east[2], 127 - 96), roll_lanes(south[2], -1))
    v_ext[:, south_row, :] = south[2]
    here, there = 0.5 * south[2] + south[3], 0.5 * south[2] - south[3]
    ft_ext[:, south_row, :] = here * south[0] + there * t[:, 0, :]
    fs_ext[:, south_row, :] = here * south[1] + there * s[:, 0, :]

    here, there = 0.5 * west[2] + west[3], 0.5 * west[2] - west[3]
    turned[...] = jnp.zeros_like(turned)
    turned[0:8, :] = here * west[0] + there * own_west[0:8, :]
    turned[8:16, :] = here * west[1] + there * own_west[8:16, :]
    turned[16:24, :] = west[2]
    for n in range(3):
        turned[24 + 8 * n : 32 + 8 * n, :] = east[n]
    head = jnp.zeros((1, LANES), jnp.float32)
    for k in range(LEVELS):
        half = (0.5 * THICK[k]) * density(turned[24 + k : 25 + k, :], turned[32 + k : 33 + k, :], k)
        turned[48 + k : 49 + k, :] = head + half
        head = head + 2.0 * half
    sides[...] = turned[...].T

    def extend(r, _):
        source = pl.ds(pl.multiple_of(r * TILE, TILE), TILE)
        target = pl.ds(pl.multiple_of(r * TILE + TILE, TILE), TILE)
        for k in range(LEVELS):
            t_ext[k, target, :] = t[k, source, :]
            s_ext[k, target, :] = s[k, source, :]
        return 0

    lax.fori_loop(0, tiles, extend, 0)

    def heads(r, _):
        rows = pl.ds(pl.multiple_of(r * TILE + TILE, TILE), TILE)
        head = jnp.zeros((TILE, LANES), jnp.float32)
        for k in range(LEVELS):
            half = (0.5 * THICK[k]) * density(t_ext[k, rows, :], s_ext[k, rows, :], k)
            p_ext[k, rows, :] = head + half
            head = head + 2.0 * half
        return 0

    lax.fori_loop(0, tiles + 1, heads, 0)

    def from_west(x, side, number):
        return jnp.where(at_first, roll_lanes(side, -number), roll_lanes(x, 1))

    def from_east(x, side, number):
        return jnp.where(at_last, roll_lanes(side, LANES - 1 - number), roll_lanes(x, -1))

    def faces(r, _):
        source = pl.ds(pl.multiple_of(r * TILE, TILE), TILE)
        rows = pl.ds(pl.multiple_of(r * TILE + TILE, TILE), TILE)
        above = pl.ds(r * TILE + TILE + 1, TILE)
        spacing_x, spacing_y = e1[source, :], e2[source, :]
        ratio = LATERAL * spacing_x / spacing_y
        side = sides[source, :]
        for k in range(LEVELS):
            flux_x = spacing_y * u[k, source, :] * zf[k, source, :].astype(jnp.float32)
            u_ext[k, rows, :] = flux_x
            a_ext[k, rows, :] = flux_x + from_west(flux_x, side, 16 + k)
            face = mf[k, source, :].astype(jnp.float32)
            flux_y = spacing_x * v[k, source, :] * face
            v_ext[k, rows, :] = flux_y
            b_ext[k, rows, :] = flux_y + from_east(flux_y, side, 40 + k)
            here, there = 0.5 * flux_y + ratio * face, 0.5 * flux_y - ratio * face
            ft_ext[k, rows, :] = here * t_ext[k, rows, :] + there * t_ext[k, above, :]
            fs_ext[k, rows, :] = here * s_ext[k, rows, :] + there * s_ext[k, above, :]
        return 0

    lax.fori_loop(0, tiles, faces, 0)

    def update(r, _):
        source = pl.ds(pl.multiple_of(r * TILE, TILE), TILE)
        rows = pl.ds(pl.multiple_of(r * TILE + TILE, TILE), TILE)
        above = pl.ds(r * TILE + TILE + 1, TILE)
        below = pl.ds(r * TILE + TILE - 1, TILE)
        spacing_x, spacing_y = e1[source, :], e2[source, :]
        side = sides[source, :]
        levels = count[source, :]
        inverse_x, inverse_y = 1.0 / spacing_x, 1.0 / spacing_y
        ratio = LATERAL * spacing_y * inverse_x
        area = spacing_x * spacing_y
        per_area = TIME_STEP * inverse_x * inverse_y
        turn = (0.25 * TIME_STEP) * coriolis[source, :]
        turn_x, turn_y = turn * inverse_x, turn * inverse_y
        push = -TIME_STEP * GRAVITY / REFERENCE_DENSITY
        push_x, push_y = push * inverse_x, push * inverse_y
        zero = jnp.zeros((TILE, LANES), jnp.float32)
        upward, t_below, s_below, u_below, v_below = zero, zero, zero, zero, zero
        for k in reversed(range(LEVELS)):
            heat, salt = t[k, source, :], s[k, source, :]
            flux_x, flux_y = u_ext[k, rows, :], v_ext[k, rows, :]
            face_x, face_y = zf[k, source, :].astype(jnp.float32), mf[k, source, :].astype(jnp.float32)
            both_x, both_y = a_ext[k, rows, :], b_ext[k, rows, :]
            wet = levels > k
            spread = ratio * face_x
            here, there = 0.5 * flux_x + spread, 0.5 * flux_x - spread
            t_east = here * heat + there * from_east(heat, side, 24 + k)
            s_east = here * salt + there * from_east(salt, side, 32 + k)
            t_net = t_east - from_west(t_east, side, k) + ft_ext[k, rows, :] - ft_ext[k, below, :]
            s_net = s_east - from_west(s_east, side, 8 + k) + fs_ext[k, rows, :] - fs_ext[k, below, :]
            converge = 2.0 * flux_x - both_x + flux_y - v_ext[k, below, :]
            upward = upward - THICK[k] * converge
            if k > 0:
                mix = jnp.where(wet, (VERTICAL / SPACING[k]) * area, 0.0)
                upper, lower = 0.5 * upward - mix, 0.5 * upward + mix
                t_above = upper * t[k - 1, source, :] + lower * heat
                s_above = upper * s[k - 1, source, :] + lower * salt
            else:
                t_above, s_above = upward * heat, upward * salt
            t_net = t_net + (t_above - t_below) * (1.0 / THICK[k])
            s_net = s_net + (s_above - s_below) * (1.0 / THICK[k])
            t_below, s_below = t_above, s_above
            t_out[k, source, :] = jnp.where(wet, heat - per_area * t_net, 0.0)
            s_out[k, source, :] = jnp.where(wet, salt - per_area * s_net, 0.0)
            zonal, meridional = u[k, source, :], v[k, source, :]
            if k > 0:
                scale = VERTICAL / SPACING[k]
                u_above = scale * (u[k - 1, source, :] - zonal) * (face_x * zf[k - 1, source, :].astype(jnp.float32))
                v_above = scale * (v[k - 1, source, :] - meridional) * (face_y * mf[k - 1, source, :].astype(jnp.float32))
            else:
                u_above, v_above = zero, zero
            head = p_ext[k, rows, :]
            slope_x = from_east(head, side, 48 + k) - head
            slope_y = p_ext[k, above, :] - head
            share = TIME_STEP / THICK[k]
            u_out[k, source, :] = (
                zonal + push_x * slope_x + turn_x * (both_y + b_ext[k, below, :]) + share * (u_above - u_below)
            ) * face_x
            v_out[k, source, :] = (
                meridional + push_y * slope_y - turn_y * (both_x + a_ext[k, above, :]) + share * (v_above - v_below)
            ) * face_y
            u_below, v_below = u_above, v_above
        return 0

    lax.fori_loop(0, tiles, update, 0)


def whole(n):
    return [pl.BlockSpec(memory_space=VMEM)] * n


def per_device(
    potential_warmth_degrees,
    dissolved_salt_content,
    zonal_edge_current,
    meridional_edge_current,
    wet_grid_flag,
    zonal_wet_edge_flag,
    meridional_wet_edge_flag,
    bottom_tier_count,
    zonal_grid_spacing,
    meridional_grid_spacing,
):
    t, s, u, v = potential_warmth_degrees, dissolved_salt_content, zonal_edge_current, meridional_edge_current
    zf, mf, e1, e2 = zonal_wet_edge_flag, meridional_wet_edge_flag, zonal_grid_spacing, meridional_grid_spacing
    lines = t.shape[1]
    lons, lats = lax.axis_size("lon"), lax.axis_size("lat")
    f32 = jnp.float32
    params = pltpu.CompilerParams(vmem_limit_bytes=24 * 1024 * 1024)
    packet = jax.ShapeDtypeStruct((PACKET, LANES), f32)
    field = jax.ShapeDtypeStruct(t.shape, f32)

    lat_to_a, lat_to_b = pl.pallas_call(
        row_pack,
        in_specs=[pl.BlockSpec(memory_space=pl.ANY)] * 8,
        out_specs=whole(2),
        out_shape=[packet, packet],
        scratch_shapes=[
            VMEM((7, LEVELS, TILE, LANES), f32),
            VMEM((3, LEVELS, TILE, LANES), jnp.int32),
            VMEM((3, TILE, LANES), f32),
            pltpu.SemaphoreType.DMA((13,)),
        ],
        name="row_pack",
    )(t, s, u, v, zf, mf, e1, e2)

    pairs_a = [(j, j ^ 1) for j in range(lats)]
    pairs_b = []
    for i in range(lons):
        for j in range(1, lats):
            other = (lons - 1 - i) * lats + j if j == lats - 1 else i * lats + (j + 1 if j % 2 else j - 1)
            pairs_b.append((i * lats + j, other))
    lat_a = lax.ppermute(lat_to_a, "lat", pairs_a)
    lat_b = lax.ppermute(lat_to_b, ("lon", "lat"), pairs_b)

    to_east, to_west, coriolis = pl.pallas_call(
        column_pack,
        in_specs=whole(8),
        out_specs=whole(3),
        out_shape=[packet, packet, jax.ShapeDtypeStruct(e1.shape, f32)],
        scratch_shapes=[VMEM((LANES, LANES), f32)],
        compiler_params=params,
        name="column_pack",
    )(t, s, u, v, zf, mf, e1, e2)

    lon_to_a, lon_to_b = pl.pallas_call(
        corner_pack,
        in_specs=whole(4),
        out_specs=whole(2),
        out_shape=[packet, packet],
        compiler_params=params,
        name="corner_pack",
    )(lat_a, lat_b, to_east, to_west)
    lon_b = lax.ppermute(lon_to_b, "lon", [(i, (i + 1 if i % 2 else i - 1) % lons) for i in range(lons)])
    lon_a = lax.ppermute(lon_to_a, "lon", [(i, i ^ 1) for i in range(lons)])

    extended = VMEM((LEVELS, lines + 2 * TILE, LANES), f32)
    square = VMEM((LANES, LANES), f32)
    return pl.pallas_call(
        step,
        in_specs=whole(15),
        out_specs=whole(4),
        out_shape=[field] * 4,
        scratch_shapes=[extended] * 9 + [square] * 2,
        compiler_params=params,
        name="step",
    )(t, s, u, v, zf, mf, bottom_tier_count, e1, e2, coriolis, to_west, lat_a, lat_b, lon_a, lon_b)


def solution(mesh):
    deep, flat = P(None, "lat", "lon"), P("lat", "lon")
    return jax.shard_map(
        per_device,
        mesh=mesh,
        in_specs=(deep,) * 7 + (flat,) * 3,
        out_specs=(deep,) * 4,
        check_vma=False,
    )
```

```python
import functools
import math

import jax
import jax.numpy as jnp
from jax import lax
from jax.experimental import pallas as pl
from jax.experimental.pallas import tpu as pltpu
from jax.sharding import PartitionSpec as P

GRAVITY = 9.81
REFERENCE_DENSITY = 1026.0
TIME_STEP = 360.0
LATERAL = 300.0
VERTICAL = 0.001
ROTATION = 7.292e-05

LEVELS = 8
LANES = 128
TILE = 8
PACKET = 4 * LEVELS
CHUNKS = 3
VMEM = pltpu.MemorySpace.VMEM

THICK = [6.0 + 4.0 * k for k in range(LEVELS)]
DEPTH = [2.0 * k * k + 6.0 * k + 3.0 for k in range(LEVELS)]
SPACING = [4.0 * k + 4.0 for k in range(LEVELS)]


def lane_index(shape):
    return lax.broadcasted_iota(jnp.int32, shape, len(shape) - 1)


def roll_lanes(x, shift):
    return pltpu.roll(x, shift % LANES, x.ndim - 1)


def density(heat, salt, k):
    anom_t = heat - 10.0
    anom_s = salt - 35.0
    by_t = -0.1655 * (1.0 + 0.0001497 * DEPTH[k])
    by_s = 0.76554 * (1.0 - 1.109e-05 * DEPTH[k])
    along_t = by_t + (-0.1655 * 0.5 * 0.05952) * anom_t - 0.0024341 * anom_s
    along_s = by_s - (0.76554 * 0.5 * 0.00054914) * anom_s
    return along_t * anom_t + along_s * anom_s


def row_pack(t, s, u, v, zf, mf, e1, e2, to_a, to_b, deep, flags, flat, arrived):
    j = lax.axis_index("lat")
    even = j % 2 == 0
    top = j == lax.axis_size("lat") - 1
    last = TILE - 1
    low, high = pl.ds(0, TILE), pl.ds(t.shape[1] - TILE, TILE)
    wanted = [(t, low), (t, high), (s, low), (s, high), (u, low), (u, high), (v, high)]
    marks = [(zf, low), (zf, high), (mf, high)]
    sizes = [(e1, high), (e2, high), (e2, low)]
    copies = [pltpu.make_async_copy(ref.at[:, rows, :], deep.at[n], arrived.at[n]) for n, (ref, rows) in enumerate(wanted)]
    copies += [pltpu.make_async_copy(ref.at[:, rows, :], flags.at[n], arrived.at[7 + n]) for n, (ref, rows) in enumerate(marks)]
    copies += [pltpu.make_async_copy(ref.at[rows, :], flat.at[n], arrived.at[10 + n]) for n, (ref, rows) in enumerate(sizes)]
    for copy in copies:
        copy.start()
    for copy in copies:
        copy.wait()

    def put(out, fields):
        for number, field in enumerate(fields):
            out[number * LEVELS : (number + 1) * LEVELS, :] = field

    def upward():
        spacing_x, spacing_y = flat[0, last:, :], flat[1, last:, :]
        face = flags[2, :, last, :].astype(jnp.float32)
        return [
            deep[1, :, last, :],
            deep[3, :, last, :],
            spacing_x * deep[6, :, last, :] * face,
            LATERAL * spacing_x / spacing_y * face,
        ]

    def downward():
        flux = flat[2, :1, :] * deep[4, :, 0, :] * flags[0, :, 0, :].astype(jnp.float32)
        return [deep[0, :, 0, :], deep[2, :, 0, :], flux, jnp.zeros_like(flux)]

    @pl.when(even)
    def _():
        put(to_a, upward())
        put(to_b, downward())

    @pl.when(jnp.logical_not(even))
    def _():
        put(to_a, downward())

    @pl.when(jnp.logical_not(even) & jnp.logical_not(top))
    def _():
        put(to_b, upward())

    @pl.when(top)
    def _():
        flux = flat[1, last:, :] * deep[5, :, last, :] * flags[1, :, last, :].astype(jnp.float32)
        rows = jnp.concatenate([deep[1, :, last, :], deep[3, :, last, :], -flux], axis=0)
        shape = (LANES, LANES)
        mirror = lane_index(shape) + lax.broadcasted_iota(jnp.int32, shape, 0) == LANES - 1
        to_b[: 3 * LEVELS, :] = lax.dot(
            rows, mirror.astype(jnp.float32), precision=lax.Precision.HIGHEST, preferred_element_type=jnp.float32
        )
        to_b[3 * LEVELS :, :] = jnp.zeros((LEVELS, LANES), jnp.float32)


def from_west(x):
    return jnp.where(lane_index(x.shape) == 0, 0.0, roll_lanes(x, 1))


def from_east(x):
    return jnp.where(lane_index(x.shape) == LANES - 1, 0.0, roll_lanes(x, -1))


def front(
    t, s, u, v, zf, mf, count, e1, e2,
    to_east, to_west, own, coriolis, p_ext, a_ext, b_ext, u_ext, v_ext, ft_ext, fs_ext, packed,
):
    lines = t.shape[1]
    tiles = lines // TILE
    lane = lane_index((TILE, LANES))
    first_row = lax.axis_index("lat") * lines
    total_rows = lines * lax.axis_size("lat")
    packed[pl.ds(lines, LANES - lines), :] = jnp.zeros((LANES - lines, LANES), jnp.float32)

    def pack(r, _):
        rows = pl.ds(pl.multiple_of(r * TILE, TILE), TILE)
        spacing_x, spacing_y = e1[rows, :], e2[rows, :]
        ratio = LATERAL * spacing_y / spacing_x
        levels = count[rows, :].astype(jnp.float32)
        row = (first_row + r * TILE + lax.broadcasted_iota(jnp.int32, (TILE, LANES), 0)).astype(jnp.float32)
        latitude = 10.0 + 78.0 * (row + 0.5) / total_rows
        turn = 2.0 * ROTATION * jnp.sin(latitude * (math.pi / 180.0))
        coriolis[rows, :] = turn
        fields = [jnp.zeros((TILE, LANES), jnp.float32) for _ in range(8)]

        def keep(number, k, x, source):
            target = number * LEVELS + k
            fields[number] = jnp.where(lane == target, roll_lanes(x, target - source), fields[number])

        for k in range(LEVELS):
            heat, salt = t[k, rows, :], s[k, rows, :]
            face_x, face_y = zf[k, rows, :].astype(jnp.float32), mf[k, rows, :].astype(jnp.float32)
            keep(0, k, heat, LANES - 1)
            keep(1, k, salt, LANES - 1)
            keep(2, k, spacing_y * u[k, rows, :] * face_x, LANES - 1)
            keep(3, k, ratio * face_x, LANES - 1)
            keep(4, k, heat, 0)
            keep(5, k, salt, 0)
            keep(6, k, spacing_x * v[k, rows, :] * face_y, 0)
            keep(7, k, face_y, 0)
        total = jnp.where(lane == 70, turn, 0.0)
        for n, (x, source) in enumerate(
            [(spacing_x, LANES - 1), (spacing_y, LANES - 1), (levels, LANES - 1), (spacing_x, 0), (spacing_y, 0), (levels, 0)]
        ):
            total = jnp.where(lane == 64 + n, roll_lanes(x, 64 + n - source), total)
        for field in fields:
            total = total + field
        packed[rows, :] = total
        return 0

    lax.fori_loop(0, tiles, pack, 0, unroll=4)
    turned = packed[...].T
    to_east[...] = turned[:PACKET]
    to_west[...] = turned[PACKET : 2 * PACKET]
    own[...] = turned[: own.shape[0]]

    def heads(r, _):
        source = pl.ds(pl.multiple_of(r * TILE, TILE), TILE)
        rows = pl.ds(pl.multiple_of(r * TILE + TILE, TILE), TILE)
        head = jnp.zeros((TILE, LANES), jnp.float32)
        for k in range(LEVELS):
            half = (0.5 * THICK[k]) * density(t[k, source, :], s[k, source, :], k)
            p_ext[k, rows, :] = head + half
            head = head + 2.0 * half
        return 0

    lax.fori_loop(0, tiles, heads, 0, unroll=2)

    def faces(r, _, last=False):
        source = pl.ds(pl.multiple_of(r * TILE, TILE), TILE)
        rows = pl.ds(pl.multiple_of(r * TILE + TILE, TILE), TILE)
        above = pl.ds(r * TILE + 1, TILE)
        spacing_x, spacing_y = e1[source, :], e2[source, :]
        ratio = LATERAL * spacing_x / spacing_y
        for k in range(LEVELS):
            flux_x = spacing_y * u[k, source, :] * zf[k, source, :].astype(jnp.float32)
            u_ext[k, rows, :] = flux_x
            a_ext[k, rows, :] = flux_x + from_west(flux_x)
            face = mf[k, source, :].astype(jnp.float32)
            flux_y = spacing_x * v[k, source, :] * face
            v_ext[k, rows, :] = flux_y
            b_ext[k, rows, :] = flux_y + from_east(flux_y)
            if not last:
                here, there = 0.5 * flux_y + ratio * face, 0.5 * flux_y - ratio * face
                ft_ext[k, rows, :] = here * t[k, source, :] + there * t[k, above, :]
                fs_ext[k, rows, :] = here * s[k, source, :] + there * s[k, above, :]
        return 0

    lax.fori_loop(0, tiles - 1, faces, 0)
    faces(tiles - 1, 0, last=True)


def corner_pack(from_a, from_b, to_east, to_west, to_a, to_b):
    even_j = lax.axis_index("lat") % 2 == 0
    even_i = lax.axis_index("lon") % 2 == 0
    shape = (PACKET, LANES)
    row = lax.broadcasted_iota(jnp.int32, shape, 0)
    corner = (lane_index(shape) == 96) & (row >= 2 * LEVELS) & (row < 3 * LEVELS)
    first, second = from_a[...], from_b[...]
    north = jnp.where(even_j, first, second)
    south = jnp.where(even_j, second, first)
    east = jnp.where(corner, roll_lanes(north, 96 - (LANES - 1)), to_east[...])
    west = jnp.where(corner, roll_lanes(south, 96), to_west[...])
    to_a[...] = jnp.where(even_i, east, west)
    to_b[...] = jnp.where(even_i, west, east)


def middle(
    t, s, u, v, zf, mf, count, e1, e2, coriolis, p_ext, a_ext, b_ext, u_ext, v_ext, ft_ext, fs_ext, lat_a, lat_b,
    t_out, s_out, u_out, v_out, beyond,
):
    lines = t.shape[1]
    tiles = lines // TILE
    even_j = lax.axis_index("lat") % 2 == 0

    def pick(ref_true, ref_false, flag, number):
        rows = slice(number * LEVELS, (number + 1) * LEVELS)
        return jnp.where(flag, ref_true[rows, :], ref_false[rows, :])

    north = [pick(lat_a, lat_b, even_j, n) for n in range(3)]
    south = [pick(lat_b, lat_a, even_j, n) for n in range(4)]
    here, there = 0.5 * south[2] + south[3], 0.5 * south[2] - south[3]
    beyond[0] = north[0]
    beyond[1] = north[1]
    beyond[2] = north[2] + from_west(north[2])
    beyond[4] = south[2] + from_east(south[2])
    beyond[5] = south[2]
    beyond[6] = here * south[0] + there * t[:, 0, :]
    beyond[7] = here * south[1] + there * s[:, 0, :]
    head = jnp.zeros((1, LANES), jnp.float32)
    for k in range(LEVELS):
        half = (0.5 * THICK[k]) * density(beyond[0, k : k + 1, :], beyond[1, k : k + 1, :], k)
        beyond[3, k : k + 1, :] = head + half
        head = head + 2.0 * half

    row = lax.broadcasted_iota(jnp.int32, (TILE, LANES), 0)

    def update(r, _, first=False, last=False):
        source = pl.ds(pl.multiple_of(r * TILE, TILE), TILE)
        rows = pl.ds(pl.multiple_of(r * TILE + TILE, TILE), TILE)
        spacing_x, spacing_y = e1[source, :], e2[source, :]
        levels = count[source, :]
        inverse_x, inverse_y = 1.0 / spacing_x, 1.0 / spacing_y
        ratio_x, ratio_y = LATERAL * spacing_y * inverse_x, LATERAL * spacing_x * inverse_y
        area = spacing_x * spacing_y
        per_area = TIME_STEP * inverse_x * inverse_y
        turn = (0.25 * TIME_STEP) * coriolis[source, :]
        turn_x, turn_y = turn * inverse_x, turn * inverse_y
        push = -TIME_STEP * GRAVITY / REFERENCE_DENSITY
        push_x, push_y = push * inverse_x, push * inverse_y
        zero = jnp.zeros((TILE, LANES), jnp.float32)

        def above(ref, k, number, offset=TILE):
            if last:
                return jnp.where(row == TILE - 1, beyond[number, k : k + 1, :], pltpu.roll(ref[k, pl.ds(r * TILE + offset, TILE), :], TILE - 1, 0))
            return ref[k, pl.ds(r * TILE + offset + 1, TILE), :]

        def below(ref, k, number):
            if first:
                return jnp.where(row == 0, beyond[number, k : k + 1, :], pltpu.roll(ref[k, rows, :], 1, 0))
            return ref[k, pl.ds(r * TILE + TILE - 1, TILE), :]

        upward, t_below, s_below, u_below, v_below = zero, zero, zero, zero, zero
        for k in reversed(range(LEVELS)):
            heat, salt = t[k, source, :], s[k, source, :]
            flux_x, flux_y = u_ext[k, rows, :], v_ext[k, rows, :]
            face_x, face_y = zf[k, source, :].astype(jnp.float32), mf[k, source, :].astype(jnp.float32)
            both_x, both_y = a_ext[k, rows, :], b_ext[k, rows, :]
            wet = levels > k
            spread = ratio_x * face_x
            here, there = 0.5 * flux_x + spread, 0.5 * flux_x - spread
            t_east = here * heat + there * from_east(heat)
            s_east = here * salt + there * from_east(salt)
            if last:
                here, there = 0.5 * flux_y + ratio_y * face_y, 0.5 * flux_y - ratio_y * face_y
                t_north, s_north = here * heat + there * above(t, k, 0, 0), here * salt + there * above(s, k, 1, 0)
                under = pl.ds(r * TILE + TILE - 1, 1)
                t_south = jnp.where(row == 0, ft_ext[k, under, :], pltpu.roll(t_north, 1, 0))
                s_south = jnp.where(row == 0, fs_ext[k, under, :], pltpu.roll(s_north, 1, 0))
            else:
                t_north, s_north = ft_ext[k, rows, :], fs_ext[k, rows, :]
                t_south, s_south = below(ft_ext, k, 6), below(fs_ext, k, 7)
            t_net = t_east - from_west(t_east) + t_north - t_south
            s_net = s_east - from_west(s_east) + s_north - s_south
            converge = 2.0 * flux_x - both_x + flux_y - below(v_ext, k, 5)
            upward = upward - THICK[k] * converge
            if k > 0:
                mix = jnp.where(wet, (VERTICAL / SPACING[k]) * area, 0.0)
                upper, lower = 0.5 * upward - mix, 0.5 * upward + mix
                t_above = upper * t[k - 1, source, :] + lower * heat
                s_above = upper * s[k - 1, source, :] + lower * salt
            else:
                t_above, s_above = upward * heat, upward * salt
            t_net = t_net + (t_above - t_below) * (1.0 / THICK[k])
            s_net = s_net + (s_above - s_below) * (1.0 / THICK[k])
            t_below, s_below = t_above, s_above
            t_out[k, source, :] = jnp.where(wet, heat - per_area * t_net, 0.0)
            s_out[k, source, :] = jnp.where(wet, salt - per_area * s_net, 0.0)
            zonal, meridional = u[k, source, :], v[k, source, :]
            if k > 0:
                u_above = (VERTICAL / SPACING[k]) * (u[k - 1, source, :] - zonal) * face_x
                v_above = (VERTICAL / SPACING[k]) * (v[k - 1, source, :] - meridional) * face_y
            else:
                u_above, v_above = zero, zero
            head = p_ext[k, rows, :]
            slope_x = from_east(head) - head
            slope_y = above(p_ext, k, 3) - head
            share = TIME_STEP / THICK[k]
            u_out[k, source, :] = (
                zonal + push_x * slope_x + turn_x * (both_y + below(b_ext, k, 4)) + share * (u_above - u_below)
            ) * face_x
            v_out[k, source, :] = (
                meridional + push_y * slope_y - turn_y * (both_x + above(a_ext, k, 2)) + share * (v_above - v_below)
            ) * face_y
            u_below, v_below = u_above, v_above
        return 0

    update(0, 0, first=True)
    lax.fori_loop(1, tiles - 1, update, 0)
    update(tiles - 1, 0, last=True)


def running_sum(x, level, upward):
    for step in (1, 2, 4):
        if upward:
            x = x + jnp.where(level < LEVELS - step, pltpu.roll(x, LEVELS - step, 0), 0.0)
        else:
            x = x + jnp.where(level >= step, pltpu.roll(x, step, 0), 0.0)
    return x


def finish(t_part, s_part, u_part, v_part, own, lon_a, lon_b, t_out, s_out, u_out, v_out, turned, sides, *buffers_and_done):
    buffers, done = buffers_and_done[:4], buffers_and_done[4]
    lines = t_part.shape[1]
    even_i = lax.axis_index("lon") % 2 == 0

    def pick(ref_true, ref_false, flag, number):
        rows = slice(number * LEVELS, (number + 1) * LEVELS)
        return jnp.where(flag, ref_true[rows, :], ref_false[rows, :])

    t_east, s_east, v_east = [pick(lon_a, lon_b, even_i, n) for n in range(3)]
    t_west, s_west, u_west, g_west = [pick(lon_b, lon_a, even_i, n) for n in range(4)]
    shape = (LEVELS, LANES)
    level, lane = lax.broadcasted_iota(jnp.int32, shape, 0), lane_index(shape)
    depth_index = level.astype(jnp.float32)
    thick = 6.0 + 4.0 * depth_index
    depth = 2.0 * depth_index * depth_index + 6.0 * depth_index + 3.0

    def mine(number):
        return own[number * LEVELS : (number + 1) * LEVELS, :]

    def single(number):
        return own[64 + number : 65 + number, :]

    u_last, g_last, t_first, s_first, face_first = mine(2), mine(3), mine(4), mine(5), mine(7)
    turn = (0.25 * TIME_STEP) * single(6)
    push = -TIME_STEP * GRAVITY / REFERENCE_DENSITY
    inverse_x, inverse_y = 1.0 / single(0), 1.0 / single(1)
    wet = depth_index < single(2)
    back = jnp.where(wet, -(TIME_STEP * inverse_x * inverse_y) * (0.5 * u_last - g_last), 0.0)
    anom_t, anom_s = t_east - 10.0, s_east - 35.0
    weight = 0.5 * thick * (
        (-0.1655 * (1.0 + 0.0001497 * depth) + (-0.1655 * 0.5 * 0.05952) * anom_t - 0.0024341 * anom_s) * anom_t
        + (0.76554 * (1.0 - 1.109e-05 * depth) - (0.76554 * 0.5 * 0.00054914) * anom_s) * anom_s
    )
    head = 2.0 * running_sum(weight, level, False) - weight
    v_south_east = jnp.where(lane == 0, roll_lanes(v_east, -lines), roll_lanes(v_east, 1))
    u_add = jnp.where(g_last > 0.0, (push * inverse_x) * head + (turn * inverse_x) * (v_east + v_south_east), 0.0)
    turned[...] = jnp.zeros_like(turned)
    turned[pl.ds(0, LEVELS, 2), :] = back * t_east
    turned[pl.ds(16, LEVELS, 2), :] = back * s_east
    turned[pl.ds(32, LEVELS, 2), :] = u_add
    inverse_x, inverse_y = 1.0 / single(3), 1.0 / single(4)
    wet = depth_index < single(5)
    scale = jnp.where(wet, -(TIME_STEP * inverse_x * inverse_y), 0.0)
    here, there = 0.5 * u_west + g_west, 0.5 * u_west - g_west
    upward = running_sum(0.5 * thick * u_west, level, True)

    def first_column(q_west, q):
        flux = upward * (q + jnp.where(level == 0, q, pltpu.roll(q, 1, 0)))
        under = jnp.where(level == LEVELS - 1, 0.0, pltpu.roll(flux, LEVELS - 1, 0))
        return scale * ((flux - under) / thick - (here * q_west + there * q))

    turned[pl.ds(1, LEVELS, 2), :] = first_column(t_west, t_first)
    turned[pl.ds(17, LEVELS, 2), :] = first_column(s_west, s_first)
    turned[pl.ds(33, LEVELS, 2), :] = -(turn * inverse_y) * (u_west + roll_lanes(u_west, -1)) * face_first
    sides[...] = turned[...].T

    at_first, at_last = lane == 0, lane == LANES - 1
    at_side = at_first | at_last
    parts, outs = (t_part, s_part, u_part, v_part), (t_out, s_out, u_out, v_out)
    chunk = lines // CHUNKS
    copies = []
    for c in range(CHUNKS):

        def tile(r, _):
            rows = pl.ds(pl.multiple_of(r * TILE, TILE), TILE)
            side = sides[rows, :]
            for k in range(LEVELS):
                both = roll_lanes(side, -(2 * k + 33))
                adds = (
                    jnp.where(at_side, roll_lanes(side, -(2 * k + 1)), 0.0),
                    jnp.where(at_side, roll_lanes(side, -(2 * k + 17)), 0.0),
                    jnp.where(at_last, both, 0.0),
                    jnp.where(at_first, both, 0.0),
                )
                for part, add, buffer in zip(parts, adds, buffers):
                    buffer[k, rows, :] = part[k, rows, :] + add
            return 0

        lax.fori_loop(c * chunk // TILE, (c + 1) * chunk // TILE, tile, 0)
        rows = pl.ds(c * chunk, chunk)
        for n in range(4):
            copy = pltpu.make_async_copy(buffers[n].at[:, rows, :], outs[n].at[:, rows, :], done.at[c * 4 + n])
            copy.start()
            copies.append(copy)
    for copy in copies:
        copy.wait()


def whole(n):
    return [pl.BlockSpec(memory_space=VMEM)] * n


def per_device(
    potential_warmth_degrees,
    dissolved_salt_content,
    zonal_edge_current,
    meridional_edge_current,
    wet_grid_flag,
    zonal_wet_edge_flag,
    meridional_wet_edge_flag,
    bottom_tier_count,
    zonal_grid_spacing,
    meridional_grid_spacing,
):
    t, s, u, v = potential_warmth_degrees, dissolved_salt_content, zonal_edge_current, meridional_edge_current
    zf, mf, e1, e2 = zonal_wet_edge_flag, meridional_wet_edge_flag, zonal_grid_spacing, meridional_grid_spacing
    lines = t.shape[1]
    lons, lats = lax.axis_size("lon"), lax.axis_size("lat")
    f32 = jnp.float32
    params = pltpu.CompilerParams(vmem_limit_bytes=24 * 1024 * 1024)
    packet = jax.ShapeDtypeStruct((PACKET, LANES), f32)
    field = jax.ShapeDtypeStruct(t.shape, f32)

    lat_to_a, lat_to_b = pl.pallas_call(
        row_pack,
        in_specs=[pl.BlockSpec(memory_space=pl.ANY)] * 8,
        out_specs=whole(2),
        out_shape=[packet, packet],
        scratch_shapes=[
            VMEM((7, LEVELS, TILE, LANES), f32),
            VMEM((3, LEVELS, TILE, LANES), jnp.int32),
            VMEM((3, TILE, LANES), f32),
            pltpu.SemaphoreType.DMA((13,)),
        ],
        name="row_pack",
    )(t, s, u, v, zf, mf, e1, e2)

    pairs_a = [(j, j ^ 1) for j in range(lats)]
    pairs_b = []
    for i in range(lons):
        for j in range(1, lats):
            other = (lons - 1 - i) * lats + j if j == lats - 1 else i * lats + (j + 1 if j % 2 else j - 1)
            pairs_b.append((i * lats + j, other))
    lat_a = lax.ppermute(lat_to_a, "lat", pairs_a)
    lat_b = lax.ppermute(lat_to_b, ("lon", "lat"), pairs_b)

    extended = jax.ShapeDtypeStruct((LEVELS, lines + 2 * TILE, LANES), f32)
    square = VMEM((LANES, LANES), f32)
    to_east, to_west, own, coriolis, *parts = pl.pallas_call(
        front,
        in_specs=whole(9),
        out_specs=whole(11),
        out_shape=[packet, packet, jax.ShapeDtypeStruct((72, LANES), f32), jax.ShapeDtypeStruct(e1.shape, f32)] + [extended] * 7,
        scratch_shapes=[square],
        compiler_params=params,
        name="front",
    )(t, s, u, v, zf, mf, bottom_tier_count, e1, e2)

    lon_to_a, lon_to_b = pl.pallas_call(
        corner_pack,
        in_specs=whole(4),
        out_specs=whole(2),
        out_shape=[packet, packet],
        compiler_params=params,
        name="corner_pack",
    )(lat_a, lat_b, to_east, to_west)
    lon_b = lax.ppermute(lon_to_b, "lon", [(i, (i + 1 if i % 2 else i - 1) % lons) for i in range(lons)])
    lon_a = lax.ppermute(lon_to_a, "lon", [(i, i ^ 1) for i in range(lons)])

    parts = pl.pallas_call(
        middle,
        in_specs=whole(19),
        out_specs=whole(4),
        out_shape=[field] * 4,
        scratch_shapes=[VMEM((8, LEVELS, LANES), f32)],
        compiler_params=params,
        name="middle",
    )(t, s, u, v, zf, mf, bottom_tier_count, e1, e2, coriolis, *parts, lat_a, lat_b)

    return pl.pallas_call(
        finish,
        in_specs=whole(7),
        out_specs=[pl.BlockSpec(memory_space=pltpu.MemorySpace.HBM)] * 4,
        out_shape=[field] * 4,
        scratch_shapes=[square] * 2 + [VMEM(t.shape, f32)] * 4 + [pltpu.SemaphoreType.DMA((4 * CHUNKS,))],
        compiler_params=params,
        name="finish",
    )(*parts, own, lon_a, lon_b)


def solution(mesh):
    deep, flat = P(None, "lat", "lon"), P("lat", "lon")
    return jax.shard_map(
        per_device,
        mesh=mesh,
        in_specs=(deep,) * 7 + (flat,) * 3,
        out_specs=(deep,) * 4,
        check_vma=False,
    )
```

```python
import functools
import math

import jax
import jax.numpy as jnp
from jax import lax
from jax.experimental import pallas as pl
from jax.experimental.pallas import tpu as pltpu
from jax.sharding import PartitionSpec as P

GRAVITY = 9.81
REFERENCE_DENSITY = 1026.0
TIME_STEP = 360.0
LATERAL = 300.0
VERTICAL = 0.001
ROTATION = 7.292e-05

LEVELS = 8
LANES = 128
TILE = 8
PACKET = 4 * LEVELS
CHUNKS = 3
VMEM = pltpu.MemorySpace.VMEM

THICK = [6.0 + 4.0 * k for k in range(LEVELS)]
DEPTH = [2.0 * k * k + 6.0 * k + 3.0 for k in range(LEVELS)]
SPACING = [4.0 * k + 4.0 for k in range(LEVELS)]


def lane_index(shape):
    return lax.broadcasted_iota(jnp.int32, shape, len(shape) - 1)


def roll_lanes(x, shift):
    return pltpu.roll(x, shift % LANES, x.ndim - 1)


def density(heat, salt, k):
    anom_t = heat - 10.0
    anom_s = salt - 35.0
    by_t = -0.1655 * (1.0 + 0.0001497 * DEPTH[k])
    by_s = 0.76554 * (1.0 - 1.109e-05 * DEPTH[k])
    along_t = by_t + (-0.1655 * 0.5 * 0.05952) * anom_t - 0.0024341 * anom_s
    along_s = by_s - (0.76554 * 0.5 * 0.00054914) * anom_s
    return along_t * anom_t + along_s * anom_s


def row_pack(t, s, u, v, zf, mf, e1, e2, to_a, to_b, deep, flags, flat, arrived):
    j = lax.axis_index("lat")
    even = j % 2 == 0
    top = j == lax.axis_size("lat") - 1
    last = TILE - 1
    low, high = pl.ds(0, TILE), pl.ds(t.shape[1] - TILE, TILE)
    wanted = [(t, low), (t, high), (s, low), (s, high), (u, low), (u, high), (v, high)]
    marks = [(zf, low), (zf, high), (mf, high)]
    sizes = [(e1, high), (e2, high), (e2, low)]
    copies = [pltpu.make_async_copy(ref.at[:, rows, :], deep.at[n], arrived.at[n]) for n, (ref, rows) in enumerate(wanted)]
    copies += [pltpu.make_async_copy(ref.at[:, rows, :], flags.at[n], arrived.at[7 + n]) for n, (ref, rows) in enumerate(marks)]
    copies += [pltpu.make_async_copy(ref.at[rows, :], flat.at[n], arrived.at[10 + n]) for n, (ref, rows) in enumerate(sizes)]
    for copy in copies:
        copy.start()
    for copy in copies:
        copy.wait()

    def put(out, fields):
        for number, field in enumerate(fields):
            out[number * LEVELS : (number + 1) * LEVELS, :] = field

    def upward():
        spacing_x, spacing_y = flat[0, last:, :], flat[1, last:, :]
        face = flags[2, :, last, :].astype(jnp.float32)
        return [
            deep[1, :, last, :],
            deep[3, :, last, :],
            spacing_x * deep[6, :, last, :] * face,
            LATERAL * spacing_x / spacing_y * face,
        ]

    def downward():
        flux = flat[2, :1, :] * deep[4, :, 0, :] * flags[0, :, 0, :].astype(jnp.float32)
        return [deep[0, :, 0, :], deep[2, :, 0, :], flux, jnp.zeros_like(flux)]

    @pl.when(even)
    def _():
        put(to_a, upward())
        put(to_b, downward())

    @pl.when(jnp.logical_not(even))
    def _():
        put(to_a, downward())

    @pl.when(jnp.logical_not(even) & jnp.logical_not(top))
    def _():
        put(to_b, upward())

    @pl.when(top)
    def _():
        flux = flat[1, last:, :] * deep[5, :, last, :] * flags[1, :, last, :].astype(jnp.float32)
        rows = jnp.concatenate([deep[1, :, last, :], deep[3, :, last, :], -flux], axis=0)
        shape = (LANES, LANES)
        mirror = lane_index(shape) + lax.broadcasted_iota(jnp.int32, shape, 0) == LANES - 1
        to_b[: 3 * LEVELS, :] = lax.dot(
            rows, mirror.astype(jnp.float32), precision=lax.Precision.HIGHEST, preferred_element_type=jnp.float32
        )
        to_b[3 * LEVELS :, :] = jnp.zeros((LEVELS, LANES), jnp.float32)


def from_west(x):
    return jnp.where(lane_index(x.shape) == 0, 0.0, roll_lanes(x, 1))


def from_east(x):
    return jnp.where(lane_index(x.shape) == LANES - 1, 0.0, roll_lanes(x, -1))


def front(
    t, s, u, v, zf, mf, e1, e2,
    to_east, to_west, own, coriolis, p_ext, a_ext, b_ext, u_ext, v_ext, ft_ext, fs_ext, packed,
):
    lines = t.shape[1]
    tiles = lines // TILE
    lane = lane_index((TILE, LANES))
    first_row = lax.axis_index("lat") * lines
    total_rows = lines * lax.axis_size("lat")
    packed[pl.ds(lines, LANES - lines), :] = jnp.zeros((LANES - lines, LANES), jnp.float32)

    def pack(r, _):
        rows = pl.ds(pl.multiple_of(r * TILE, TILE), TILE)
        spacing_x, spacing_y = e1[rows, :], e2[rows, :]
        ratio = LATERAL * spacing_y / spacing_x
        row = (first_row + r * TILE + lax.broadcasted_iota(jnp.int32, (TILE, LANES), 0)).astype(jnp.float32)
        latitude = 10.0 + 78.0 * (row + 0.5) / total_rows
        turn = 2.0 * ROTATION * jnp.sin(latitude * (math.pi / 180.0))
        coriolis[rows, :] = turn
        fields = [jnp.zeros((TILE, LANES), jnp.float32) for _ in range(8)]

        def keep(number, k, x, source):
            target = number * LEVELS + k
            fields[number] = jnp.where(lane == target, roll_lanes(x, target - source), fields[number])

        for k in range(LEVELS):
            heat, salt = t[k, rows, :], s[k, rows, :]
            face_x, face_y = zf[k, rows, :].astype(jnp.float32), mf[k, rows, :].astype(jnp.float32)
            keep(0, k, heat, LANES - 1)
            keep(1, k, salt, LANES - 1)
            keep(2, k, spacing_y * u[k, rows, :] * face_x, LANES - 1)
            keep(3, k, ratio * face_x, LANES - 1)
            keep(4, k, heat, 0)
            keep(5, k, salt, 0)
            keep(6, k, spacing_x * v[k, rows, :] * face_y, 0)
            keep(7, k, face_y, 0)
        total = jnp.where(lane == 68, turn, 0.0)
        for n, (x, source) in enumerate([(spacing_x, LANES - 1), (spacing_y, LANES - 1), (spacing_x, 0), (spacing_y, 0)]):
            total = jnp.where(lane == 64 + n, roll_lanes(x, 64 + n - source), total)
        for field in fields:
            total = total + field
        packed[rows, :] = total
        return 0

    lax.fori_loop(0, tiles, pack, 0, unroll=4)
    turned = packed[...].T
    to_east[...] = turned[:PACKET]
    to_west[...] = turned[PACKET : 2 * PACKET]
    own[...] = turned[: own.shape[0]]

    def heads(r, _):
        source = pl.ds(pl.multiple_of(r * TILE, TILE), TILE)
        rows = pl.ds(pl.multiple_of(r * TILE + TILE, TILE), TILE)
        head = jnp.zeros((TILE, LANES), jnp.float32)
        for k in range(LEVELS):
            half = (0.5 * THICK[k]) * density(t[k, source, :], s[k, source, :], k)
            p_ext[k, rows, :] = head + half
            head = head + 2.0 * half
        return 0

    lax.fori_loop(0, tiles, heads, 0, unroll=2)

    def faces(r, _, last=False):
        source = pl.ds(pl.multiple_of(r * TILE, TILE), TILE)
        rows = pl.ds(pl.multiple_of(r * TILE + TILE, TILE), TILE)
        above = pl.ds(r * TILE + 1, TILE)
        spacing_x, spacing_y = e1[source, :], e2[source, :]
        ratio = LATERAL * spacing_x / spacing_y
        for k in range(LEVELS):
            flux_x = spacing_y * u[k, source, :] * zf[k, source, :].astype(jnp.float32)
            u_ext[k, rows, :] = flux_x
            a_ext[k, rows, :] = flux_x + from_west(flux_x)
            face = mf[k, source, :].astype(jnp.float32)
            flux_y = spacing_x * v[k, source, :] * face
            v_ext[k, rows, :] = flux_y
            b_ext[k, rows, :] = flux_y + from_east(flux_y)
            if not last:
                here, there = 0.5 * flux_y + ratio * face, 0.5 * flux_y - ratio * face
                ft_ext[k, rows, :] = here * t[k, source, :] + there * t[k, above, :]
                fs_ext[k, rows, :] = here * s[k, source, :] + there * s[k, above, :]
        return 0

    lax.fori_loop(0, tiles - 1, faces, 0, unroll=3)
    faces(tiles - 1, 0, last=True)


def corner_pack(from_a, from_b, to_east, to_west, to_a, to_b):
    even_j = lax.axis_index("lat") % 2 == 0
    even_i = lax.axis_index("lon") % 2 == 0
    shape = (PACKET, LANES)
    row = lax.broadcasted_iota(jnp.int32, shape, 0)
    corner = (lane_index(shape) == 96) & (row >= 2 * LEVELS) & (row < 3 * LEVELS)
    first, second = from_a[...], from_b[...]
    north = jnp.where(even_j, first, second)
    south = jnp.where(even_j, second, first)
    east = jnp.where(corner, roll_lanes(north, 96 - (LANES - 1)), to_east[...])
    west = jnp.where(corner, roll_lanes(south, 96), to_west[...])
    to_a[...] = jnp.where(even_i, east, west)
    to_b[...] = jnp.where(even_i, west, east)


def middle(
    t, s, u, v, zf, mf, count, e1, e2, coriolis, p_ext, a_ext, b_ext, u_ext, v_ext, ft_ext, fs_ext, lat_a, lat_b,
    t_out, s_out, u_out, v_out, beyond,
):
    lines = t.shape[1]
    tiles = lines // TILE
    even_j = lax.axis_index("lat") % 2 == 0

    def pick(ref_true, ref_false, flag, number):
        rows = slice(number * LEVELS, (number + 1) * LEVELS)
        return jnp.where(flag, ref_true[rows, :], ref_false[rows, :])

    north = [pick(lat_a, lat_b, even_j, n) for n in range(3)]
    south = [pick(lat_b, lat_a, even_j, n) for n in range(4)]
    here, there = 0.5 * south[2] + south[3], 0.5 * south[2] - south[3]
    beyond[0] = north[0]
    beyond[1] = north[1]
    beyond[2] = north[2] + from_west(north[2])
    beyond[4] = south[2] + from_east(south[2])
    beyond[5] = south[2]
    beyond[6] = here * south[0] + there * t[:, 0, :]
    beyond[7] = here * south[1] + there * s[:, 0, :]
    head = jnp.zeros((1, LANES), jnp.float32)
    for k in range(LEVELS):
        half = (0.5 * THICK[k]) * density(beyond[0, k : k + 1, :], beyond[1, k : k + 1, :], k)
        beyond[3, k : k + 1, :] = head + half
        head = head + 2.0 * half

    row = lax.broadcasted_iota(jnp.int32, (TILE, LANES), 0)

    def update(r, _, first=False, last=False):
        source = pl.ds(pl.multiple_of(r * TILE, TILE), TILE)
        rows = pl.ds(pl.multiple_of(r * TILE + TILE, TILE), TILE)
        spacing_x, spacing_y = e1[source, :], e2[source, :]
        levels = count[source, :]
        inverse_x, inverse_y = 1.0 / spacing_x, 1.0 / spacing_y
        ratio_x, ratio_y = LATERAL * spacing_y * inverse_x, LATERAL * spacing_x * inverse_y
        area = spacing_x * spacing_y
        per_area = TIME_STEP * inverse_x * inverse_y
        turn = (0.25 * TIME_STEP) * coriolis[source, :]
        turn_x, turn_y = turn * inverse_x, turn * inverse_y
        push = -TIME_STEP * GRAVITY / REFERENCE_DENSITY
        push_x, push_y = push * inverse_x, push * inverse_y
        zero = jnp.zeros((TILE, LANES), jnp.float32)

        def above(ref, k, number, offset=TILE):
            if last:
                return jnp.where(row == TILE - 1, beyond[number, k : k + 1, :], pltpu.roll(ref[k, pl.ds(r * TILE + offset, TILE), :], TILE - 1, 0))
            return ref[k, pl.ds(r * TILE + offset + 1, TILE), :]

        def below(ref, k, number):
            if first:
                return jnp.where(row == 0, beyond[number, k : k + 1, :], pltpu.roll(ref[k, rows, :], 1, 0))
            return ref[k, pl.ds(r * TILE + TILE - 1, TILE), :]

        upward, t_below, s_below, u_below, v_below = zero, zero, zero, zero, zero
        for k in reversed(range(LEVELS)):
            heat, salt = t[k, source, :], s[k, source, :]
            flux_x, flux_y = u_ext[k, rows, :], v_ext[k, rows, :]
            face_x, face_y = zf[k, source, :].astype(jnp.float32), mf[k, source, :].astype(jnp.float32)
            both_x, both_y = a_ext[k, rows, :], b_ext[k, rows, :]
            wet = levels > k
            spread = ratio_x * face_x
            here, there = 0.5 * flux_x + spread, 0.5 * flux_x - spread
            t_east = here * heat + there * from_east(heat)
            s_east = here * salt + there * from_east(salt)
            if last:
                here, there = 0.5 * flux_y + ratio_y * face_y, 0.5 * flux_y - ratio_y * face_y
                t_north, s_north = here * heat + there * above(t, k, 0, 0), here * salt + there * above(s, k, 1, 0)
                under = pl.ds(r * TILE + TILE - 1, 1)
                t_south = jnp.where(row == 0, ft_ext[k, under, :], pltpu.roll(t_north, 1, 0))
                s_south = jnp.where(row == 0, fs_ext[k, under, :], pltpu.roll(s_north, 1, 0))
            else:
                t_north, s_north = ft_ext[k, rows, :], fs_ext[k, rows, :]
                t_south, s_south = below(ft_ext, k, 6), below(fs_ext, k, 7)
            t_net = t_east - from_west(t_east) + t_north - t_south
            s_net = s_east - from_west(s_east) + s_north - s_south
            converge = 2.0 * flux_x - both_x + flux_y - below(v_ext, k, 5)
            upward = upward - THICK[k] * converge
            if k > 0:
                mix = jnp.where(wet, (VERTICAL / SPACING[k]) * area, 0.0)
                upper, lower = 0.5 * upward - mix, 0.5 * upward + mix
                t_above = upper * t[k - 1, source, :] + lower * heat
                s_above = upper * s[k - 1, source, :] + lower * salt
            else:
                t_above, s_above = upward * heat, upward * salt
            t_net = t_net + (t_above - t_below) * (1.0 / THICK[k])
            s_net = s_net + (s_above - s_below) * (1.0 / THICK[k])
            t_below, s_below = t_above, s_above
            t_out[k, source, :] = jnp.where(wet, heat - per_area * t_net, 0.0)
            s_out[k, source, :] = jnp.where(wet, salt - per_area * s_net, 0.0)
            zonal, meridional = u[k, source, :], v[k, source, :]
            if k > 0:
                u_above = (VERTICAL / SPACING[k]) * (u[k - 1, source, :] - zonal) * face_x
                v_above = (VERTICAL / SPACING[k]) * (v[k - 1, source, :] - meridional) * face_y
            else:
                u_above, v_above = zero, zero
            head = p_ext[k, rows, :]
            slope_x = from_east(head) - head
            slope_y = above(p_ext, k, 3) - head
            share = TIME_STEP / THICK[k]
            u_out[k, source, :] = (
                zonal + push_x * slope_x + turn_x * (both_y + below(b_ext, k, 4)) + share * (u_above - u_below)
            ) * face_x
            v_out[k, source, :] = (
                meridional + push_y * slope_y - turn_y * (both_x + above(a_ext, k, 2)) + share * (v_above - v_below)
            ) * face_y
            u_below, v_below = u_above, v_above
        return 0

    update(0, 0, first=True)
    lax.fori_loop(1, tiles - 1, update, 0, unroll=2)
    update(tiles - 1, 0, last=True)


def running_sum(x, level, upward):
    for step in (1, 2, 4):
        if upward:
            x = x + jnp.where(level < LEVELS - step, pltpu.roll(x, LEVELS - step, 0), 0.0)
        else:
            x = x + jnp.where(level >= step, pltpu.roll(x, step, 0), 0.0)
    return x


def finish(t_part, s_part, u_part, v_part, count, own, lon_a, lon_b, t_out, s_out, u_out, v_out, turned, sides, *buffers_and_done):
    buffers, done = buffers_and_done[:4], buffers_and_done[4]
    lines = t_part.shape[1]
    even_i = lax.axis_index("lon") % 2 == 0

    def pick(ref_true, ref_false, flag, number):
        rows = slice(number * LEVELS, (number + 1) * LEVELS)
        return jnp.where(flag, ref_true[rows, :], ref_false[rows, :])

    t_east, s_east, v_east = [pick(lon_a, lon_b, even_i, n) for n in range(3)]
    t_west, s_west, u_west, g_west = [pick(lon_b, lon_a, even_i, n) for n in range(4)]
    shape = (LEVELS, LANES)
    level, lane = lax.broadcasted_iota(jnp.int32, shape, 0), lane_index(shape)
    depth_index = level.astype(jnp.float32)
    thick = 6.0 + 4.0 * depth_index
    depth = 2.0 * depth_index * depth_index + 6.0 * depth_index + 3.0

    def mine(number):
        return own[number * LEVELS : (number + 1) * LEVELS, :]

    def single(number):
        return own[64 + number : 65 + number, :]

    u_last, g_last, t_first, s_first, face_first = mine(2), mine(3), mine(4), mine(5), mine(7)
    turn = (0.25 * TIME_STEP) * single(4)
    push = -TIME_STEP * GRAVITY / REFERENCE_DENSITY
    inverse_x, inverse_y = 1.0 / single(0), 1.0 / single(1)
    back = -(TIME_STEP * inverse_x * inverse_y) * (0.5 * u_last - g_last)
    anom_t, anom_s = t_east - 10.0, s_east - 35.0
    weight = 0.5 * thick * (
        (-0.1655 * (1.0 + 0.0001497 * depth) + (-0.1655 * 0.5 * 0.05952) * anom_t - 0.0024341 * anom_s) * anom_t
        + (0.76554 * (1.0 - 1.109e-05 * depth) - (0.76554 * 0.5 * 0.00054914) * anom_s) * anom_s
    )
    head = 2.0 * running_sum(weight, level, False) - weight
    v_south_east = jnp.where(lane == 0, roll_lanes(v_east, -lines), roll_lanes(v_east, 1))
    u_add = jnp.where(g_last > 0.0, (push * inverse_x) * head + (turn * inverse_x) * (v_east + v_south_east), 0.0)
    turned[...] = jnp.zeros_like(turned)
    turned[pl.ds(0, LEVELS, 2), :] = back * t_east
    turned[pl.ds(16, LEVELS, 2), :] = back * s_east
    turned[pl.ds(32, LEVELS, 2), :] = u_add
    inverse_x, inverse_y = 1.0 / single(2), 1.0 / single(3)
    scale = -(TIME_STEP * inverse_x * inverse_y)
    here, there = 0.5 * u_west + g_west, 0.5 * u_west - g_west
    upward = running_sum(0.5 * thick * u_west, level, True)

    def first_column(q_west, q):
        flux = upward * (q + jnp.where(level == 0, q, pltpu.roll(q, 1, 0)))
        under = jnp.where(level == LEVELS - 1, 0.0, pltpu.roll(flux, LEVELS - 1, 0))
        return scale * ((flux - under) / thick - (here * q_west + there * q))

    turned[pl.ds(1, LEVELS, 2), :] = first_column(t_west, t_first)
    turned[pl.ds(17, LEVELS, 2), :] = first_column(s_west, s_first)
    turned[pl.ds(33, LEVELS, 2), :] = -(turn * inverse_y) * (u_west + roll_lanes(u_west, -1)) * face_first
    sides[...] = turned[...].T

    at_first, at_last = lane == 0, lane == LANES - 1
    at_side = at_first | at_last
    parts, outs = (t_part, s_part, u_part, v_part), (t_out, s_out, u_out, v_out)
    chunk = lines // CHUNKS
    copies = []
    for c in range(CHUNKS):

        def tile(r, _):
            rows = pl.ds(pl.multiple_of(r * TILE, TILE), TILE)
            side = sides[rows, :]
            levels = jnp.where(at_side, count[rows, :], 0)
            for k in range(LEVELS):
                wet = levels > k
                both = roll_lanes(side, -(2 * k + 33))
                adds = (
                    jnp.where(wet, roll_lanes(side, -(2 * k + 1)), 0.0),
                    jnp.where(wet, roll_lanes(side, -(2 * k + 17)), 0.0),
                    jnp.where(at_last, both, 0.0),
                    jnp.where(at_first, both, 0.0),
                )
                for part, add, buffer in zip(parts, adds, buffers):
                    buffer[k, rows, :] = part[k, rows, :] + add
            return 0

        lax.fori_loop(c * chunk // TILE, (c + 1) * chunk // TILE, tile, 0, unroll=True)
        rows = pl.ds(c * chunk, chunk)
        for n in range(4):
            copy = pltpu.make_async_copy(buffers[n].at[:, rows, :], outs[n].at[:, rows, :], done.at[c * 4 + n])
            copy.start()
            copies.append(copy)
    for copy in copies:
        copy.wait()


def whole(n):
    return [pl.BlockSpec(memory_space=VMEM)] * n


def per_device(
    potential_warmth_degrees,
    dissolved_salt_content,
    zonal_edge_current,
    meridional_edge_current,
    wet_grid_flag,
    zonal_wet_edge_flag,
    meridional_wet_edge_flag,
    bottom_tier_count,
    zonal_grid_spacing,
    meridional_grid_spacing,
):
    t, s, u, v = potential_warmth_degrees, dissolved_salt_content, zonal_edge_current, meridional_edge_current
    zf, mf, e1, e2 = zonal_wet_edge_flag, meridional_wet_edge_flag, zonal_grid_spacing, meridional_grid_spacing
    lines = t.shape[1]
    lons, lats = lax.axis_size("lon"), lax.axis_size("lat")
    f32 = jnp.float32
    params = pltpu.CompilerParams(vmem_limit_bytes=24 * 1024 * 1024)
    packet = jax.ShapeDtypeStruct((PACKET, LANES), f32)
    field = jax.ShapeDtypeStruct(t.shape, f32)

    lat_to_a, lat_to_b = pl.pallas_call(
        row_pack,
        in_specs=[pl.BlockSpec(memory_space=pl.ANY)] * 8,
        out_specs=whole(2),
        out_shape=[packet, packet],
        scratch_shapes=[
            VMEM((7, LEVELS, TILE, LANES), f32),
            VMEM((3, LEVELS, TILE, LANES), jnp.int32),
            VMEM((3, TILE, LANES), f32),
            pltpu.SemaphoreType.DMA((13,)),
        ],
        name="row_pack",
    )(t, s, u, v, zf, mf, e1, e2)

    pairs_a = [(j, j ^ 1) for j in range(lats)]
    pairs_b = []
    for i in range(lons):
        for j in range(1, lats):
            other = (lons - 1 - i) * lats + j if j == lats - 1 else i * lats + (j + 1 if j % 2 else j - 1)
            pairs_b.append((i * lats + j, other))
    lat_a = lax.ppermute(lat_to_a, "lat", pairs_a)
    lat_b = lax.ppermute(lat_to_b, ("lon", "lat"), pairs_b)

    extended = jax.ShapeDtypeStruct((LEVELS, lines + 2 * TILE, LANES), f32)
    square = VMEM((LANES, LANES), f32)
    to_east, to_west, own, coriolis, *parts = pl.pallas_call(
        front,
        in_specs=whole(8),
        out_specs=whole(11),
        out_shape=[packet, packet, jax.ShapeDtypeStruct((72, LANES), f32), jax.ShapeDtypeStruct(e1.shape, f32)] + [extended] * 7,
        scratch_shapes=[square],
        compiler_params=params,
        name="front",
    )(t, s, u, v, zf, mf, e1, e2)

    lon_to_a, lon_to_b = pl.pallas_call(
        corner_pack,
        in_specs=whole(4),
        out_specs=whole(2),
        out_shape=[packet, packet],
        compiler_params=params,
        name="corner_pack",
    )(lat_a, lat_b, to_east, to_west)
    lon_b = lax.ppermute(lon_to_b, "lon", [(i, (i + 1 if i % 2 else i - 1) % lons) for i in range(lons)])
    lon_a = lax.ppermute(lon_to_a, "lon", [(i, i ^ 1) for i in range(lons)])

    parts = pl.pallas_call(
        middle,
        in_specs=whole(19),
        out_specs=whole(4),
        out_shape=[field] * 4,
        scratch_shapes=[VMEM((8, LEVELS, LANES), f32)],
        compiler_params=params,
        name="middle",
    )(t, s, u, v, zf, mf, bottom_tier_count, e1, e2, coriolis, *parts, lat_a, lat_b)

    return pl.pallas_call(
        finish,
        in_specs=whole(8),
        out_specs=[pl.BlockSpec(memory_space=pltpu.MemorySpace.HBM)] * 4,
        out_shape=[field] * 4,
        scratch_shapes=[square] * 2 + [VMEM(t.shape, f32)] * 4 + [pltpu.SemaphoreType.DMA((4 * CHUNKS,))],
        compiler_params=params,
        name="finish",
    )(*parts, bottom_tier_count, own, lon_a, lon_b)


def solution(mesh):
    deep, flat = P(None, "lat", "lon"), P("lat", "lon")
    return jax.shard_map(
        per_device,
        mesh=mesh,
        in_specs=(deep,) * 7 + (flat,) * 3,
        out_specs=(deep,) * 4,
        check_vma=False,
    )
```

```python
import functools
import math

import jax
import jax.numpy as jnp
from jax import lax
from jax.experimental import pallas as pl
from jax.experimental.pallas import tpu as pltpu
from jax.sharding import PartitionSpec as P

GRAVITY = 9.81
REFERENCE_DENSITY = 1026.0
TIME_STEP = 360.0
LATERAL = 300.0
VERTICAL = 0.001
ROTATION = 7.292e-05

LEVELS = 8
LANES = 128
TILE = 8
PACKET = 4 * LEVELS
CHUNKS = 3
VMEM = pltpu.MemorySpace.VMEM

THICK = [6.0 + 4.0 * k for k in range(LEVELS)]
DEPTH = [2.0 * k * k + 6.0 * k + 3.0 for k in range(LEVELS)]
SPACING = [4.0 * k + 4.0 for k in range(LEVELS)]


def lane_index(shape):
    return lax.broadcasted_iota(jnp.int32, shape, len(shape) - 1)


def roll_lanes(x, shift):
    return pltpu.roll(x, shift % LANES, x.ndim - 1)


def density(heat, salt, k):
    anom_t = heat - 10.0
    anom_s = salt - 35.0
    by_t = -0.1655 * (1.0 + 0.0001497 * DEPTH[k])
    by_s = 0.76554 * (1.0 - 1.109e-05 * DEPTH[k])
    along_t = by_t + (-0.1655 * 0.5 * 0.05952) * anom_t - 0.0024341 * anom_s
    along_s = by_s - (0.76554 * 0.5 * 0.00054914) * anom_s
    return along_t * anom_t + along_s * anom_s


def row_pack(t, s, u, v, zf, mf, e1, e2, to_a, to_b, deep, flags, flat, arrived):
    j = lax.axis_index("lat")
    even = j % 2 == 0
    top = j == lax.axis_size("lat") - 1
    last = TILE - 1
    low, high = pl.ds(0, TILE), pl.ds(t.shape[1] - TILE, TILE)
    wanted = [(t, low), (t, high), (s, low), (s, high), (u, low), (u, high), (v, high)]
    marks = [(zf, low), (zf, high), (mf, high)]
    sizes = [(e1, high), (e2, high), (e2, low)]
    copies = [pltpu.make_async_copy(ref.at[:, rows, :], deep.at[n], arrived.at[n]) for n, (ref, rows) in enumerate(wanted)]
    copies += [pltpu.make_async_copy(ref.at[:, rows, :], flags.at[n], arrived.at[7 + n]) for n, (ref, rows) in enumerate(marks)]
    copies += [pltpu.make_async_copy(ref.at[rows, :], flat.at[n], arrived.at[10 + n]) for n, (ref, rows) in enumerate(sizes)]
    for copy in copies:
        copy.start()
    for copy in copies:
        copy.wait()

    def put(out, fields):
        for number, field in enumerate(fields):
            out[number * LEVELS : (number + 1) * LEVELS, :] = field

    def upward():
        spacing_x, spacing_y = flat[0, last:, :], flat[1, last:, :]
        face = flags[2, :, last, :].astype(jnp.float32)
        return [
            deep[1, :, last, :],
            deep[3, :, last, :],
            spacing_x * deep[6, :, last, :] * face,
            LATERAL * spacing_x / spacing_y * face,
        ]

    def downward():
        flux = flat[2, :1, :] * deep[4, :, 0, :] * flags[0, :, 0, :].astype(jnp.float32)
        return [deep[0, :, 0, :], deep[2, :, 0, :], flux, jnp.zeros_like(flux)]

    @pl.when(even)
    def _():
        put(to_a, upward())
        put(to_b, downward())

    @pl.when(jnp.logical_not(even))
    def _():
        put(to_a, downward())

    @pl.when(jnp.logical_not(even) & jnp.logical_not(top))
    def _():
        put(to_b, upward())

    @pl.when(top)
    def _():
        flux = flat[1, last:, :] * deep[5, :, last, :] * flags[1, :, last, :].astype(jnp.float32)
        put(to_b, [deep[1, :, last, :], deep[3, :, last, :], -flux, jnp.zeros_like(flux)])


def from_west(x):
    return jnp.where(lane_index(x.shape) == 0, 0.0, roll_lanes(x, 1))


def from_east(x):
    return jnp.where(lane_index(x.shape) == LANES - 1, 0.0, roll_lanes(x, -1))


def front(
    t, s, u, v, zf, mf, e1, e2,
    to_east, to_west, own, coriolis, p_ext, a_ext, b_ext, u_ext, v_ext, ft_ext, fs_ext, packed,
):
    lines = t.shape[1]
    tiles = lines // TILE
    lane = lane_index((TILE, LANES))
    first_row = lax.axis_index("lat") * lines
    total_rows = lines * lax.axis_size("lat")
    packed[pl.ds(lines, LANES - lines), :] = jnp.zeros((LANES - lines, LANES), jnp.float32)

    def pack(r, _):
        rows = pl.ds(pl.multiple_of(r * TILE, TILE), TILE)
        spacing_x, spacing_y = e1[rows, :], e2[rows, :]
        ratio = LATERAL * spacing_y / spacing_x
        row = (first_row + r * TILE + lax.broadcasted_iota(jnp.int32, (TILE, LANES), 0)).astype(jnp.float32)
        latitude = 10.0 + 78.0 * (row + 0.5) / total_rows
        turn = 2.0 * ROTATION * jnp.sin(latitude * (math.pi / 180.0))
        coriolis[rows, :] = turn
        fields = [jnp.zeros((TILE, LANES), jnp.float32) for _ in range(8)]

        def keep(number, k, x, source):
            target = number * LEVELS + k
            fields[number] = jnp.where(lane == target, roll_lanes(x, target - source), fields[number])

        for k in range(LEVELS):
            heat, salt = t[k, rows, :], s[k, rows, :]
            face_x, face_y = zf[k, rows, :].astype(jnp.float32), mf[k, rows, :].astype(jnp.float32)
            keep(0, k, heat, LANES - 1)
            keep(1, k, salt, LANES - 1)
            keep(2, k, spacing_y * u[k, rows, :] * face_x, LANES - 1)
            keep(3, k, ratio * face_x, LANES - 1)
            keep(4, k, heat, 0)
            keep(5, k, salt, 0)
            keep(6, k, spacing_x * v[k, rows, :] * face_y, 0)
            keep(7, k, face_y, 0)
        total = jnp.where(lane == 68, turn, 0.0)
        for n, (x, source) in enumerate([(spacing_x, LANES - 1), (spacing_y, LANES - 1), (spacing_x, 0), (spacing_y, 0)]):
            total = jnp.where(lane == 64 + n, roll_lanes(x, 64 + n - source), total)
        for field in fields:
            total = total + field
        packed[rows, :] = total
        return 0

    lax.fori_loop(0, tiles, pack, 0, unroll=4)
    turned = packed[...].T
    to_east[...] = turned[:PACKET]
    to_west[...] = turned[PACKET : 2 * PACKET]
    own[...] = turned[: own.shape[0]]

    def heads(r, _):
        source = pl.ds(pl.multiple_of(r * TILE, TILE), TILE)
        rows = pl.ds(pl.multiple_of(r * TILE + TILE, TILE), TILE)
        head = jnp.zeros((TILE, LANES), jnp.float32)
        for k in range(LEVELS):
            half = (0.5 * THICK[k]) * density(t[k, source, :], s[k, source, :], k)
            p_ext[k, rows, :] = head + half
            head = head + 2.0 * half
        return 0

    lax.fori_loop(0, tiles, heads, 0, unroll=2)

    def faces(r, _, last=False):
        source = pl.ds(pl.multiple_of(r * TILE, TILE), TILE)
        rows = pl.ds(pl.multiple_of(r * TILE + TILE, TILE), TILE)
        above = pl.ds(r * TILE + 1, TILE)
        spacing_x, spacing_y = e1[source, :], e2[source, :]
        ratio = LATERAL * spacing_x / spacing_y
        for k in range(LEVELS):
            flux_x = spacing_y * u[k, source, :] * zf[k, source, :].astype(jnp.float32)
            u_ext[k, rows, :] = flux_x
            a_ext[k, rows, :] = flux_x + from_west(flux_x)
            face = mf[k, source, :].astype(jnp.float32)
            flux_y = spacing_x * v[k, source, :] * face
            v_ext[k, rows, :] = flux_y
            b_ext[k, rows, :] = flux_y + from_east(flux_y)
            if not last:
                here, there = 0.5 * flux_y + ratio * face, 0.5 * flux_y - ratio * face
                ft_ext[k, rows, :] = here * t[k, source, :] + there * t[k, above, :]
                fs_ext[k, rows, :] = here * s[k, source, :] + there * s[k, above, :]
        return 0

    lax.fori_loop(0, tiles - 1, faces, 0, unroll=3)
    faces(tiles - 1, 0, last=True)


def corner_pack(from_a, from_b, to_east, to_west, to_a, to_b):
    even_j = lax.axis_index("lat") % 2 == 0
    even_i = lax.axis_index("lon") % 2 == 0
    shape = (PACKET, LANES)
    row = lax.broadcasted_iota(jnp.int32, shape, 0)
    corner = (lane_index(shape) == 96) & (row >= 2 * LEVELS) & (row < 3 * LEVELS)
    first, second = from_a[...], from_b[...]
    north = jnp.where(even_j, first, second)
    south = jnp.where(even_j, second, first)
    top = lax.axis_index("lat") == lax.axis_size("lat") - 1
    last_north = jnp.where(top, roll_lanes(north, 96), roll_lanes(north, 96 - (LANES - 1)))
    east = jnp.where(corner, last_north, to_east[...])
    west = jnp.where(corner, roll_lanes(south, 96), to_west[...])
    to_a[...] = jnp.where(even_i, east, west)
    to_b[...] = jnp.where(even_i, west, east)


def middle(
    t, s, u, v, zf, mf, count, e1, e2, coriolis, p_ext, a_ext, b_ext, u_ext, v_ext, ft_ext, fs_ext, lat_a, lat_b,
    t_out, s_out, u_out, v_out, beyond, beyond_north,
):
    lines = t.shape[1]
    tiles = lines // TILE
    even_j = lax.axis_index("lat") % 2 == 0

    def pick(ref_true, ref_false, flag, number):
        rows = slice(number * LEVELS, (number + 1) * LEVELS)
        return jnp.where(flag, ref_true[rows, :], ref_false[rows, :])

    beyond_north[...] = jnp.where(even_j, lat_a[: 3 * LEVELS, :], lat_b[: 3 * LEVELS, :])

    @pl.when(lax.axis_index("lat") == lax.axis_size("lat") - 1)
    def _():
        shape = (LANES, LANES)
        mirror = lane_index(shape) + lax.broadcasted_iota(jnp.int32, shape, 0) == LANES - 1
        beyond_north[...] = lax.dot(
            beyond_north[...], mirror.astype(jnp.float32), precision=lax.Precision.HIGHEST, preferred_element_type=jnp.float32
        )

    north = [beyond_north[n * LEVELS : (n + 1) * LEVELS, :] for n in range(3)]
    south = [pick(lat_b, lat_a, even_j, n) for n in range(4)]
    here, there = 0.5 * south[2] + south[3], 0.5 * south[2] - south[3]
    beyond[0] = north[0]
    beyond[1] = north[1]
    beyond[2] = north[2] + from_west(north[2])
    beyond[4] = south[2] + from_east(south[2])
    beyond[5] = south[2]
    beyond[6] = here * south[0] + there * t[:, 0, :]
    beyond[7] = here * south[1] + there * s[:, 0, :]
    head = jnp.zeros((1, LANES), jnp.float32)
    for k in range(LEVELS):
        half = (0.5 * THICK[k]) * density(beyond[0, k : k + 1, :], beyond[1, k : k + 1, :], k)
        beyond[3, k : k + 1, :] = head + half
        head = head + 2.0 * half

    row = lax.broadcasted_iota(jnp.int32, (TILE, LANES), 0)

    def update(r, _, first=False, last=False):
        source = pl.ds(pl.multiple_of(r * TILE, TILE), TILE)
        rows = pl.ds(pl.multiple_of(r * TILE + TILE, TILE), TILE)
        spacing_x, spacing_y = e1[source, :], e2[source, :]
        levels = count[source, :]
        inverse_x, inverse_y = 1.0 / spacing_x, 1.0 / spacing_y
        ratio_x, ratio_y = LATERAL * spacing_y * inverse_x, LATERAL * spacing_x * inverse_y
        area = spacing_x * spacing_y
        per_area = TIME_STEP * inverse_x * inverse_y
        turn = (0.25 * TIME_STEP) * coriolis[source, :]
        turn_x, turn_y = turn * inverse_x, turn * inverse_y
        push = -TIME_STEP * GRAVITY / REFERENCE_DENSITY
        push_x, push_y = push * inverse_x, push * inverse_y
        zero = jnp.zeros((TILE, LANES), jnp.float32)

        def above(ref, k, number, offset=TILE):
            if last:
                return jnp.where(row == TILE - 1, beyond[number, k : k + 1, :], pltpu.roll(ref[k, pl.ds(r * TILE + offset, TILE), :], TILE - 1, 0))
            return ref[k, pl.ds(r * TILE + offset + 1, TILE), :]

        def below(ref, k, number):
            if first:
                return jnp.where(row == 0, beyond[number, k : k + 1, :], pltpu.roll(ref[k, rows, :], 1, 0))
            return ref[k, pl.ds(r * TILE + TILE - 1, TILE), :]

        upward, t_below, s_below, u_below, v_below = zero, zero, zero, zero, zero
        for k in reversed(range(LEVELS)):
            heat, salt = t[k, source, :], s[k, source, :]
            flux_x, flux_y = u_ext[k, rows, :], v_ext[k, rows, :]
            face_x, face_y = zf[k, source, :].astype(jnp.float32), mf[k, source, :].astype(jnp.float32)
            both_x, both_y = a_ext[k, rows, :], b_ext[k, rows, :]
            wet = levels > k
            spread = ratio_x * face_x
            here, there = 0.5 * flux_x + spread, 0.5 * flux_x - spread
            t_east = here * heat + there * from_east(heat)
            s_east = here * salt + there * from_east(salt)
            if last:
                here, there = 0.5 * flux_y + ratio_y * face_y, 0.5 * flux_y - ratio_y * face_y
                t_north, s_north = here * heat + there * above(t, k, 0, 0), here * salt + there * above(s, k, 1, 0)
                under = pl.ds(r * TILE + TILE - 1, 1)
                t_south = jnp.where(row == 0, ft_ext[k, under, :], pltpu.roll(t_north, 1, 0))
                s_south = jnp.where(row == 0, fs_ext[k, under, :], pltpu.roll(s_north, 1, 0))
            else:
                t_north, s_north = ft_ext[k, rows, :], fs_ext[k, rows, :]
                t_south, s_south = below(ft_ext, k, 6), below(fs_ext, k, 7)
            t_net = t_east - from_west(t_east) + t_north - t_south
            s_net = s_east - from_west(s_east) + s_north - s_south
            converge = 2.0 * flux_x - both_x + flux_y - below(v_ext, k, 5)
            upward = upward - THICK[k] * converge
            if k > 0:
                mix = jnp.where(wet, (VERTICAL / SPACING[k]) * area, 0.0)
                upper, lower = 0.5 * upward - mix, 0.5 * upward + mix
                t_above = upper * t[k - 1, source, :] + lower * heat
                s_above = upper * s[k - 1, source, :] + lower * salt
            else:
                t_above, s_above = upward * heat, upward * salt
            t_net = t_net + (t_above - t_below) * (1.0 / THICK[k])
            s_net = s_net + (s_above - s_below) * (1.0 / THICK[k])
            t_below, s_below = t_above, s_above
            t_out[k, source, :] = jnp.where(wet, heat - per_area * t_net, 0.0)
            s_out[k, source, :] = jnp.where(wet, salt - per_area * s_net, 0.0)
            zonal, meridional = u[k, source, :], v[k, source, :]
            if k > 0:
                u_above = (VERTICAL / SPACING[k]) * (u[k - 1, source, :] - zonal) * face_x
                v_above = (VERTICAL / SPACING[k]) * (v[k - 1, source, :] - meridional) * face_y
            else:
                u_above, v_above = zero, zero
            head = p_ext[k, rows, :]
            slope_x = from_east(head) - head
            slope_y = above(p_ext, k, 3) - head
            share = TIME_STEP / THICK[k]
            u_out[k, source, :] = (
                zonal + push_x * slope_x + turn_x * (both_y + below(b_ext, k, 4)) + share * (u_above - u_below)
            ) * face_x
            v_out[k, source, :] = (
                meridional + push_y * slope_y - turn_y * (both_x + above(a_ext, k, 2)) + share * (v_above - v_below)
            ) * face_y
            u_below, v_below = u_above, v_above
        return 0

    update(0, 0, first=True)
    lax.fori_loop(1, tiles - 1, update, 0, unroll=2)
    update(tiles - 1, 0, last=True)


def running_sum(x, level, upward):
    for step in (1, 2, 4):
        if upward:
            x = x + jnp.where(level < LEVELS - step, pltpu.roll(x, LEVELS - step, 0), 0.0)
        else:
            x = x + jnp.where(level >= step, pltpu.roll(x, step, 0), 0.0)
    return x


def finish(t_part, s_part, u_part, v_part, count, own, lon_b, lon_a, t_out, s_out, u_out, v_out, turned, sides, *buffers_and_done):
    buffers, done = buffers_and_done[:4], buffers_and_done[4]
    lines = t_part.shape[1]
    even_i = lax.axis_index("lon") % 2 == 0

    def pick(ref_true, ref_false, flag, number):
        rows = slice(number * LEVELS, (number + 1) * LEVELS)
        return jnp.where(flag, ref_true[rows, :], ref_false[rows, :])

    t_east, s_east, v_east = [pick(lon_a, lon_b, even_i, n) for n in range(3)]
    t_west, s_west, u_west, g_west = [pick(lon_b, lon_a, even_i, n) for n in range(4)]
    shape = (LEVELS, LANES)
    level, lane = lax.broadcasted_iota(jnp.int32, shape, 0), lane_index(shape)
    depth_index = level.astype(jnp.float32)
    thick = 6.0 + 4.0 * depth_index
    depth = 2.0 * depth_index * depth_index + 6.0 * depth_index + 3.0

    def mine(number):
        return own[number * LEVELS : (number + 1) * LEVELS, :]

    def single(number):
        return own[64 + number : 65 + number, :]

    u_last, g_last, t_first, s_first, face_first = mine(2), mine(3), mine(4), mine(5), mine(7)
    turn = (0.25 * TIME_STEP) * single(4)
    push = -TIME_STEP * GRAVITY / REFERENCE_DENSITY
    inverse_x, inverse_y = 1.0 / single(0), 1.0 / single(1)
    back = -(TIME_STEP * inverse_x * inverse_y) * (0.5 * u_last - g_last)
    anom_t, anom_s = t_east - 10.0, s_east - 35.0
    weight = 0.5 * thick * (
        (-0.1655 * (1.0 + 0.0001497 * depth) + (-0.1655 * 0.5 * 0.05952) * anom_t - 0.0024341 * anom_s) * anom_t
        + (0.76554 * (1.0 - 1.109e-05 * depth) - (0.76554 * 0.5 * 0.00054914) * anom_s) * anom_s
    )
    head = 2.0 * running_sum(weight, level, False) - weight
    v_south_east = jnp.where(lane == 0, roll_lanes(v_east, -lines), roll_lanes(v_east, 1))
    u_add = jnp.where(g_last > 0.0, (push * inverse_x) * head + (turn * inverse_x) * (v_east + v_south_east), 0.0)
    turned[...] = jnp.zeros_like(turned)
    turned[pl.ds(0, LEVELS, 2), :] = back * t_east
    turned[pl.ds(16, LEVELS, 2), :] = back * s_east
    turned[pl.ds(32, LEVELS, 2), :] = u_add
    inverse_x, inverse_y = 1.0 / single(2), 1.0 / single(3)
    scale = -(TIME_STEP * inverse_x * inverse_y)
    here, there = 0.5 * u_west + g_west, 0.5 * u_west - g_west
    upward = running_sum(0.5 * thick * u_west, level, True)

    def first_column(q_west, q):
        flux = upward * (q + jnp.where(level == 0, q, pltpu.roll(q, 1, 0)))
        under = jnp.where(level == LEVELS - 1, 0.0, pltpu.roll(flux, LEVELS - 1, 0))
        return scale * ((flux - under) / thick - (here * q_west + there * q))

    turned[pl.ds(1, LEVELS, 2), :] = first_column(t_west, t_first)
    turned[pl.ds(17, LEVELS, 2), :] = first_column(s_west, s_first)
    turned[pl.ds(33, LEVELS, 2), :] = -(turn * inverse_y) * (u_west + roll_lanes(u_west, -1)) * face_first
    sides[...] = turned[...].T

    at_first, at_last = lane == 0, lane == LANES - 1
    at_side = at_first | at_last
    parts, outs = (t_part, s_part, u_part, v_part), (t_out, s_out, u_out, v_out)
    chunk = lines // CHUNKS
    copies = []
    for c in range(CHUNKS):

        def tile(r, _):
            rows = pl.ds(pl.multiple_of(r * TILE, TILE), TILE)
            side = sides[rows, :]
            levels = jnp.where(at_side, count[rows, :], 0)
            for k in range(LEVELS):
                wet = levels > k
                both = roll_lanes(side, -(2 * k + 33))
                adds = (
                    jnp.where(wet, roll_lanes(side, -(2 * k + 1)), 0.0),
                    jnp.where(wet, roll_lanes(side, -(2 * k + 17)), 0.0),
                    jnp.where(at_last, both, 0.0),
                    jnp.where(at_first, both, 0.0),
                )
                for part, add, buffer in zip(parts, adds, buffers):
                    buffer[k, rows, :] = part[k, rows, :] + add
            return 0

        lax.fori_loop(c * chunk // TILE, (c + 1) * chunk // TILE, tile, 0, unroll=True)
        rows = pl.ds(c * chunk, chunk)
        for n in range(4):
            copy = pltpu.make_async_copy(buffers[n].at[:, rows, :], outs[n].at[:, rows, :], done.at[c * 4 + n])
            copy.start()
            copies.append(copy)
    for copy in copies:
        copy.wait()


def whole(n):
    return [pl.BlockSpec(memory_space=VMEM)] * n


def per_device(
    potential_warmth_degrees,
    dissolved_salt_content,
    zonal_edge_current,
    meridional_edge_current,
    wet_grid_flag,
    zonal_wet_edge_flag,
    meridional_wet_edge_flag,
    bottom_tier_count,
    zonal_grid_spacing,
    meridional_grid_spacing,
):
    t, s, u, v = potential_warmth_degrees, dissolved_salt_content, zonal_edge_current, meridional_edge_current
    zf, mf, e1, e2 = zonal_wet_edge_flag, meridional_wet_edge_flag, zonal_grid_spacing, meridional_grid_spacing
    lines = t.shape[1]
    lons, lats = lax.axis_size("lon"), lax.axis_size("lat")
    f32 = jnp.float32
    params = pltpu.CompilerParams(vmem_limit_bytes=24 * 1024 * 1024)
    packet = jax.ShapeDtypeStruct((PACKET, LANES), f32)
    field = jax.ShapeDtypeStruct(t.shape, f32)

    lat_to_a, lat_to_b = pl.pallas_call(
        row_pack,
        in_specs=[pl.BlockSpec(memory_space=pl.ANY)] * 8,
        out_specs=whole(2),
        out_shape=[packet, packet],
        scratch_shapes=[
            VMEM((7, LEVELS, TILE, LANES), f32),
            VMEM((3, LEVELS, TILE, LANES), jnp.int32),
            VMEM((3, TILE, LANES), f32),
            pltpu.SemaphoreType.DMA((13,)),
        ],
        name="row_pack",
    )(t, s, u, v, zf, mf, e1, e2)

    pairs_a = [(j, j ^ 1) for j in range(lats)]
    pairs_b = []
    for i in range(lons):
        for j in range(1, lats):
            other = (lons - 1 - i) * lats + j if j == lats - 1 else i * lats + (j + 1 if j % 2 else j - 1)
            pairs_b.append((i * lats + j, other))
    lat_a = lax.ppermute(lat_to_a, "lat", pairs_a)
    lat_b = lax.ppermute(lat_to_b, ("lon", "lat"), pairs_b)

    extended = jax.ShapeDtypeStruct((LEVELS, lines + 2 * TILE, LANES), f32)
    square = VMEM((LANES, LANES), f32)
    to_east, to_west, own, coriolis, *parts = pl.pallas_call(
        front,
        in_specs=whole(8),
        out_specs=whole(11),
        out_shape=[packet, packet, jax.ShapeDtypeStruct((72, LANES), f32), jax.ShapeDtypeStruct(e1.shape, f32)] + [extended] * 7,
        scratch_shapes=[square],
        compiler_params=params,
        name="front",
    )(t, s, u, v, zf, mf, e1, e2)

    lon_to_a, lon_to_b = pl.pallas_call(
        corner_pack,
        in_specs=whole(4),
        out_specs=whole(2),
        out_shape=[packet, packet],
        compiler_params=params,
        name="corner_pack",
    )(lat_a, lat_b, to_east, to_west)
    lon_b = lax.ppermute(lon_to_b, "lon", [(i, (i + 1 if i % 2 else i - 1) % lons) for i in range(lons)])
    lon_a = lax.ppermute(lon_to_a, "lon", [(i, i ^ 1) for i in range(lons)])

    parts = pl.pallas_call(
        middle,
        in_specs=whole(19),
        out_specs=whole(4),
        out_shape=[field] * 4,
        scratch_shapes=[VMEM((8, LEVELS, LANES), f32), VMEM((3 * LEVELS, LANES), f32)],
        compiler_params=params,
        name="middle",
    )(t, s, u, v, zf, mf, bottom_tier_count, e1, e2, coriolis, *parts, lat_a, lat_b)

    return pl.pallas_call(
        finish,
        in_specs=whole(8),
        out_specs=[pl.BlockSpec(memory_space=pltpu.MemorySpace.HBM)] * 4,
        out_shape=[field] * 4,
        scratch_shapes=[square] * 2 + [VMEM(t.shape, f32)] * 4 + [pltpu.SemaphoreType.DMA((4 * CHUNKS,))],
        compiler_params=params,
        name="finish",
    )(*parts, bottom_tier_count, own, lon_b, lon_a)


def solution(mesh):
    deep, flat = P(None, "lat", "lon"), P("lat", "lon")
    return jax.shard_map(
        per_device,
        mesh=mesh,
        in_specs=(deep,) * 7 + (flat,) * 3,
        out_specs=(deep,) * 4,
        check_vma=False,
    )
```

```python
import functools
import math

import jax
import jax.numpy as jnp
from jax import lax
from jax.experimental import pallas as pl
from jax.experimental.pallas import tpu as pltpu
from jax.sharding import PartitionSpec as P

GRAVITY = 9.81
REFERENCE_DENSITY = 1026.0
TIME_STEP = 360.0
LATERAL = 300.0
VERTICAL = 0.001
ROTATION = 7.292e-05

LEVELS = 8
LANES = 128
TILE = 8
PACKET = 4 * LEVELS
CHUNKS = 3
EARLY = 7
VMEM = pltpu.MemorySpace.VMEM

THICK = [6.0 + 4.0 * k for k in range(LEVELS)]
DEPTH = [2.0 * k * k + 6.0 * k + 3.0 for k in range(LEVELS)]
SPACING = [4.0 * k + 4.0 for k in range(LEVELS)]


def lane_index(shape):
    return lax.broadcasted_iota(jnp.int32, shape, len(shape) - 1)


def roll_lanes(x, shift):
    return pltpu.roll(x, shift % LANES, x.ndim - 1)


def density(heat, salt, k):
    anom_t = heat - 10.0
    anom_s = salt - 35.0
    by_t = -0.1655 * (1.0 + 0.0001497 * DEPTH[k])
    by_s = 0.76554 * (1.0 - 1.109e-05 * DEPTH[k])
    along_t = by_t + (-0.1655 * 0.5 * 0.05952) * anom_t - 0.0024341 * anom_s
    along_s = by_s - (0.76554 * 0.5 * 0.00054914) * anom_s
    return along_t * anom_t + along_s * anom_s


def row_pack(t, s, u, v, zf, mf, e1, e2, bottom, to_a, to_b, count, deep, flags, flat, arrived):
    j = lax.axis_index("lat")
    even = j % 2 == 0
    top = j == lax.axis_size("lat") - 1
    last = TILE - 1
    low, high = pl.ds(0, TILE), pl.ds(t.shape[1] - TILE, TILE)
    wanted = [(t, low), (t, high), (s, low), (s, high), (u, low), (u, high), (v, high)]
    marks = [(zf, low), (zf, high), (mf, high)]
    sizes = [(e1, high), (e2, high), (e2, low)]
    copies = [pltpu.make_async_copy(ref.at[:, rows, :], deep.at[n], arrived.at[n]) for n, (ref, rows) in enumerate(wanted)]
    copies += [pltpu.make_async_copy(ref.at[:, rows, :], flags.at[n], arrived.at[7 + n]) for n, (ref, rows) in enumerate(marks)]
    copies += [pltpu.make_async_copy(ref.at[rows, :], flat.at[n], arrived.at[10 + n]) for n, (ref, rows) in enumerate(sizes)]
    copies.append(pltpu.make_async_copy(bottom, count, arrived.at[13]))
    for copy in copies:
        copy.start()
    for copy in copies:
        copy.wait()

    def put(out, fields):
        for number, field in enumerate(fields):
            out[number * LEVELS : (number + 1) * LEVELS, :] = field

    def upward():
        spacing_x, spacing_y = flat[0, last:, :], flat[1, last:, :]
        face = flags[2, :, last, :].astype(jnp.float32)
        return [
            deep[1, :, last, :],
            deep[3, :, last, :],
            spacing_x * deep[6, :, last, :] * face,
            LATERAL * spacing_x / spacing_y * face,
        ]

    def downward():
        flux = flat[2, :1, :] * deep[4, :, 0, :] * flags[0, :, 0, :].astype(jnp.float32)
        return [deep[0, :, 0, :], deep[2, :, 0, :], flux, jnp.zeros_like(flux)]

    @pl.when(even)
    def _():
        put(to_a, upward())
        put(to_b, downward())

    @pl.when(jnp.logical_not(even))
    def _():
        put(to_a, downward())

    @pl.when(jnp.logical_not(even) & jnp.logical_not(top))
    def _():
        put(to_b, upward())

    @pl.when(top)
    def _():
        flux = flat[1, last:, :] * deep[5, :, last, :] * flags[1, :, last, :].astype(jnp.float32)
        put(to_b, [deep[1, :, last, :], deep[3, :, last, :], -flux, jnp.zeros_like(flux)])


def from_west(x):
    return jnp.where(lane_index(x.shape) == 0, 0.0, roll_lanes(x, 1))


def from_east(x):
    return jnp.where(lane_index(x.shape) == LANES - 1, 0.0, roll_lanes(x, -1))


def tile_update(
    t, s, u, v, zf, mf, count, e1, e2, coriolis, p_ext, a_ext, b_ext, u_ext, v_ext, ft_ext, fs_ext,
    t_out, s_out, u_out, v_out, beyond,
):
    row = lax.broadcasted_iota(jnp.int32, (TILE, LANES), 0)

    def update(r, _, first=False, last=False):
        source = pl.ds(pl.multiple_of(r * TILE, TILE), TILE)
        rows = pl.ds(pl.multiple_of(r * TILE + TILE, TILE), TILE)
        spacing_x, spacing_y = e1[source, :], e2[source, :]
        levels = count[source, :]
        inverse_x, inverse_y = 1.0 / spacing_x, 1.0 / spacing_y
        ratio_x, ratio_y = LATERAL * spacing_y * inverse_x, LATERAL * spacing_x * inverse_y
        area = spacing_x * spacing_y
        per_area = TIME_STEP * inverse_x * inverse_y
        turn = (0.25 * TIME_STEP) * coriolis[source, :]
        turn_x, turn_y = turn * inverse_x, turn * inverse_y
        push = -TIME_STEP * GRAVITY / REFERENCE_DENSITY
        push_x, push_y = push * inverse_x, push * inverse_y
        zero = jnp.zeros((TILE, LANES), jnp.float32)

        def above(ref, k, number, offset=TILE):
            if last:
                return jnp.where(row == TILE - 1, beyond[number, k : k + 1, :], pltpu.roll(ref[k, pl.ds(r * TILE + offset, TILE), :], TILE - 1, 0))
            return ref[k, pl.ds(r * TILE + offset + 1, TILE), :]

        def below(ref, k, number):
            if first:
                return jnp.where(row == 0, beyond[number, k : k + 1, :], pltpu.roll(ref[k, rows, :], 1, 0))
            return ref[k, pl.ds(r * TILE + TILE - 1, TILE), :]

        upward, t_below, s_below, u_below, v_below = zero, zero, zero, zero, zero
        for k in reversed(range(LEVELS)):
            heat, salt = t[k, source, :], s[k, source, :]
            flux_x, flux_y = u_ext[k, rows, :], v_ext[k, rows, :]
            face_x, face_y = zf[k, source, :].astype(jnp.float32), mf[k, source, :].astype(jnp.float32)
            both_x, both_y = a_ext[k, rows, :], b_ext[k, rows, :]
            wet = levels > k
            spread = ratio_x * face_x
            here, there = 0.5 * flux_x + spread, 0.5 * flux_x - spread
            t_east = here * heat + there * from_east(heat)
            s_east = here * salt + there * from_east(salt)
            if last:
                here, there = 0.5 * flux_y + ratio_y * face_y, 0.5 * flux_y - ratio_y * face_y
                t_north, s_north = here * heat + there * above(t, k, 0, 0), here * salt + there * above(s, k, 1, 0)
                under = pl.ds(r * TILE + TILE - 1, 1)
                t_south = jnp.where(row == 0, ft_ext[k, under, :], pltpu.roll(t_north, 1, 0))
                s_south = jnp.where(row == 0, fs_ext[k, under, :], pltpu.roll(s_north, 1, 0))
            else:
                t_north, s_north = ft_ext[k, rows, :], fs_ext[k, rows, :]
                t_south, s_south = below(ft_ext, k, 6), below(fs_ext, k, 7)
            t_net = t_east - from_west(t_east) + t_north - t_south
            s_net = s_east - from_west(s_east) + s_north - s_south
            converge = 2.0 * flux_x - both_x + flux_y - below(v_ext, k, 5)
            upward = upward - THICK[k] * converge
            if k > 0:
                mix = jnp.where(wet, (VERTICAL / SPACING[k]) * area, 0.0)
                upper, lower = 0.5 * upward - mix, 0.5 * upward + mix
                t_above = upper * t[k - 1, source, :] + lower * heat
                s_above = upper * s[k - 1, source, :] + lower * salt
            else:
                t_above, s_above = upward * heat, upward * salt
            t_net = t_net + (t_above - t_below) * (1.0 / THICK[k])
            s_net = s_net + (s_above - s_below) * (1.0 / THICK[k])
            t_below, s_below = t_above, s_above
            t_out[k, source, :] = jnp.where(wet, heat - per_area * t_net, 0.0)
            s_out[k, source, :] = jnp.where(wet, salt - per_area * s_net, 0.0)
            zonal, meridional = u[k, source, :], v[k, source, :]
            if k > 0:
                u_above = (VERTICAL / SPACING[k]) * (u[k - 1, source, :] - zonal) * face_x
                v_above = (VERTICAL / SPACING[k]) * (v[k - 1, source, :] - meridional) * face_y
            else:
                u_above, v_above = zero, zero
            head = p_ext[k, rows, :]
            slope_x = from_east(head) - head
            slope_y = above(p_ext, k, 3) - head
            share = TIME_STEP / THICK[k]
            u_out[k, source, :] = (
                zonal + push_x * slope_x + turn_x * (both_y + below(b_ext, k, 4)) + share * (u_above - u_below)
            ) * face_x
            v_out[k, source, :] = (
                meridional + push_y * slope_y - turn_y * (both_x + above(a_ext, k, 2)) + share * (v_above - v_below)
            ) * face_y
            u_below, v_below = u_above, v_above
        return 0

    return update


def front(
    t, s, u, v, zf, mf, count, e1, e2,
    to_east, to_west, own, coriolis, p_ext, a_ext, b_ext, u_ext, v_ext, ft_ext, fs_ext,
    t_out, s_out, u_out, v_out, packed,
):
    lines = t.shape[1]
    tiles = lines // TILE
    lane = lane_index((TILE, LANES))
    first_row = lax.axis_index("lat") * lines
    total_rows = lines * lax.axis_size("lat")
    packed[pl.ds(lines, LANES - lines), :] = jnp.zeros((LANES - lines, LANES), jnp.float32)

    def pack(r, _):
        rows = pl.ds(pl.multiple_of(r * TILE, TILE), TILE)
        spacing_x, spacing_y = e1[rows, :], e2[rows, :]
        ratio = LATERAL * spacing_y / spacing_x
        row = (first_row + r * TILE + lax.broadcasted_iota(jnp.int32, (TILE, LANES), 0)).astype(jnp.float32)
        latitude = 10.0 + 78.0 * (row + 0.5) / total_rows
        turn = 2.0 * ROTATION * jnp.sin(latitude * (math.pi / 180.0))
        coriolis[rows, :] = turn
        fields = [jnp.zeros((TILE, LANES), jnp.float32) for _ in range(8)]

        def keep(number, k, x, source):
            target = number * LEVELS + k
            fields[number] = jnp.where(lane == target, roll_lanes(x, target - source), fields[number])

        for k in range(LEVELS):
            heat, salt = t[k, rows, :], s[k, rows, :]
            face_x, face_y = zf[k, rows, :].astype(jnp.float32), mf[k, rows, :].astype(jnp.float32)
            keep(0, k, heat, LANES - 1)
            keep(1, k, salt, LANES - 1)
            keep(2, k, spacing_y * u[k, rows, :] * face_x, LANES - 1)
            keep(3, k, ratio * face_x, LANES - 1)
            keep(4, k, heat, 0)
            keep(5, k, salt, 0)
            keep(6, k, spacing_x * v[k, rows, :] * face_y, 0)
            keep(7, k, face_y, 0)
        total = jnp.where(lane == 68, turn, 0.0)
        for n, (x, source) in enumerate([(spacing_x, LANES - 1), (spacing_y, LANES - 1), (spacing_x, 0), (spacing_y, 0)]):
            total = jnp.where(lane == 64 + n, roll_lanes(x, 64 + n - source), total)
        for field in fields:
            total = total + field
        packed[rows, :] = total
        return 0

    lax.fori_loop(0, tiles, pack, 0, unroll=4)
    turned = packed[...].T
    to_east[...] = turned[:PACKET]
    to_west[...] = turned[PACKET : 2 * PACKET]
    own[...] = turned[: own.shape[0]]

    def heads(r, _):
        source = pl.ds(pl.multiple_of(r * TILE, TILE), TILE)
        rows = pl.ds(pl.multiple_of(r * TILE + TILE, TILE), TILE)
        head = jnp.zeros((TILE, LANES), jnp.float32)
        for k in range(LEVELS):
            half = (0.5 * THICK[k]) * density(t[k, source, :], s[k, source, :], k)
            p_ext[k, rows, :] = head + half
            head = head + 2.0 * half
        return 0

    lax.fori_loop(0, tiles, heads, 0, unroll=2)

    def faces(r, _, last=False):
        source = pl.ds(pl.multiple_of(r * TILE, TILE), TILE)
        rows = pl.ds(pl.multiple_of(r * TILE + TILE, TILE), TILE)
        above = pl.ds(r * TILE + 1, TILE)
        spacing_x, spacing_y = e1[source, :], e2[source, :]
        ratio = LATERAL * spacing_x / spacing_y
        for k in range(LEVELS):
            flux_x = spacing_y * u[k, source, :] * zf[k, source, :].astype(jnp.float32)
            u_ext[k, rows, :] = flux_x
            a_ext[k, rows, :] = flux_x + from_west(flux_x)
            face = mf[k, source, :].astype(jnp.float32)
            flux_y = spacing_x * v[k, source, :] * face
            v_ext[k, rows, :] = flux_y
            b_ext[k, rows, :] = flux_y + from_east(flux_y)
            if not last:
                here, there = 0.5 * flux_y + ratio * face, 0.5 * flux_y - ratio * face
                ft_ext[k, rows, :] = here * t[k, source, :] + there * t[k, above, :]
                fs_ext[k, rows, :] = here * s[k, source, :] + there * s[k, above, :]
        return 0

    lax.fori_loop(0, tiles - 1, faces, 0, unroll=3)
    faces(tiles - 1, 0, last=True)
    update = tile_update(
        t, s, u, v, zf, mf, count, e1, e2, coriolis, p_ext, a_ext, b_ext, u_ext, v_ext, ft_ext, fs_ext,
        t_out, s_out, u_out, v_out, None,
    )
    lax.fori_loop(1, EARLY, update, 0, unroll=2)


def corner_pack(from_a, from_b, to_east, to_west, to_a, to_b):
    even_j = lax.axis_index("lat") % 2 == 0
    even_i = lax.axis_index("lon") % 2 == 0
    shape = (PACKET, LANES)
    row = lax.broadcasted_iota(jnp.int32, shape, 0)
    corner = (lane_index(shape) == 96) & (row >= 2 * LEVELS) & (row < 3 * LEVELS)
    first, second = from_a[...], from_b[...]
    north = jnp.where(even_j, first, second)
    south = jnp.where(even_j, second, first)
    top = lax.axis_index("lat") == lax.axis_size("lat") - 1
    last_north = jnp.where(top, roll_lanes(north, 96), roll_lanes(north, 96 - (LANES - 1)))
    east = jnp.where(corner, last_north, to_east[...])
    west = jnp.where(corner, roll_lanes(south, 96), to_west[...])
    to_a[...] = jnp.where(even_i, east, west)
    to_b[...] = jnp.where(even_i, west, east)


def middle(
    t, s, u, v, zf, mf, count, e1, e2, coriolis, p_ext, a_ext, b_ext, u_ext, v_ext, ft_ext, fs_ext, lat_a, lat_b,
    t_out, s_out, u_out, v_out, beyond, beyond_north,
):
    lines = t.shape[1]
    tiles = lines // TILE
    even_j = lax.axis_index("lat") % 2 == 0

    def pick(ref_true, ref_false, flag, number):
        rows = slice(number * LEVELS, (number + 1) * LEVELS)
        return jnp.where(flag, ref_true[rows, :], ref_false[rows, :])

    beyond_north[...] = jnp.where(even_j, lat_a[: 3 * LEVELS, :], lat_b[: 3 * LEVELS, :])

    @pl.when(lax.axis_index("lat") == lax.axis_size("lat") - 1)
    def _():
        shape = (LANES, LANES)
        mirror = lane_index(shape) + lax.broadcasted_iota(jnp.int32, shape, 0) == LANES - 1
        beyond_north[...] = lax.dot(
            beyond_north[...], mirror.astype(jnp.float32), precision=lax.Precision.HIGHEST, preferred_element_type=jnp.float32
        )

    north = [beyond_north[n * LEVELS : (n + 1) * LEVELS, :] for n in range(3)]
    south = [pick(lat_b, lat_a, even_j, n) for n in range(4)]
    here, there = 0.5 * south[2] + south[3], 0.5 * south[2] - south[3]
    beyond[0] = north[0]
    beyond[1] = north[1]
    beyond[2] = north[2] + from_west(north[2])
    beyond[4] = south[2] + from_east(south[2])
    beyond[5] = south[2]
    beyond[6] = here * south[0] + there * t[:, 0, :]
    beyond[7] = here * south[1] + there * s[:, 0, :]
    head = jnp.zeros((1, LANES), jnp.float32)
    for k in range(LEVELS):
        half = (0.5 * THICK[k]) * density(beyond[0, k : k + 1, :], beyond[1, k : k + 1, :], k)
        beyond[3, k : k + 1, :] = head + half
        head = head + 2.0 * half

    update = tile_update(
        t, s, u, v, zf, mf, count, e1, e2, coriolis, p_ext, a_ext, b_ext, u_ext, v_ext, ft_ext, fs_ext,
        t_out, s_out, u_out, v_out, beyond,
    )
    update(0, 0, first=True)
    lax.fori_loop(EARLY, tiles - 1, update, 0, unroll=2)
    update(tiles - 1, 0, last=True)


def running_sum(x, level, upward):
    for step in (1, 2, 4):
        if upward:
            x = x + jnp.where(level < LEVELS - step, pltpu.roll(x, LEVELS - step, 0), 0.0)
        else:
            x = x + jnp.where(level >= step, pltpu.roll(x, step, 0), 0.0)
    return x


def finish(t_early, s_early, u_early, v_early, t_part, s_part, u_part, v_part, count, own, lon_b, lon_a, t_out, s_out, u_out, v_out, turned, sides, *buffers_and_done):
    buffers, done = buffers_and_done[:4], buffers_and_done[4]
    lines = t_part.shape[1]
    even_i = lax.axis_index("lon") % 2 == 0

    def pick(ref_true, ref_false, flag, number):
        rows = slice(number * LEVELS, (number + 1) * LEVELS)
        return jnp.where(flag, ref_true[rows, :], ref_false[rows, :])

    t_east, s_east, v_east = [pick(lon_a, lon_b, even_i, n) for n in range(3)]
    t_west, s_west, u_west, g_west = [pick(lon_b, lon_a, even_i, n) for n in range(4)]
    shape = (LEVELS, LANES)
    level, lane = lax.broadcasted_iota(jnp.int32, shape, 0), lane_index(shape)
    depth_index = level.astype(jnp.float32)
    thick = 6.0 + 4.0 * depth_index
    depth = 2.0 * depth_index * depth_index + 6.0 * depth_index + 3.0

    def mine(number):
        return own[number * LEVELS : (number + 1) * LEVELS, :]

    def single(number):
        return own[64 + number : 65 + number, :]

    u_last, g_last, t_first, s_first, face_first = mine(2), mine(3), mine(4), mine(5), mine(7)
    turn = (0.25 * TIME_STEP) * single(4)
    push = -TIME_STEP * GRAVITY / REFERENCE_DENSITY
    inverse_x, inverse_y = 1.0 / single(0), 1.0 / single(1)
    back = -(TIME_STEP * inverse_x * inverse_y) * (0.5 * u_last - g_last)
    anom_t, anom_s = t_east - 10.0, s_east - 35.0
    weight = 0.5 * thick * (
        (-0.1655 * (1.0 + 0.0001497 * depth) + (-0.1655 * 0.5 * 0.05952) * anom_t - 0.0024341 * anom_s) * anom_t
        + (0.76554 * (1.0 - 1.109e-05 * depth) - (0.76554 * 0.5 * 0.00054914) * anom_s) * anom_s
    )
    head = 2.0 * running_sum(weight, level, False) - weight
    v_south_east = jnp.where(lane == 0, roll_lanes(v_east, -lines), roll_lanes(v_east, 1))
    u_add = jnp.where(g_last > 0.0, (push * inverse_x) * head + (turn * inverse_x) * (v_east + v_south_east), 0.0)
    turned[...] = jnp.zeros_like(turned)
    turned[pl.ds(0, LEVELS, 2), :] = back * t_east
    turned[pl.ds(16, LEVELS, 2), :] = back * s_east
    turned[pl.ds(32, LEVELS, 2), :] = u_add
    inverse_x, inverse_y = 1.0 / single(2), 1.0 / single(3)
    scale = -(TIME_STEP * inverse_x * inverse_y)
    here, there = 0.5 * u_west + g_west, 0.5 * u_west - g_west
    upward = running_sum(0.5 * thick * u_west, level, True)

    def first_column(q_west, q):
        flux = upward * (q + jnp.where(level == 0, q, pltpu.roll(q, 1, 0)))
        under = jnp.where(level == LEVELS - 1, 0.0, pltpu.roll(flux, LEVELS - 1, 0))
        return scale * ((flux - under) / thick - (here * q_west + there * q))

    turned[pl.ds(1, LEVELS, 2), :] = first_column(t_west, t_first)
    turned[pl.ds(17, LEVELS, 2), :] = first_column(s_west, s_first)
    turned[pl.ds(33, LEVELS, 2), :] = -(turn * inverse_y) * (u_west + roll_lanes(u_west, -1)) * face_first
    sides[...] = turned[...].T

    at_first, at_last = lane == 0, lane == LANES - 1
    at_side = at_first | at_last
    early, parts, outs = (t_early, s_early, u_early, v_early), (t_part, s_part, u_part, v_part), (t_out, s_out, u_out, v_out)
    chunk = lines // CHUNKS
    copies = []
    for c in range(CHUNKS):

        for r in range(c * chunk // TILE, (c + 1) * chunk // TILE):
            rows = pl.ds(r * TILE, TILE)
            side = sides[rows, :]
            levels = jnp.where(at_side, count[rows, :], 0)
            for k in range(LEVELS):
                wet = levels > k
                both = roll_lanes(side, -(2 * k + 33))
                adds = (
                    jnp.where(wet, roll_lanes(side, -(2 * k + 1)), 0.0),
                    jnp.where(wet, roll_lanes(side, -(2 * k + 17)), 0.0),
                    jnp.where(at_last, both, 0.0),
                    jnp.where(at_first, both, 0.0),
                )
                for part, add, buffer in zip(early if 1 <= r < EARLY else parts, adds, buffers):
                    buffer[k, rows, :] = part[k, rows, :] + add
        rows = pl.ds(c * chunk, chunk)
        for n in range(4):
            copy = pltpu.make_async_copy(buffers[n].at[:, rows, :], outs[n].at[:, rows, :], done.at[c * 4 + n])
            copy.start()
            copies.append(copy)
    for copy in copies:
        copy.wait()


def whole(n):
    return [pl.BlockSpec(memory_space=VMEM)] * n


def per_device(
    potential_warmth_degrees,
    dissolved_salt_content,
    zonal_edge_current,
    meridional_edge_current,
    wet_grid_flag,
    zonal_wet_edge_flag,
    meridional_wet_edge_flag,
    bottom_tier_count,
    zonal_grid_spacing,
    meridional_grid_spacing,
):
    t, s, u, v = potential_warmth_degrees, dissolved_salt_content, zonal_edge_current, meridional_edge_current
    zf, mf, e1, e2 = zonal_wet_edge_flag, meridional_wet_edge_flag, zonal_grid_spacing, meridional_grid_spacing
    lines = t.shape[1]
    lons, lats = lax.axis_size("lon"), lax.axis_size("lat")
    f32 = jnp.float32
    params = pltpu.CompilerParams(vmem_limit_bytes=24 * 1024 * 1024)
    packet = jax.ShapeDtypeStruct((PACKET, LANES), f32)
    field = jax.ShapeDtypeStruct(t.shape, f32)

    lat_to_a, lat_to_b, count = pl.pallas_call(
        row_pack,
        in_specs=[pl.BlockSpec(memory_space=pl.ANY)] * 9,
        out_specs=whole(3),
        out_shape=[packet, packet, jax.ShapeDtypeStruct(e1.shape, jnp.int32)],
        scratch_shapes=[
            VMEM((7, LEVELS, TILE, LANES), f32),
            VMEM((3, LEVELS, TILE, LANES), jnp.int32),
            VMEM((3, TILE, LANES), f32),
            pltpu.SemaphoreType.DMA((14,)),
        ],
        compiler_params=pltpu.CompilerParams(vmem_limit_bytes=4 * 1024 * 1024),
        name="row_pack",
    )(*[pltpu.with_memory_space_constraint(x, pltpu.HBM) for x in (t, s, u, v, zf, mf, e1, e2, bottom_tier_count)])

    pairs_a = [(j, j ^ 1) for j in range(lats)]
    pairs_b = []
    for i in range(lons):
        for j in range(1, lats):
            other = (lons - 1 - i) * lats + j if j == lats - 1 else i * lats + (j + 1 if j % 2 else j - 1)
            pairs_b.append((i * lats + j, other))
    lat_a = lax.ppermute(lat_to_a, "lat", pairs_a)
    lat_b = lax.ppermute(lat_to_b, ("lon", "lat"), pairs_b)

    extended = jax.ShapeDtypeStruct((LEVELS, lines + 2 * TILE, LANES), f32)
    square = VMEM((LANES, LANES), f32)
    to_east, to_west, own, coriolis, *parts = pl.pallas_call(
        front,
        in_specs=whole(9),
        out_specs=whole(15),
        out_shape=[packet, packet, jax.ShapeDtypeStruct((72, LANES), f32), jax.ShapeDtypeStruct(e1.shape, f32)] + [extended] * 7 + [field] * 4,
        scratch_shapes=[square],
        compiler_params=params,
        name="front",
    )(t, s, u, v, zf, mf, count, e1, e2)
    parts, early = parts[:7], parts[7:]

    lon_to_a, lon_to_b = pl.pallas_call(
        corner_pack,
        in_specs=whole(4),
        out_specs=whole(2),
        out_shape=[packet, packet],
        compiler_params=params,
        name="corner_pack",
    )(lat_a, lat_b, to_east, to_west)
    lon_b = lax.ppermute(lon_to_b, "lon", [(i, (i + 1 if i % 2 else i - 1) % lons) for i in range(lons)])
    lon_a = lax.ppermute(lon_to_a, "lon", [(i, i ^ 1) for i in range(lons)])

    parts = pl.pallas_call(
        middle,
        in_specs=whole(19),
        out_specs=whole(4),
        out_shape=[field] * 4,
        scratch_shapes=[VMEM((8, LEVELS, LANES), f32), VMEM((3 * LEVELS, LANES), f32)],
        compiler_params=params,
        name="middle",
    )(t, s, u, v, zf, mf, count, e1, e2, coriolis, *parts, lat_a, lat_b)

    return pl.pallas_call(
        finish,
        in_specs=whole(12),
        out_specs=[pl.BlockSpec(memory_space=pltpu.MemorySpace.HBM)] * 4,
        out_shape=[field] * 4,
        scratch_shapes=[square] * 2 + [VMEM(t.shape, f32)] * 4 + [pltpu.SemaphoreType.DMA((4 * CHUNKS,))],
        compiler_params=params,
        name="finish",
    )(*early, *parts, count, own, lon_b, lon_a)


def solution(mesh):
    deep, flat = P(None, "lat", "lon"), P("lat", "lon")
    return jax.shard_map(
        per_device,
        mesh=mesh,
        in_specs=(deep,) * 7 + (flat,) * 3,
        out_specs=(deep,) * 4,
        check_vma=False,
    )
```

```python
import functools
import math

import jax
import jax.numpy as jnp
from jax import lax
from jax.experimental import pallas as pl
from jax.experimental.pallas import tpu as pltpu
from jax.sharding import PartitionSpec as P

GRAVITY = 9.81
REFERENCE_DENSITY = 1026.0
TIME_STEP = 360.0
LATERAL = 300.0
VERTICAL = 0.001
ROTATION = 7.292e-05

LEVELS = 8
LANES = 128
TILE = 8
PACKET = 4 * LEVELS
CHUNKS = 3
EARLY = 9
VMEM = pltpu.MemorySpace.VMEM

THICK = [6.0 + 4.0 * k for k in range(LEVELS)]
DEPTH = [2.0 * k * k + 6.0 * k + 3.0 for k in range(LEVELS)]
SPACING = [4.0 * k + 4.0 for k in range(LEVELS)]


def lane_index(shape):
    return lax.broadcasted_iota(jnp.int32, shape, len(shape) - 1)


def roll_lanes(x, shift):
    return pltpu.roll(x, shift % LANES, x.ndim - 1)


def density(heat, salt, k):
    anom_t = heat - 10.0
    anom_s = salt - 35.0
    by_t = -0.1655 * (1.0 + 0.0001497 * DEPTH[k])
    by_s = 0.76554 * (1.0 - 1.109e-05 * DEPTH[k])
    along_t = by_t + (-0.1655 * 0.5 * 0.05952) * anom_t - 0.0024341 * anom_s
    along_s = by_s - (0.76554 * 0.5 * 0.00054914) * anom_s
    return along_t * anom_t + along_s * anom_s


def row_pack(t, s, u, v, zf, mf, e1, e2, bottom, to_a, to_b, count, deep, flags, flat, arrived):
    j = lax.axis_index("lat")
    even = j % 2 == 0
    top = j == lax.axis_size("lat") - 1
    last = TILE - 1
    low, high = pl.ds(0, TILE), pl.ds(t.shape[1] - TILE, TILE)
    wanted = [(t, low), (t, high), (s, low), (s, high), (u, low), (u, high), (v, high)]
    marks = [(zf, low), (zf, high), (mf, high)]
    sizes = [(e1, high), (e2, high), (e2, low)]
    copies = [pltpu.make_async_copy(ref.at[:, rows, :], deep.at[n], arrived.at[n]) for n, (ref, rows) in enumerate(wanted)]
    copies += [pltpu.make_async_copy(ref.at[:, rows, :], flags.at[n], arrived.at[7 + n]) for n, (ref, rows) in enumerate(marks)]
    copies += [pltpu.make_async_copy(ref.at[rows, :], flat.at[n], arrived.at[10 + n]) for n, (ref, rows) in enumerate(sizes)]
    copies.append(pltpu.make_async_copy(bottom, count, arrived.at[13]))
    for copy in copies:
        copy.start()
    for copy in copies:
        copy.wait()

    def put(out, fields):
        for number, field in enumerate(fields):
            out[number * LEVELS : (number + 1) * LEVELS, :] = field

    def upward():
        spacing_x, spacing_y = flat[0, last:, :], flat[1, last:, :]
        face = flags[2, :, last, :].astype(jnp.float32)
        return [
            deep[1, :, last, :],
            deep[3, :, last, :],
            spacing_x * deep[6, :, last, :] * face,
            LATERAL * spacing_x / spacing_y * face,
        ]

    def downward():
        flux = flat[2, :1, :] * deep[4, :, 0, :] * flags[0, :, 0, :].astype(jnp.float32)
        return [deep[0, :, 0, :], deep[2, :, 0, :], flux, jnp.zeros_like(flux)]

    @pl.when(even)
    def _():
        put(to_a, upward())
        put(to_b, downward())

    @pl.when(jnp.logical_not(even))
    def _():
        put(to_a, downward())

    @pl.when(jnp.logical_not(even) & jnp.logical_not(top))
    def _():
        put(to_b, upward())

    @pl.when(top)
    def _():
        flux = flat[1, last:, :] * deep[5, :, last, :] * flags[1, :, last, :].astype(jnp.float32)
        put(to_b, [deep[1, :, last, :], deep[3, :, last, :], -flux, jnp.zeros_like(flux)])


def from_west(x):
    return jnp.where(lane_index(x.shape) == 0, 0.0, roll_lanes(x, 1))


def from_east(x):
    return jnp.where(lane_index(x.shape) == LANES - 1, 0.0, roll_lanes(x, -1))


def tile_update(
    t, s, u, v, zf, mf, count, e1, e2, coriolis, p_ext, a_ext, b_ext, u_ext, v_ext, ft_ext, fs_ext,
    t_out, s_out, u_out, v_out, beyond,
):
    row = lax.broadcasted_iota(jnp.int32, (TILE, LANES), 0)

    def update(r, _, first=False, last=False):
        source = pl.ds(pl.multiple_of(r * TILE, TILE), TILE)
        rows = pl.ds(pl.multiple_of(r * TILE + TILE, TILE), TILE)
        spacing_x, spacing_y = e1[source, :], e2[source, :]
        levels = count[source, :]
        inverse_x, inverse_y = 1.0 / spacing_x, 1.0 / spacing_y
        ratio_x, ratio_y = LATERAL * spacing_y * inverse_x, LATERAL * spacing_x * inverse_y
        area = spacing_x * spacing_y
        per_area = TIME_STEP * inverse_x * inverse_y
        turn = (0.25 * TIME_STEP) * coriolis[source, :]
        turn_x, turn_y = turn * inverse_x, turn * inverse_y
        push = -TIME_STEP * GRAVITY / REFERENCE_DENSITY
        push_x, push_y = push * inverse_x, push * inverse_y
        zero = jnp.zeros((TILE, LANES), jnp.float32)

        def above(ref, k, number, offset=TILE):
            if last:
                return jnp.where(row == TILE - 1, beyond[number, k : k + 1, :], pltpu.roll(ref[k, pl.ds(r * TILE + offset, TILE), :], TILE - 1, 0))
            return ref[k, pl.ds(r * TILE + offset + 1, TILE), :]

        def below(ref, k, number):
            if first:
                return jnp.where(row == 0, beyond[number, k : k + 1, :], pltpu.roll(ref[k, rows, :], 1, 0))
            return ref[k, pl.ds(r * TILE + TILE - 1, TILE), :]

        upward, t_below, s_below, u_below, v_below = zero, zero, zero, zero, zero
        for k in reversed(range(LEVELS)):
            heat, salt = t[k, source, :], s[k, source, :]
            flux_x, flux_y = u_ext[k, rows, :], v_ext[k, rows, :]
            face_x, face_y = zf[k, source, :].astype(jnp.float32), mf[k, source, :].astype(jnp.float32)
            both_x, both_y = a_ext[k, rows, :], b_ext[k, rows, :]
            wet = levels > k
            spread = ratio_x * face_x
            here, there = 0.5 * flux_x + spread, 0.5 * flux_x - spread
            t_east = here * heat + there * from_east(heat)
            s_east = here * salt + there * from_east(salt)
            if last:
                here, there = 0.5 * flux_y + ratio_y * face_y, 0.5 * flux_y - ratio_y * face_y
                t_north, s_north = here * heat + there * above(t, k, 0, 0), here * salt + there * above(s, k, 1, 0)
                under = pl.ds(r * TILE + TILE - 1, 1)
                t_south = jnp.where(row == 0, ft_ext[k, under, :], pltpu.roll(t_north, 1, 0))
                s_south = jnp.where(row == 0, fs_ext[k, under, :], pltpu.roll(s_north, 1, 0))
            else:
                t_north, s_north = ft_ext[k, rows, :], fs_ext[k, rows, :]
                t_south, s_south = below(ft_ext, k, 6), below(fs_ext, k, 7)
            t_net = t_east - from_west(t_east) + t_north - t_south
            s_net = s_east - from_west(s_east) + s_north - s_south
            converge = 2.0 * flux_x - both_x + flux_y - below(v_ext, k, 5)
            upward = upward - THICK[k] * converge
            if k > 0:
                mix = jnp.where(wet, (VERTICAL / SPACING[k]) * area, 0.0)
                upper, lower = 0.5 * upward - mix, 0.5 * upward + mix
                t_above = upper * t[k - 1, source, :] + lower * heat
                s_above = upper * s[k - 1, source, :] + lower * salt
            else:
                t_above, s_above = upward * heat, upward * salt
            t_net = t_net + (t_above - t_below) * (1.0 / THICK[k])
            s_net = s_net + (s_above - s_below) * (1.0 / THICK[k])
            t_below, s_below = t_above, s_above
            t_out[k, source, :] = jnp.where(wet, heat - per_area * t_net, 0.0)
            s_out[k, source, :] = jnp.where(wet, salt - per_area * s_net, 0.0)
            zonal, meridional = u[k, source, :], v[k, source, :]
            if k > 0:
                u_above = (VERTICAL / SPACING[k]) * (u[k - 1, source, :] - zonal) * face_x
                v_above = (VERTICAL / SPACING[k]) * (v[k - 1, source, :] - meridional) * face_y
            else:
                u_above, v_above = zero, zero
            head = p_ext[k, rows, :]
            slope_x = from_east(head) - head
            slope_y = above(p_ext, k, 3) - head
            share = TIME_STEP / THICK[k]
            u_out[k, source, :] = (
                zonal + push_x * slope_x + turn_x * (both_y + below(b_ext, k, 4)) + share * (u_above - u_below)
            ) * face_x
            v_out[k, source, :] = (
                meridional + push_y * slope_y - turn_y * (both_x + above(a_ext, k, 2)) + share * (v_above - v_below)
            ) * face_y
            u_below, v_below = u_above, v_above
        return 0

    return update


def front(
    t, s, u, v, zf, mf, count, e1, e2,
    to_east, to_west, own, coriolis, p_ext, a_ext, b_ext, u_ext, v_ext, ft_ext, fs_ext,
    t_out, s_out, u_out, v_out, packed,
):
    lines = t.shape[1]
    tiles = lines // TILE
    lane = lane_index((TILE, LANES))
    first_row = lax.axis_index("lat") * lines
    total_rows = lines * lax.axis_size("lat")
    packed[pl.ds(lines, LANES - lines), :] = jnp.zeros((LANES - lines, LANES), jnp.float32)

    def pack(r, _):
        rows = pl.ds(pl.multiple_of(r * TILE, TILE), TILE)
        spacing_x, spacing_y = e1[rows, :], e2[rows, :]
        ratio = LATERAL * spacing_y / spacing_x
        row = (first_row + r * TILE + lax.broadcasted_iota(jnp.int32, (TILE, LANES), 0)).astype(jnp.float32)
        latitude = 10.0 + 78.0 * (row + 0.5) / total_rows
        turn = 2.0 * ROTATION * jnp.sin(latitude * (math.pi / 180.0))
        coriolis[rows, :] = turn
        fields = [jnp.zeros((TILE, LANES), jnp.float32) for _ in range(8)]

        def keep(number, k, x, source):
            target = number * LEVELS + k
            fields[number] = jnp.where(lane == target, roll_lanes(x, target - source), fields[number])

        for k in range(LEVELS):
            heat, salt = t[k, rows, :], s[k, rows, :]
            face_x, face_y = zf[k, rows, :].astype(jnp.float32), mf[k, rows, :].astype(jnp.float32)
            keep(0, k, heat, LANES - 1)
            keep(1, k, salt, LANES - 1)
            keep(2, k, spacing_y * u[k, rows, :] * face_x, LANES - 1)
            keep(3, k, ratio * face_x, LANES - 1)
            keep(4, k, heat, 0)
            keep(5, k, salt, 0)
            keep(6, k, spacing_x * v[k, rows, :] * face_y, 0)
            keep(7, k, face_y, 0)
        total = jnp.where(lane == 68, turn, 0.0)
        for n, (x, source) in enumerate([(spacing_x, LANES - 1), (spacing_y, LANES - 1), (spacing_x, 0), (spacing_y, 0)]):
            total = jnp.where(lane == 64 + n, roll_lanes(x, 64 + n - source), total)
        for field in fields:
            total = total + field
        packed[rows, :] = total
        return 0

    lax.fori_loop(0, tiles, pack, 0, unroll=4)
    turned = packed[...].T
    to_east[...] = turned[:PACKET]
    to_west[...] = turned[PACKET : 2 * PACKET]
    own[...] = turned[: own.shape[0]]

    def heads(r, _):
        source = pl.ds(pl.multiple_of(r * TILE, TILE), TILE)
        rows = pl.ds(pl.multiple_of(r * TILE + TILE, TILE), TILE)
        head = jnp.zeros((TILE, LANES), jnp.float32)
        for k in range(LEVELS):
            half = (0.5 * THICK[k]) * density(t[k, source, :], s[k, source, :], k)
            p_ext[k, rows, :] = head + half
            head = head + 2.0 * half
        return 0

    lax.fori_loop(0, tiles, heads, 0, unroll=2)

    def faces(r, _, last=False):
        source = pl.ds(pl.multiple_of(r * TILE, TILE), TILE)
        rows = pl.ds(pl.multiple_of(r * TILE + TILE, TILE), TILE)
        above = pl.ds(r * TILE + 1, TILE)
        spacing_x, spacing_y = e1[source, :], e2[source, :]
        ratio = LATERAL * spacing_x / spacing_y
        for k in range(LEVELS):
            flux_x = spacing_y * u[k, source, :] * zf[k, source, :].astype(jnp.float32)
            u_ext[k, rows, :] = flux_x
            a_ext[k, rows, :] = flux_x + from_west(flux_x)
            face = mf[k, source, :].astype(jnp.float32)
            flux_y = spacing_x * v[k, source, :] * face
            v_ext[k, rows, :] = flux_y
            b_ext[k, rows, :] = flux_y + from_east(flux_y)
            if not last:
                here, there = 0.5 * flux_y + ratio * face, 0.5 * flux_y - ratio * face
                ft_ext[k, rows, :] = here * t[k, source, :] + there * t[k, above, :]
                fs_ext[k, rows, :] = here * s[k, source, :] + there * s[k, above, :]
        return 0

    lax.fori_loop(0, tiles - 1, faces, 0, unroll=3)
    faces(tiles - 1, 0, last=True)
    update = tile_update(
        t, s, u, v, zf, mf, count, e1, e2, coriolis, p_ext, a_ext, b_ext, u_ext, v_ext, ft_ext, fs_ext,
        t_out, s_out, u_out, v_out, None,
    )
    lax.fori_loop(1, EARLY, update, 0, unroll=2)


def corner_pack(from_a, from_b, to_east, to_west, to_a, to_b):
    even_j = lax.axis_index("lat") % 2 == 0
    even_i = lax.axis_index("lon") % 2 == 0
    shape = (PACKET, LANES)
    row = lax.broadcasted_iota(jnp.int32, shape, 0)
    corner = (lane_index(shape) == 96) & (row >= 2 * LEVELS) & (row < 3 * LEVELS)
    first, second = from_a[...], from_b[...]
    north = jnp.where(even_j, first, second)
    south = jnp.where(even_j, second, first)
    top = lax.axis_index("lat") == lax.axis_size("lat") - 1
    last_north = jnp.where(top, roll_lanes(north, 96), roll_lanes(north, 96 - (LANES - 1)))
    east = jnp.where(corner, last_north, to_east[...])
    west = jnp.where(corner, roll_lanes(south, 96), to_west[...])
    to_a[...] = jnp.where(even_i, east, west)
    to_b[...] = jnp.where(even_i, west, east)


def middle(
    t, s, u, v, zf, mf, count, e1, e2, coriolis, p_ext, a_ext, b_ext, u_ext, v_ext, ft_ext, fs_ext, lat_a, lat_b,
    t_out, s_out, u_out, v_out, beyond,
):
    lines = t.shape[1]
    tiles = lines // TILE
    even_j = lax.axis_index("lat") % 2 == 0

    def pick(ref_true, ref_false, flag, number):
        rows = slice(number * LEVELS, (number + 1) * LEVELS)
        return jnp.where(flag, ref_true[rows, :], ref_false[rows, :])

    lane = lane_index((LEVELS, LANES))
    source = jnp.where(lax.axis_index("lat") == lax.axis_size("lat") - 1, LANES - 1 - lane, lane)
    north = [jnp.take_along_axis(pick(lat_a, lat_b, even_j, n), source, axis=1) for n in range(3)]
    south = [pick(lat_b, lat_a, even_j, n) for n in range(4)]
    here, there = 0.5 * south[2] + south[3], 0.5 * south[2] - south[3]
    beyond[0] = north[0]
    beyond[1] = north[1]
    beyond[2] = north[2] + from_west(north[2])
    beyond[4] = south[2] + from_east(south[2])
    beyond[5] = south[2]
    beyond[6] = here * south[0] + there * t[:, 0, :]
    beyond[7] = here * south[1] + there * s[:, 0, :]
    head = jnp.zeros((1, LANES), jnp.float32)
    for k in range(LEVELS):
        half = (0.5 * THICK[k]) * density(beyond[0, k : k + 1, :], beyond[1, k : k + 1, :], k)
        beyond[3, k : k + 1, :] = head + half
        head = head + 2.0 * half

    update = tile_update(
        t, s, u, v, zf, mf, count, e1, e2, coriolis, p_ext, a_ext, b_ext, u_ext, v_ext, ft_ext, fs_ext,
        t_out, s_out, u_out, v_out, beyond,
    )
    update(0, 0, first=True)
    lax.fori_loop(EARLY, tiles - 1, update, 0, unroll=2)
    update(tiles - 1, 0, last=True)


def running_sum(x, level, upward):
    for step in (1, 2, 4):
        if upward:
            x = x + jnp.where(level < LEVELS - step, pltpu.roll(x, LEVELS - step, 0), 0.0)
        else:
            x = x + jnp.where(level >= step, pltpu.roll(x, step, 0), 0.0)
    return x


def finish(t_early, s_early, u_early, v_early, t_part, s_part, u_part, v_part, count, own, lon_b, lon_a, t_out, s_out, u_out, v_out, turned, sides, *buffers_and_done):
    buffers, done = buffers_and_done[:4], buffers_and_done[4]
    lines = t_part.shape[1]
    even_i = lax.axis_index("lon") % 2 == 0

    def pick(ref_true, ref_false, flag, number):
        rows = slice(number * LEVELS, (number + 1) * LEVELS)
        return jnp.where(flag, ref_true[rows, :], ref_false[rows, :])

    t_east, s_east, v_east = [pick(lon_a, lon_b, even_i, n) for n in range(3)]
    t_west, s_west, u_west, g_west = [pick(lon_b, lon_a, even_i, n) for n in range(4)]
    shape = (LEVELS, LANES)
    level, lane = lax.broadcasted_iota(jnp.int32, shape, 0), lane_index(shape)
    depth_index = level.astype(jnp.float32)
    thick = 6.0 + 4.0 * depth_index
    depth = 2.0 * depth_index * depth_index + 6.0 * depth_index + 3.0

    def mine(number):
        return own[number * LEVELS : (number + 1) * LEVELS, :]

    def single(number):
        return own[64 + number : 65 + number, :]

    u_last, g_last, t_first, s_first, face_first = mine(2), mine(3), mine(4), mine(5), mine(7)
    turn = (0.25 * TIME_STEP) * single(4)
    push = -TIME_STEP * GRAVITY / REFERENCE_DENSITY
    inverse_x, inverse_y = 1.0 / single(0), 1.0 / single(1)
    back = -(TIME_STEP * inverse_x * inverse_y) * (0.5 * u_last - g_last)
    anom_t, anom_s = t_east - 10.0, s_east - 35.0
    weight = 0.5 * thick * (
        (-0.1655 * (1.0 + 0.0001497 * depth) + (-0.1655 * 0.5 * 0.05952) * anom_t - 0.0024341 * anom_s) * anom_t
        + (0.76554 * (1.0 - 1.109e-05 * depth) - (0.76554 * 0.5 * 0.00054914) * anom_s) * anom_s
    )
    head = 2.0 * running_sum(weight, level, False) - weight
    v_south_east = jnp.where(lane == 0, roll_lanes(v_east, -lines), roll_lanes(v_east, 1))
    u_add = jnp.where(g_last > 0.0, (push * inverse_x) * head + (turn * inverse_x) * (v_east + v_south_east), 0.0)
    turned[...] = jnp.zeros_like(turned)
    turned[pl.ds(0, LEVELS, 2), :] = back * t_east
    turned[pl.ds(16, LEVELS, 2), :] = back * s_east
    turned[pl.ds(32, LEVELS, 2), :] = u_add
    inverse_x, inverse_y = 1.0 / single(2), 1.0 / single(3)
    scale = -(TIME_STEP * inverse_x * inverse_y)
    here, there = 0.5 * u_west + g_west, 0.5 * u_west - g_west
    upward = running_sum(0.5 * thick * u_west, level, True)

    def first_column(q_west, q):
        flux = upward * (q + jnp.where(level == 0, q, pltpu.roll(q, 1, 0)))
        under = jnp.where(level == LEVELS - 1, 0.0, pltpu.roll(flux, LEVELS - 1, 0))
        return scale * ((flux - under) / thick - (here * q_west + there * q))

    turned[pl.ds(1, LEVELS, 2), :] = first_column(t_west, t_first)
    turned[pl.ds(17, LEVELS, 2), :] = first_column(s_west, s_first)
    turned[pl.ds(33, LEVELS, 2), :] = -(turn * inverse_y) * (u_west + roll_lanes(u_west, -1)) * face_first
    sides[...] = turned[...].T

    at_first, at_last = lane == 0, lane == LANES - 1
    at_side = at_first | at_last
    early, parts, outs = (t_early, s_early, u_early, v_early), (t_part, s_part, u_part, v_part), (t_out, s_out, u_out, v_out)
    chunk = lines // CHUNKS
    copies = []
    for c in range(CHUNKS):

        for r in range(c * chunk // TILE, (c + 1) * chunk // TILE):
            rows = pl.ds(r * TILE, TILE)
            side = sides[rows, :]
            levels = jnp.where(at_side, count[rows, :], 0)
            for k in range(LEVELS):
                wet = levels > k
                both = roll_lanes(side, -(2 * k + 33))
                adds = (
                    jnp.where(wet, roll_lanes(side, -(2 * k + 1)), 0.0),
                    jnp.where(wet, roll_lanes(side, -(2 * k + 17)), 0.0),
                    jnp.where(at_last, both, 0.0),
                    jnp.where(at_first, both, 0.0),
                )
                for part, add, buffer in zip(early if 1 <= r < EARLY else parts, adds, buffers):
                    buffer[k, rows, :] = part[k, rows, :] + add
        rows = pl.ds(c * chunk, chunk)
        for n in range(4):
            copy = pltpu.make_async_copy(buffers[n].at[:, rows, :], outs[n].at[:, rows, :], done.at[c * 4 + n])
            copy.start()
            copies.append(copy)
    for copy in copies:
        copy.wait()


def whole(n):
    return [pl.BlockSpec(memory_space=VMEM)] * n


def per_device(
    potential_warmth_degrees,
    dissolved_salt_content,
    zonal_edge_current,
    meridional_edge_current,
    wet_grid_flag,
    zonal_wet_edge_flag,
    meridional_wet_edge_flag,
    bottom_tier_count,
    zonal_grid_spacing,
    meridional_grid_spacing,
):
    t, s, u, v = potential_warmth_degrees, dissolved_salt_content, zonal_edge_current, meridional_edge_current
    zf, mf, e1, e2 = zonal_wet_edge_flag, meridional_wet_edge_flag, zonal_grid_spacing, meridional_grid_spacing
    lines = t.shape[1]
    lons, lats = lax.axis_size("lon"), lax.axis_size("lat")
    f32 = jnp.float32
    params = pltpu.CompilerParams(vmem_limit_bytes=24 * 1024 * 1024)
    packet = jax.ShapeDtypeStruct((PACKET, LANES), f32)
    field = jax.ShapeDtypeStruct(t.shape, f32)

    lat_to_a, lat_to_b, count = pl.pallas_call(
        row_pack,
        in_specs=[pl.BlockSpec(memory_space=pl.ANY)] * 9,
        out_specs=whole(3),
        out_shape=[packet, packet, jax.ShapeDtypeStruct(e1.shape, jnp.int32)],
        scratch_shapes=[
            VMEM((7, LEVELS, TILE, LANES), f32),
            VMEM((3, LEVELS, TILE, LANES), jnp.int32),
            VMEM((3, TILE, LANES), f32),
            pltpu.SemaphoreType.DMA((14,)),
        ],
        compiler_params=pltpu.CompilerParams(vmem_limit_bytes=4 * 1024 * 1024),
        name="row_pack",
    )(*[pltpu.with_memory_space_constraint(x, pltpu.HBM) for x in (t, s, u, v, zf, mf, e1, e2, bottom_tier_count)])

    pairs_a = [(j, j ^ 1) for j in range(lats)]
    pairs_b = []
    for i in range(lons):
        for j in range(1, lats):
            other = (lons - 1 - i) * lats + j if j == lats - 1 else i * lats + (j + 1 if j % 2 else j - 1)
            pairs_b.append((i * lats + j, other))
    lat_a = lax.ppermute(lat_to_a, "lat", pairs_a)
    lat_b = lax.ppermute(lat_to_b, ("lon", "lat"), pairs_b)

    extended = jax.ShapeDtypeStruct((LEVELS, lines + 2 * TILE, LANES), f32)
    square = VMEM((LANES, LANES), f32)
    to_east, to_west, own, coriolis, *parts = pl.pallas_call(
        front,
        in_specs=whole(9),
        out_specs=whole(15),
        out_shape=[packet, packet, jax.ShapeDtypeStruct((72, LANES), f32), jax.ShapeDtypeStruct(e1.shape, f32)] + [extended] * 7 + [field] * 4,
        scratch_shapes=[square],
        compiler_params=params,
        name="front",
    )(t, s, u, v, zf, mf, count, e1, e2)
    parts, early = parts[:7], parts[7:]

    lon_to_a, lon_to_b = pl.pallas_call(
        corner_pack,
        in_specs=whole(4),
        out_specs=whole(2),
        out_shape=[packet, packet],
        compiler_params=params,
        name="corner_pack",
    )(lat_a, lat_b, to_east, to_west)
    lon_b = lax.ppermute(lon_to_b, "lon", [(i, (i + 1 if i % 2 else i - 1) % lons) for i in range(lons)])
    lon_a = lax.ppermute(lon_to_a, "lon", [(i, i ^ 1) for i in range(lons)])

    parts = pl.pallas_call(
        middle,
        in_specs=whole(19),
        out_specs=whole(4),
        out_shape=[field] * 4,
        scratch_shapes=[VMEM((8, LEVELS, LANES), f32)],
        compiler_params=params,
        name="middle",
    )(t, s, u, v, zf, mf, count, e1, e2, coriolis, *parts, lat_a, lat_b)

    return pl.pallas_call(
        finish,
        in_specs=whole(12),
        out_specs=[pl.BlockSpec(memory_space=pltpu.MemorySpace.HBM)] * 4,
        out_shape=[field] * 4,
        scratch_shapes=[square] * 2 + [VMEM(t.shape, f32)] * 4 + [pltpu.SemaphoreType.DMA((4 * CHUNKS,))],
        compiler_params=params,
        name="finish",
    )(*early, *parts, count, own, lon_b, lon_a)


def solution(mesh):
    deep, flat = P(None, "lat", "lon"), P("lat", "lon")
    return jax.shard_map(
        per_device,
        mesh=mesh,
        in_specs=(deep,) * 7 + (flat,) * 3,
        out_specs=(deep,) * 4,
        check_vma=False,
    )
```

```python
import functools
import math

import jax
import jax.numpy as jnp
from jax import lax
from jax.experimental import pallas as pl
from jax.experimental.pallas import tpu as pltpu
from jax.sharding import PartitionSpec as P

GRAVITY = 9.81
REFERENCE_DENSITY = 1026.0
TIME_STEP = 360.0
LATERAL = 300.0
VERTICAL = 0.001
ROTATION = 7.292e-05

LEVELS = 8
LANES = 128
TILE = 8
PACKET = 4 * LEVELS
CHUNKS = 3
EARLY = 7
VMEM = pltpu.MemorySpace.VMEM

THICK = [6.0 + 4.0 * k for k in range(LEVELS)]
DEPTH = [2.0 * k * k + 6.0 * k + 3.0 for k in range(LEVELS)]
SPACING = [4.0 * k + 4.0 for k in range(LEVELS)]


def lane_index(shape):
    return lax.broadcasted_iota(jnp.int32, shape, len(shape) - 1)


def roll_lanes(x, shift):
    return pltpu.roll(x, shift % LANES, x.ndim - 1)


def density(heat, salt, k):
    anom_t = heat - 10.0
    anom_s = salt - 35.0
    by_t = -0.1655 * (1.0 + 0.0001497 * DEPTH[k])
    by_s = 0.76554 * (1.0 - 1.109e-05 * DEPTH[k])
    along_t = by_t + (-0.1655 * 0.5 * 0.05952) * anom_t - 0.0024341 * anom_s
    along_s = by_s - (0.76554 * 0.5 * 0.00054914) * anom_s
    return along_t * anom_t + along_s * anom_s


def row_pack(t, s, u, v, zf, mf, e1, e2, bottom, to_a, to_b, count, deep, flags, flat, arrived):
    j = lax.axis_index("lat")
    even = j % 2 == 0
    top = j == lax.axis_size("lat") - 1
    last = TILE - 1
    low, high = pl.ds(0, TILE), pl.ds(t.shape[1] - TILE, TILE)
    wanted = [(t, low), (t, high), (s, low), (s, high), (u, low), (u, high), (v, high)]
    marks = [(zf, low), (zf, high), (mf, high)]
    sizes = [(e1, high), (e2, high), (e2, low)]
    copies = [pltpu.make_async_copy(ref.at[:, rows, :], deep.at[n], arrived.at[n]) for n, (ref, rows) in enumerate(wanted)]
    copies += [pltpu.make_async_copy(ref.at[:, rows, :], flags.at[n], arrived.at[7 + n]) for n, (ref, rows) in enumerate(marks)]
    copies += [pltpu.make_async_copy(ref.at[rows, :], flat.at[n], arrived.at[10 + n]) for n, (ref, rows) in enumerate(sizes)]
    copies.append(pltpu.make_async_copy(bottom, count, arrived.at[13]))
    for copy in copies:
        copy.start()
    for copy in copies:
        copy.wait()

    def put(out, fields):
        for number, field in enumerate(fields):
            out[number * LEVELS : (number + 1) * LEVELS, :] = field

    def upward():
        spacing_x, spacing_y = flat[0, last:, :], flat[1, last:, :]
        face = flags[2, :, last, :].astype(jnp.float32)
        return [
            deep[1, :, last, :],
            deep[3, :, last, :],
            spacing_x * deep[6, :, last, :] * face,
            LATERAL * spacing_x / spacing_y * face,
        ]

    def downward():
        flux = flat[2, :1, :] * deep[4, :, 0, :] * flags[0, :, 0, :].astype(jnp.float32)
        return [deep[0, :, 0, :], deep[2, :, 0, :], flux, jnp.zeros_like(flux)]

    @pl.when(even)
    def _():
        put(to_a, upward())
        put(to_b, downward())

    @pl.when(jnp.logical_not(even))
    def _():
        put(to_a, downward())

    @pl.when(jnp.logical_not(even) & jnp.logical_not(top))
    def _():
        put(to_b, upward())

    @pl.when(top)
    def _():
        flux = flat[1, last:, :] * deep[5, :, last, :] * flags[1, :, last, :].astype(jnp.float32)
        put(to_b, [deep[1, :, last, :], deep[3, :, last, :], -flux, jnp.zeros_like(flux)])


def from_west(x):
    return jnp.where(lane_index(x.shape) == 0, 0.0, roll_lanes(x, 1))


def from_east(x):
    return jnp.where(lane_index(x.shape) == LANES - 1, 0.0, roll_lanes(x, -1))


def tile_update(
    t, s, u, v, zf, mf, count, e1, e2, coriolis, p_ext, a_ext, b_ext, u_ext, v_ext, ft_ext, fs_ext,
    t_out, s_out, u_out, v_out, beyond,
):
    row = lax.broadcasted_iota(jnp.int32, (TILE, LANES), 0)

    def update(r, _, first=False, last=False):
        source = pl.ds(pl.multiple_of(r * TILE, TILE), TILE)
        rows = pl.ds(pl.multiple_of(r * TILE + TILE, TILE), TILE)
        spacing_x, spacing_y = e1[source, :], e2[source, :]
        levels = count[source, :]
        inverse_x, inverse_y = 1.0 / spacing_x, 1.0 / spacing_y
        ratio_x, ratio_y = LATERAL * spacing_y * inverse_x, LATERAL * spacing_x * inverse_y
        area = spacing_x * spacing_y
        per_area = TIME_STEP * inverse_x * inverse_y
        turn = (0.25 * TIME_STEP) * coriolis[source, :]
        turn_x, turn_y = turn * inverse_x, turn * inverse_y
        push = -TIME_STEP * GRAVITY / REFERENCE_DENSITY
        push_x, push_y = push * inverse_x, push * inverse_y
        zero = jnp.zeros((TILE, LANES), jnp.float32)

        def above(ref, k, number, offset=TILE):
            if last:
                return jnp.where(row == TILE - 1, beyond[number, k : k + 1, :], pltpu.roll(ref[k, pl.ds(r * TILE + offset, TILE), :], TILE - 1, 0))
            return ref[k, pl.ds(r * TILE + offset + 1, TILE), :]

        def below(ref, k, number):
            if first:
                return jnp.where(row == 0, beyond[number, k : k + 1, :], pltpu.roll(ref[k, rows, :], 1, 0))
            return ref[k, pl.ds(r * TILE + TILE - 1, TILE), :]

        upward, t_below, s_below, u_below, v_below = zero, zero, zero, zero, zero
        for k in reversed(range(LEVELS)):
            heat, salt = t[k, source, :], s[k, source, :]
            flux_x, flux_y = u_ext[k, rows, :], v_ext[k, rows, :]
            face_x, face_y = zf[k, source, :].astype(jnp.float32), mf[k, source, :].astype(jnp.float32)
            both_x, both_y = a_ext[k, rows, :], b_ext[k, rows, :]
            wet = levels > k
            spread = ratio_x * face_x
            here, there = 0.5 * flux_x + spread, 0.5 * flux_x - spread
            t_east = here * heat + there * from_east(heat)
            s_east = here * salt + there * from_east(salt)
            if last:
                here, there = 0.5 * flux_y + ratio_y * face_y, 0.5 * flux_y - ratio_y * face_y
                t_north, s_north = here * heat + there * above(t, k, 0, 0), here * salt + there * above(s, k, 1, 0)
                under = pl.ds(r * TILE + TILE - 1, 1)
                t_south = jnp.where(row == 0, ft_ext[k, under, :], pltpu.roll(t_north, 1, 0))
                s_south = jnp.where(row == 0, fs_ext[k, under, :], pltpu.roll(s_north, 1, 0))
            else:
                t_north, s_north = ft_ext[k, rows, :], fs_ext[k, rows, :]
                t_south, s_south = below(ft_ext, k, 6), below(fs_ext, k, 7)
            t_net = t_east - from_west(t_east) + t_north - t_south
            s_net = s_east - from_west(s_east) + s_north - s_south
            converge = 2.0 * flux_x - both_x + flux_y - below(v_ext, k, 5)
            upward = upward - THICK[k] * converge
            if k > 0:
                mix = jnp.where(wet, (VERTICAL / SPACING[k]) * area, 0.0)
                upper, lower = 0.5 * upward - mix, 0.5 * upward + mix
                t_above = upper * t[k - 1, source, :] + lower * heat
                s_above = upper * s[k - 1, source, :] + lower * salt
            else:
                t_above, s_above = upward * heat, upward * salt
            t_net = t_net + (t_above - t_below) * (1.0 / THICK[k])
            s_net = s_net + (s_above - s_below) * (1.0 / THICK[k])
            t_below, s_below = t_above, s_above
            t_out[k, source, :] = jnp.where(wet, heat - per_area * t_net, 0.0)
            s_out[k, source, :] = jnp.where(wet, salt - per_area * s_net, 0.0)
            zonal, meridional = u[k, source, :], v[k, source, :]
            if k > 0:
                u_above = (VERTICAL / SPACING[k]) * (u[k - 1, source, :] - zonal) * face_x
                v_above = (VERTICAL / SPACING[k]) * (v[k - 1, source, :] - meridional) * face_y
            else:
                u_above, v_above = zero, zero
            head = p_ext[k, rows, :]
            slope_x = from_east(head) - head
            slope_y = above(p_ext, k, 3) - head
            share = TIME_STEP / THICK[k]
            u_out[k, source, :] = (
                zonal + push_x * slope_x + turn_x * (both_y + below(b_ext, k, 4)) + share * (u_above - u_below)
            ) * face_x
            v_out[k, source, :] = (
                meridional + push_y * slope_y - turn_y * (both_x + above(a_ext, k, 2)) + share * (v_above - v_below)
            ) * face_y
            u_below, v_below = u_above, v_above
        return 0

    return update


def front(
    t, s, u, v, zf, mf, count, e1, e2,
    to_east, to_west, own, coriolis, p_ext, a_ext, b_ext, u_ext, v_ext, ft_ext, fs_ext,
    t_out, s_out, u_out, v_out, packed,
):
    lines = t.shape[1]
    tiles = lines // TILE
    lane = lane_index((TILE, LANES))
    first_row = lax.axis_index("lat") * lines
    total_rows = lines * lax.axis_size("lat")
    packed[pl.ds(lines, LANES - lines), :] = jnp.zeros((LANES - lines, LANES), jnp.float32)

    def pack(r, _):
        rows = pl.ds(pl.multiple_of(r * TILE, TILE), TILE)
        spacing_x, spacing_y = e1[rows, :], e2[rows, :]
        ratio = LATERAL * spacing_y / spacing_x
        row = (first_row + r * TILE + lax.broadcasted_iota(jnp.int32, (TILE, LANES), 0)).astype(jnp.float32)
        latitude = 10.0 + 78.0 * (row + 0.5) / total_rows
        turn = 2.0 * ROTATION * jnp.sin(latitude * (math.pi / 180.0))
        coriolis[rows, :] = turn
        fields = [jnp.zeros((TILE, LANES), jnp.float32) for _ in range(8)]

        def keep(number, k, x, source):
            target = number * LEVELS + k
            fields[number] = jnp.where(lane == target, roll_lanes(x, target - source), fields[number])

        for k in range(LEVELS):
            heat, salt = t[k, rows, :], s[k, rows, :]
            face_x, face_y = zf[k, rows, :].astype(jnp.float32), mf[k, rows, :].astype(jnp.float32)
            keep(0, k, heat, LANES - 1)
            keep(1, k, salt, LANES - 1)
            keep(2, k, spacing_y * u[k, rows, :] * face_x, LANES - 1)
            keep(3, k, ratio * face_x, LANES - 1)
            keep(4, k, heat, 0)
            keep(5, k, salt, 0)
            keep(6, k, spacing_x * v[k, rows, :] * face_y, 0)
            keep(7, k, face_y, 0)
        total = jnp.where(lane == 68, turn, 0.0)
        for n, (x, source) in enumerate([(spacing_x, LANES - 1), (spacing_y, LANES - 1), (spacing_x, 0), (spacing_y, 0)]):
            total = jnp.where(lane == 64 + n, roll_lanes(x, 64 + n - source), total)
        for field in fields:
            total = total + field
        packed[rows, :] = total
        return 0

    lax.fori_loop(0, tiles, pack, 0, unroll=4)
    turned = packed[...].T
    to_east[...] = turned[:PACKET]
    to_west[...] = turned[PACKET : 2 * PACKET]
    own[...] = turned[: own.shape[0]]

    def heads(r, _):
        source = pl.ds(pl.multiple_of(r * TILE, TILE), TILE)
        rows = pl.ds(pl.multiple_of(r * TILE + TILE, TILE), TILE)
        head = jnp.zeros((TILE, LANES), jnp.float32)
        for k in range(LEVELS):
            half = (0.5 * THICK[k]) * density(t[k, source, :], s[k, source, :], k)
            p_ext[k, rows, :] = head + half
            head = head + 2.0 * half
        return 0

    lax.fori_loop(0, tiles, heads, 0, unroll=2)

    def faces(r, _, last=False):
        source = pl.ds(pl.multiple_of(r * TILE, TILE), TILE)
        rows = pl.ds(pl.multiple_of(r * TILE + TILE, TILE), TILE)
        above = pl.ds(r * TILE + 1, TILE)
        spacing_x, spacing_y = e1[source, :], e2[source, :]
        ratio = LATERAL * spacing_x / spacing_y
        for k in range(LEVELS):
            flux_x = spacing_y * u[k, source, :] * zf[k, source, :].astype(jnp.float32)
            u_ext[k, rows, :] = flux_x
            a_ext[k, rows, :] = flux_x + from_west(flux_x)
            face = mf[k, source, :].astype(jnp.float32)
            flux_y = spacing_x * v[k, source, :] * face
            v_ext[k, rows, :] = flux_y
            b_ext[k, rows, :] = flux_y + from_east(flux_y)
            if not last:
                here, there = 0.5 * flux_y + ratio * face, 0.5 * flux_y - ratio * face
                ft_ext[k, rows, :] = here * t[k, source, :] + there * t[k, above, :]
                fs_ext[k, rows, :] = here * s[k, source, :] + there * s[k, above, :]
        return 0

    lax.fori_loop(0, tiles - 1, faces, 0, unroll=3)
    faces(tiles - 1, 0, last=True)
    update = tile_update(
        t, s, u, v, zf, mf, count, e1, e2, coriolis, p_ext, a_ext, b_ext, u_ext, v_ext, ft_ext, fs_ext,
        t_out, s_out, u_out, v_out, None,
    )
    lax.fori_loop(1, EARLY, update, 0, unroll=2)


def corner_pack(from_a, from_b, to_east, to_west, to_a, to_b):
    even_j = lax.axis_index("lat") % 2 == 0
    even_i = lax.axis_index("lon") % 2 == 0
    shape = (PACKET, LANES)
    row = lax.broadcasted_iota(jnp.int32, shape, 0)
    corner = (lane_index(shape) == 96) & (row >= 2 * LEVELS) & (row < 3 * LEVELS)
    first, second = from_a[...], from_b[...]
    north = jnp.where(even_j, first, second)
    south = jnp.where(even_j, second, first)
    top = lax.axis_index("lat") == lax.axis_size("lat") - 1
    last_north = jnp.where(top, roll_lanes(north, 96), roll_lanes(north, 96 - (LANES - 1)))
    east = jnp.where(corner, last_north, to_east[...])
    west = jnp.where(corner, roll_lanes(south, 96), to_west[...])
    to_a[...] = jnp.where(even_i, east, west)
    to_b[...] = jnp.where(even_i, west, east)


def middle(
    t, s, u, v, zf, mf, count, e1, e2, coriolis, p_ext, a_ext, b_ext, u_ext, v_ext, ft_ext, fs_ext, lat_a, lat_b,
    t_out, s_out, u_out, v_out, beyond,
):
    lines = t.shape[1]
    tiles = lines // TILE
    even_j = lax.axis_index("lat") % 2 == 0

    def pick(ref_true, ref_false, flag, number):
        rows = slice(number * LEVELS, (number + 1) * LEVELS)
        return jnp.where(flag, ref_true[rows, :], ref_false[rows, :])

    lane = lane_index((LEVELS, LANES))
    source = jnp.where(lax.axis_index("lat") == lax.axis_size("lat") - 1, LANES - 1 - lane, lane)
    north = [jnp.take_along_axis(pick(lat_a, lat_b, even_j, n), source, axis=1) for n in range(3)]
    south = [pick(lat_b, lat_a, even_j, n) for n in range(4)]
    here, there = 0.5 * south[2] + south[3], 0.5 * south[2] - south[3]
    beyond[0] = north[0]
    beyond[1] = north[1]
    beyond[2] = north[2] + from_west(north[2])
    beyond[4] = south[2] + from_east(south[2])
    beyond[5] = south[2]
    beyond[6] = here * south[0] + there * t[:, 0, :]
    beyond[7] = here * south[1] + there * s[:, 0, :]
    head = jnp.zeros((1, LANES), jnp.float32)
    for k in range(LEVELS):
        half = (0.5 * THICK[k]) * density(beyond[0, k : k + 1, :], beyond[1, k : k + 1, :], k)
        beyond[3, k : k + 1, :] = head + half
        head = head + 2.0 * half

    update = tile_update(
        t, s, u, v, zf, mf, count, e1, e2, coriolis, p_ext, a_ext, b_ext, u_ext, v_ext, ft_ext, fs_ext,
        t_out, s_out, u_out, v_out, beyond,
    )
    update(0, 0, first=True)
    lax.fori_loop(EARLY, tiles - 1, update, 0, unroll=2)
    update(tiles - 1, 0, last=True)


def running_sum(x, level, upward):
    for step in (1, 2, 4):
        if upward:
            x = x + jnp.where(level < LEVELS - step, pltpu.roll(x, LEVELS - step, 0), 0.0)
        else:
            x = x + jnp.where(level >= step, pltpu.roll(x, step, 0), 0.0)
    return x


def finish(t_early, s_early, u_early, v_early, t_part, s_part, u_part, v_part, count, own, lon_b, lon_a, t_out, s_out, u_out, v_out, turned, sides, *buffers_and_done):
    buffers, done = buffers_and_done[:4], buffers_and_done[4]
    lines = t_part.shape[1]
    even_i = lax.axis_index("lon") % 2 == 0

    def part(ref, number):
        return ref[number * LEVELS : (number + 1) * LEVELS, :]

    t_east, s_east, v_east = [jnp.where(even_i, part(lon_a, 4 + n), part(lon_b, n)) for n in range(3)]
    t_west, s_west, u_west, g_west = [jnp.where(even_i, part(lon_b, n), part(lon_a, n)) for n in range(4)]
    shape = (LEVELS, LANES)
    level, lane = lax.broadcasted_iota(jnp.int32, shape, 0), lane_index(shape)
    depth_index = level.astype(jnp.float32)
    thick = 6.0 + 4.0 * depth_index
    depth = 2.0 * depth_index * depth_index + 6.0 * depth_index + 3.0

    def mine(number):
        return own[number * LEVELS : (number + 1) * LEVELS, :]

    def single(number):
        return own[64 + number : 65 + number, :]

    u_last, g_last, t_first, s_first, face_first = mine(2), mine(3), mine(4), mine(5), mine(7)
    turn = (0.25 * TIME_STEP) * single(4)
    push = -TIME_STEP * GRAVITY / REFERENCE_DENSITY
    inverse_x, inverse_y = 1.0 / single(0), 1.0 / single(1)
    back = -(TIME_STEP * inverse_x * inverse_y) * (0.5 * u_last - g_last)
    anom_t, anom_s = t_east - 10.0, s_east - 35.0
    weight = 0.5 * thick * (
        (-0.1655 * (1.0 + 0.0001497 * depth) + (-0.1655 * 0.5 * 0.05952) * anom_t - 0.0024341 * anom_s) * anom_t
        + (0.76554 * (1.0 - 1.109e-05 * depth) - (0.76554 * 0.5 * 0.00054914) * anom_s) * anom_s
    )
    head = 2.0 * running_sum(weight, level, False) - weight
    v_south_east = jnp.where(lane == 0, roll_lanes(v_east, -lines), roll_lanes(v_east, 1))
    u_add = jnp.where(g_last > 0.0, (push * inverse_x) * head + (turn * inverse_x) * (v_east + v_south_east), 0.0)
    turned[...] = jnp.zeros_like(turned)
    turned[pl.ds(0, LEVELS, 2), :] = back * t_east
    turned[pl.ds(16, LEVELS, 2), :] = back * s_east
    turned[pl.ds(32, LEVELS, 2), :] = u_add
    inverse_x, inverse_y = 1.0 / single(2), 1.0 / single(3)
    scale = -(TIME_STEP * inverse_x * inverse_y)
    here, there = 0.5 * u_west + g_west, 0.5 * u_west - g_west
    upward = running_sum(0.5 * thick * u_west, level, True)

    def first_column(q_west, q):
        flux = upward * (q + jnp.where(level == 0, q, pltpu.roll(q, 1, 0)))
        under = jnp.where(level == LEVELS - 1, 0.0, pltpu.roll(flux, LEVELS - 1, 0))
        return scale * ((flux - under) / thick - (here * q_west + there * q))

    turned[pl.ds(1, LEVELS, 2), :] = first_column(t_west, t_first)
    turned[pl.ds(17, LEVELS, 2), :] = first_column(s_west, s_first)
    turned[pl.ds(33, LEVELS, 2), :] = -(turn * inverse_y) * (u_west + roll_lanes(u_west, -1)) * face_first
    sides[...] = turned[...].T

    at_first, at_last = lane == 0, lane == LANES - 1
    at_side = at_first | at_last
    early, parts, outs = (t_early, s_early, u_early, v_early), (t_part, s_part, u_part, v_part), (t_out, s_out, u_out, v_out)
    chunk = lines // CHUNKS
    copies = []
    for c in range(CHUNKS):

        for r in range(c * chunk // TILE, (c + 1) * chunk // TILE):
            rows = pl.ds(r * TILE, TILE)
            side = sides[rows, :]
            levels = jnp.where(at_side, count[rows, :], 0)
            for k in range(LEVELS):
                wet = levels > k
                both = roll_lanes(side, -(2 * k + 33))
                adds = (
                    jnp.where(wet, roll_lanes(side, -(2 * k + 1)), 0.0),
                    jnp.where(wet, roll_lanes(side, -(2 * k + 17)), 0.0),
                    jnp.where(at_last, both, 0.0),
                    jnp.where(at_first, both, 0.0),
                )
                for part, add, buffer in zip(early if 1 <= r < EARLY else parts, adds, buffers):
                    buffer[k, rows, :] = part[k, rows, :] + add
        rows = pl.ds(c * chunk, chunk)
        for n in range(4):
            copy = pltpu.make_async_copy(buffers[n].at[:, rows, :], outs[n].at[:, rows, :], done.at[c * 4 + n])
            copy.start()
            copies.append(copy)
    for copy in copies:
        copy.wait()


def whole(n):
    return [pl.BlockSpec(memory_space=VMEM)] * n


def per_device(
    potential_warmth_degrees,
    dissolved_salt_content,
    zonal_edge_current,
    meridional_edge_current,
    wet_grid_flag,
    zonal_wet_edge_flag,
    meridional_wet_edge_flag,
    bottom_tier_count,
    zonal_grid_spacing,
    meridional_grid_spacing,
):
    t, s, u, v = potential_warmth_degrees, dissolved_salt_content, zonal_edge_current, meridional_edge_current
    zf, mf, e1, e2 = zonal_wet_edge_flag, meridional_wet_edge_flag, zonal_grid_spacing, meridional_grid_spacing
    lines = t.shape[1]
    lons, lats = lax.axis_size("lon"), lax.axis_size("lat")
    f32 = jnp.float32
    params = pltpu.CompilerParams(vmem_limit_bytes=24 * 1024 * 1024)
    packet = jax.ShapeDtypeStruct((PACKET, LANES), f32)
    field = jax.ShapeDtypeStruct(t.shape, f32)

    lat_to_a, lat_to_b, count = pl.pallas_call(
        row_pack,
        in_specs=[pl.BlockSpec(memory_space=pl.ANY)] * 9,
        out_specs=whole(3),
        out_shape=[packet, packet, jax.ShapeDtypeStruct(e1.shape, jnp.int32)],
        scratch_shapes=[
            VMEM((7, LEVELS, TILE, LANES), f32),
            VMEM((3, LEVELS, TILE, LANES), jnp.int32),
            VMEM((3, TILE, LANES), f32),
            pltpu.SemaphoreType.DMA((14,)),
        ],
        compiler_params=pltpu.CompilerParams(vmem_limit_bytes=4 * 1024 * 1024),
        name="row_pack",
    )(*[pltpu.with_memory_space_constraint(x, pltpu.HBM) for x in (t, s, u, v, zf, mf, e1, e2, bottom_tier_count)])

    pairs_a = [(j, j ^ 1) for j in range(lats)]
    pairs_b = []
    for i in range(lons):
        for j in range(1, lats):
            other = (lons - 1 - i) * lats + j if j == lats - 1 else i * lats + (j + 1 if j % 2 else j - 1)
            pairs_b.append((i * lats + j, other))
    lat_a = lax.ppermute(lat_to_a, "lat", pairs_a)
    lat_b = lax.ppermute(lat_to_b, ("lon", "lat"), pairs_b)

    extended = jax.ShapeDtypeStruct((LEVELS, lines + 2 * TILE, LANES), f32)
    square = VMEM((LANES, LANES), f32)
    to_east, to_west, own, coriolis, *parts = pl.pallas_call(
        front,
        in_specs=whole(9),
        out_specs=whole(15),
        out_shape=[packet, packet, jax.ShapeDtypeStruct((72, LANES), f32), jax.ShapeDtypeStruct(e1.shape, f32)] + [extended] * 7 + [field] * 4,
        scratch_shapes=[square],
        compiler_params=params,
        name="front",
    )(t, s, u, v, zf, mf, count, e1, e2)
    parts, early = parts[:7], parts[7:]

    lon_to_a, lon_to_b = pl.pallas_call(
        corner_pack,
        in_specs=whole(4),
        out_specs=whole(2),
        out_shape=[packet, packet],
        compiler_params=params,
        name="corner_pack",
    )(lat_a, lat_b, to_east, to_west)
    lon_b = lax.ppermute(lon_to_b, "lon", [(i, (i + 1 if i % 2 else i - 1) % lons) for i in range(lons)])
    lon_a = lax.all_gather(lon_to_a, "lon", axis_index_groups=[[i, i + 1] for i in range(0, lons, 2)], tiled=True)

    parts = pl.pallas_call(
        middle,
        in_specs=whole(19),
        out_specs=whole(4),
        out_shape=[field] * 4,
        scratch_shapes=[VMEM((8, LEVELS, LANES), f32)],
        compiler_params=params,
        name="middle",
    )(t, s, u, v, zf, mf, count, e1, e2, coriolis, *parts, lat_a, lat_b)

    return pl.pallas_call(
        finish,
        in_specs=whole(12),
        out_specs=[pl.BlockSpec(memory_space=pltpu.MemorySpace.HBM)] * 4,
        out_shape=[field] * 4,
        scratch_shapes=[square] * 2 + [VMEM(t.shape, f32)] * 4 + [pltpu.SemaphoreType.DMA((4 * CHUNKS,))],
        compiler_params=params,
        name="finish",
    )(*early, *parts, count, own, lon_b, lon_a)


def solution(mesh):
    deep, flat = P(None, "lat", "lon"), P("lat", "lon")
    return jax.shard_map(
        per_device,
        mesh=mesh,
        in_specs=(deep,) * 7 + (flat,) * 3,
        out_specs=(deep,) * 4,
        check_vma=False,
    )
```

```python
import functools
import math

import jax
import jax.numpy as jnp
from jax import lax
from jax.experimental import pallas as pl
from jax.experimental.pallas import tpu as pltpu
from jax.sharding import PartitionSpec as P

GRAVITY = 9.81
REFERENCE_DENSITY = 1026.0
TIME_STEP = 360.0
LATERAL = 300.0
VERTICAL = 0.001
ROTATION = 7.292e-05

LEVELS = 8
LANES = 128
TILE = 8
PACKET = 4 * LEVELS
CHUNKS = 4
EARLY = 7
VMEM = pltpu.MemorySpace.VMEM

THICK = [6.0 + 4.0 * k for k in range(LEVELS)]
DEPTH = [2.0 * k * k + 6.0 * k + 3.0 for k in range(LEVELS)]
SPACING = [4.0 * k + 4.0 for k in range(LEVELS)]


def lane_index(shape):
    return lax.broadcasted_iota(jnp.int32, shape, len(shape) - 1)


def roll_lanes(x, shift):
    return pltpu.roll(x, shift % LANES, x.ndim - 1)


def density(heat, salt, k):
    anom_t = heat - 10.0
    anom_s = salt - 35.0
    by_t = -0.1655 * (1.0 + 0.0001497 * DEPTH[k])
    by_s = 0.76554 * (1.0 - 1.109e-05 * DEPTH[k])
    along_t = by_t + (-0.1655 * 0.5 * 0.05952) * anom_t - 0.0024341 * anom_s
    along_s = by_s - (0.76554 * 0.5 * 0.00054914) * anom_s
    return along_t * anom_t + along_s * anom_s


def row_pack(t, s, u, v, zf, mf, e1, e2, bottom, to_a, to_b, count, deep, flags, flat, arrived):
    j = lax.axis_index("lat")
    even = j % 2 == 0
    top = j == lax.axis_size("lat") - 1
    last = TILE - 1
    low, high = pl.ds(0, TILE), pl.ds(t.shape[1] - TILE, TILE)
    wanted = [(t, low), (t, high), (s, low), (s, high), (u, low), (u, high), (v, high)]
    marks = [(zf, low), (zf, high), (mf, high)]
    sizes = [(e1, high), (e2, high), (e2, low)]
    copies = [pltpu.make_async_copy(ref.at[:, rows, :], deep.at[n], arrived.at[n]) for n, (ref, rows) in enumerate(wanted)]
    copies += [pltpu.make_async_copy(ref.at[:, rows, :], flags.at[n], arrived.at[7 + n]) for n, (ref, rows) in enumerate(marks)]
    copies += [pltpu.make_async_copy(ref.at[rows, :], flat.at[n], arrived.at[10 + n]) for n, (ref, rows) in enumerate(sizes)]
    copies.append(pltpu.make_async_copy(bottom, count, arrived.at[13]))
    for copy in copies:
        copy.start()
    for copy in copies:
        copy.wait()

    def put(out, fields):
        for number, field in enumerate(fields):
            out[number * LEVELS : (number + 1) * LEVELS, :] = field

    def upward():
        spacing_x, spacing_y = flat[0, last:, :], flat[1, last:, :]
        face = flags[2, :, last, :].astype(jnp.float32)
        return [
            deep[1, :, last, :],
            deep[3, :, last, :],
            spacing_x * deep[6, :, last, :] * face,
            LATERAL * spacing_x / spacing_y * face,
        ]

    def downward():
        flux = flat[2, :1, :] * deep[4, :, 0, :] * flags[0, :, 0, :].astype(jnp.float32)
        return [deep[0, :, 0, :], deep[2, :, 0, :], flux, jnp.zeros_like(flux)]

    @pl.when(even)
    def _():
        put(to_a, upward())
        put(to_b, downward())

    @pl.when(jnp.logical_not(even))
    def _():
        put(to_a, downward())

    @pl.when(jnp.logical_not(even) & jnp.logical_not(top))
    def _():
        put(to_b, upward())

    @pl.when(top)
    def _():
        flux = flat[1, last:, :] * deep[5, :, last, :] * flags[1, :, last, :].astype(jnp.float32)
        put(to_b, [deep[1, :, last, :], deep[3, :, last, :], -flux, jnp.zeros_like(flux)])


def from_west(x):
    return jnp.where(lane_index(x.shape) == 0, 0.0, roll_lanes(x, 1))


def from_east(x):
    return jnp.where(lane_index(x.shape) == LANES - 1, 0.0, roll_lanes(x, -1))


def tile_update(
    t, s, u, v, zf, mf, count, e1, e2, coriolis, p_ext, a_ext, b_ext, u_ext, v_ext, ft_ext, fs_ext,
    t_out, s_out, u_out, v_out, beyond,
):
    row = lax.broadcasted_iota(jnp.int32, (TILE, LANES), 0)

    def update(r, _, first=False, last=False):
        source = pl.ds(pl.multiple_of(r * TILE, TILE), TILE)
        rows = pl.ds(pl.multiple_of(r * TILE + TILE, TILE), TILE)
        spacing_x, spacing_y = e1[source, :], e2[source, :]
        levels = count[source, :]
        inverse_x, inverse_y = 1.0 / spacing_x, 1.0 / spacing_y
        ratio_x, ratio_y = LATERAL * spacing_y * inverse_x, LATERAL * spacing_x * inverse_y
        area = spacing_x * spacing_y
        per_area = TIME_STEP * inverse_x * inverse_y
        turn = (0.25 * TIME_STEP) * coriolis[source, :]
        turn_x, turn_y = turn * inverse_x, turn * inverse_y
        push = -TIME_STEP * GRAVITY / REFERENCE_DENSITY
        push_x, push_y = push * inverse_x, push * inverse_y
        zero = jnp.zeros((TILE, LANES), jnp.float32)

        def above(ref, k, number, offset=TILE):
            if last:
                return jnp.where(row == TILE - 1, beyond[number, k : k + 1, :], pltpu.roll(ref[k, pl.ds(r * TILE + offset, TILE), :], TILE - 1, 0))
            return ref[k, pl.ds(r * TILE + offset + 1, TILE), :]

        def below(ref, k, number):
            if first:
                return jnp.where(row == 0, beyond[number, k : k + 1, :], pltpu.roll(ref[k, rows, :], 1, 0))
            return ref[k, pl.ds(r * TILE + TILE - 1, TILE), :]

        upward, t_below, s_below, u_below, v_below = zero, zero, zero, zero, zero
        for k in reversed(range(LEVELS)):
            heat, salt = t[k, source, :], s[k, source, :]
            flux_x, flux_y = u_ext[k, rows, :], v_ext[k, rows, :]
            face_x, face_y = zf[k, source, :].astype(jnp.float32), mf[k, source, :].astype(jnp.float32)
            both_x, both_y = a_ext[k, rows, :], b_ext[k, rows, :]
            wet = levels > k
            spread = ratio_x * face_x
            here, there = 0.5 * flux_x + spread, 0.5 * flux_x - spread
            t_east = here * heat + there * from_east(heat)
            s_east = here * salt + there * from_east(salt)
            if last:
                here, there = 0.5 * flux_y + ratio_y * face_y, 0.5 * flux_y - ratio_y * face_y
                t_north, s_north = here * heat + there * above(t, k, 0, 0), here * salt + there * above(s, k, 1, 0)
                under = pl.ds(r * TILE + TILE - 1, 1)
                t_south = jnp.where(row == 0, ft_ext[k, under, :], pltpu.roll(t_north, 1, 0))
                s_south = jnp.where(row == 0, fs_ext[k, under, :], pltpu.roll(s_north, 1, 0))
            else:
                t_north, s_north = ft_ext[k, rows, :], fs_ext[k, rows, :]
                t_south, s_south = below(ft_ext, k, 6), below(fs_ext, k, 7)
            t_net = t_east - from_west(t_east) + t_north - t_south
            s_net = s_east - from_west(s_east) + s_north - s_south
            converge = 2.0 * flux_x - both_x + flux_y - below(v_ext, k, 5)
            upward = upward - THICK[k] * converge
            if k > 0:
                mix = jnp.where(wet, (VERTICAL / SPACING[k]) * area, 0.0)
                upper, lower = 0.5 * upward - mix, 0.5 * upward + mix
                t_above = upper * t[k - 1, source, :] + lower * heat
                s_above = upper * s[k - 1, source, :] + lower * salt
            else:
                t_above, s_above = upward * heat, upward * salt
            t_net = t_net + (t_above - t_below) * (1.0 / THICK[k])
            s_net = s_net + (s_above - s_below) * (1.0 / THICK[k])
            t_below, s_below = t_above, s_above
            t_out[k, source, :] = jnp.where(wet, heat - per_area * t_net, 0.0)
            s_out[k, source, :] = jnp.where(wet, salt - per_area * s_net, 0.0)
            zonal, meridional = u[k, source, :], v[k, source, :]
            if k > 0:
                u_above = (VERTICAL / SPACING[k]) * (u[k - 1, source, :] - zonal) * face_x
                v_above = (VERTICAL / SPACING[k]) * (v[k - 1, source, :] - meridional) * face_y
            else:
                u_above, v_above = zero, zero
            head = p_ext[k, rows, :]
            slope_x = from_east(head) - head
            slope_y = above(p_ext, k, 3) - head
            share = TIME_STEP / THICK[k]
            u_out[k, source, :] = (
                zonal + push_x * slope_x + turn_x * (both_y + below(b_ext, k, 4)) + share * (u_above - u_below)
            ) * face_x
            v_out[k, source, :] = (
                meridional + push_y * slope_y - turn_y * (both_x + above(a_ext, k, 2)) + share * (v_above - v_below)
            ) * face_y
            u_below, v_below = u_above, v_above
        return 0

    return update


def front(
    t, s, u, v, zf, mf, count, e1, e2,
    to_east, to_west, own, coriolis, p_ext, a_ext, b_ext, u_ext, v_ext, ft_ext, fs_ext,
    t_out, s_out, u_out, v_out, packed,
):
    lines = t.shape[1]
    tiles = lines // TILE
    lane = lane_index((TILE, LANES))
    first_row = lax.axis_index("lat") * lines
    total_rows = lines * lax.axis_size("lat")
    packed[pl.ds(lines, LANES - lines), :] = jnp.zeros((LANES - lines, LANES), jnp.float32)

    def pack(r, _):
        rows = pl.ds(pl.multiple_of(r * TILE, TILE), TILE)
        spacing_x, spacing_y = e1[rows, :], e2[rows, :]
        ratio = LATERAL * spacing_y / spacing_x
        row = (first_row + r * TILE + lax.broadcasted_iota(jnp.int32, (TILE, LANES), 0)).astype(jnp.float32)
        latitude = 10.0 + 78.0 * (row + 0.5) / total_rows
        turn = 2.0 * ROTATION * jnp.sin(latitude * (math.pi / 180.0))
        coriolis[rows, :] = turn
        fields = [jnp.zeros((TILE, LANES), jnp.float32) for _ in range(8)]

        def keep(number, k, x, source):
            target = number * LEVELS + k
            fields[number] = jnp.where(lane == target, roll_lanes(x, target - source), fields[number])

        for k in range(LEVELS):
            heat, salt = t[k, rows, :], s[k, rows, :]
            face_x, face_y = zf[k, rows, :].astype(jnp.float32), mf[k, rows, :].astype(jnp.float32)
            keep(0, k, heat, LANES - 1)
            keep(1, k, salt, LANES - 1)
            keep(2, k, spacing_y * u[k, rows, :] * face_x, LANES - 1)
            keep(3, k, ratio * face_x, LANES - 1)
            keep(4, k, heat, 0)
            keep(5, k, salt, 0)
            keep(6, k, spacing_x * v[k, rows, :] * face_y, 0)
            keep(7, k, face_y, 0)
        total = jnp.where(lane == 68, turn, 0.0)
        for n, (x, source) in enumerate([(spacing_x, LANES - 1), (spacing_y, LANES - 1), (spacing_x, 0), (spacing_y, 0)]):
            total = jnp.where(lane == 64 + n, roll_lanes(x, 64 + n - source), total)
        for field in fields:
            total = total + field
        packed[rows, :] = total
        return 0

    lax.fori_loop(0, tiles, pack, 0, unroll=True)
    turned = packed[...].T
    to_east[...] = turned[:PACKET]
    to_west[...] = turned[PACKET : 2 * PACKET]
    own[...] = turned[: own.shape[0]]

    def heads(r, _):
        source = pl.ds(pl.multiple_of(r * TILE, TILE), TILE)
        rows = pl.ds(pl.multiple_of(r * TILE + TILE, TILE), TILE)
        head = jnp.zeros((TILE, LANES), jnp.float32)
        for k in range(LEVELS):
            half = (0.5 * THICK[k]) * density(t[k, source, :], s[k, source, :], k)
            p_ext[k, rows, :] = head + half
            head = head + 2.0 * half
        return 0

    lax.fori_loop(0, tiles, heads, 0, unroll=4)

    def faces(r, _, last=False):
        source = pl.ds(pl.multiple_of(r * TILE, TILE), TILE)
        rows = pl.ds(pl.multiple_of(r * TILE + TILE, TILE), TILE)
        above = pl.ds(r * TILE + 1, TILE)
        spacing_x, spacing_y = e1[source, :], e2[source, :]
        ratio = LATERAL * spacing_x / spacing_y
        for k in range(LEVELS):
            flux_x = spacing_y * u[k, source, :] * zf[k, source, :].astype(jnp.float32)
            u_ext[k, rows, :] = flux_x
            a_ext[k, rows, :] = flux_x + from_west(flux_x)
            face = mf[k, source, :].astype(jnp.float32)
            flux_y = spacing_x * v[k, source, :] * face
            v_ext[k, rows, :] = flux_y
            b_ext[k, rows, :] = flux_y + from_east(flux_y)
            if not last:
                here, there = 0.5 * flux_y + ratio * face, 0.5 * flux_y - ratio * face
                ft_ext[k, rows, :] = here * t[k, source, :] + there * t[k, above, :]
                fs_ext[k, rows, :] = here * s[k, source, :] + there * s[k, above, :]
        return 0

    lax.fori_loop(0, tiles - 1, faces, 0, unroll=3)
    faces(tiles - 1, 0, last=True)
    update = tile_update(
        t, s, u, v, zf, mf, count, e1, e2, coriolis, p_ext, a_ext, b_ext, u_ext, v_ext, ft_ext, fs_ext,
        t_out, s_out, u_out, v_out, None,
    )
    lax.fori_loop(1, EARLY, update, 0, unroll=3)


def corner_pack(from_a, from_b, to_east, to_west, to_a, to_b):
    even_j = lax.axis_index("lat") % 2 == 0
    even_i = lax.axis_index("lon") % 2 == 0
    shape = (PACKET, LANES)
    row = lax.broadcasted_iota(jnp.int32, shape, 0)
    corner = (lane_index(shape) == 96) & (row >= 2 * LEVELS) & (row < 3 * LEVELS)
    first, second = from_a[...], from_b[...]
    north = jnp.where(even_j, first, second)
    south = jnp.where(even_j, second, first)
    top = lax.axis_index("lat") == lax.axis_size("lat") - 1
    last_north = jnp.where(top, roll_lanes(north, 96), roll_lanes(north, 96 - (LANES - 1)))
    east = jnp.where(corner, last_north, to_east[...])
    west = jnp.where(corner, roll_lanes(south, 96), to_west[...])
    to_a[...] = jnp.where(even_i, east, west)
    to_b[...] = jnp.where(even_i, west, east)


def middle(
    t, s, u, v, zf, mf, count, e1, e2, coriolis, p_ext, a_ext, b_ext, u_ext, v_ext, ft_ext, fs_ext, lat_a, lat_b,
    t_out, s_out, u_out, v_out, beyond,
):
    lines = t.shape[1]
    tiles = lines // TILE
    even_j = lax.axis_index("lat") % 2 == 0

    def pick(ref_true, ref_false, flag, number):
        rows = slice(number * LEVELS, (number + 1) * LEVELS)
        return jnp.where(flag, ref_true[rows, :], ref_false[rows, :])

    lane = lane_index((LEVELS, LANES))
    source = jnp.where(lax.axis_index("lat") == lax.axis_size("lat") - 1, LANES - 1 - lane, lane)
    north = [jnp.take_along_axis(pick(lat_a, lat_b, even_j, n), source, axis=1) for n in range(3)]
    south = [pick(lat_b, lat_a, even_j, n) for n in range(4)]
    here, there = 0.5 * south[2] + south[3], 0.5 * south[2] - south[3]
    beyond[0] = north[0]
    beyond[1] = north[1]
    beyond[2] = north[2] + from_west(north[2])
    beyond[4] = south[2] + from_east(south[2])
    beyond[5] = south[2]
    beyond[6] = here * south[0] + there * t[:, 0, :]
    beyond[7] = here * south[1] + there * s[:, 0, :]
    head = jnp.zeros((1, LANES), jnp.float32)
    for k in range(LEVELS):
        half = (0.5 * THICK[k]) * density(beyond[0, k : k + 1, :], beyond[1, k : k + 1, :], k)
        beyond[3, k : k + 1, :] = head + half
        head = head + 2.0 * half

    update = tile_update(
        t, s, u, v, zf, mf, count, e1, e2, coriolis, p_ext, a_ext, b_ext, u_ext, v_ext, ft_ext, fs_ext,
        t_out, s_out, u_out, v_out, beyond,
    )
    update(0, 0, first=True)
    lax.fori_loop(EARLY, tiles - 1, update, 0, unroll=2)
    update(tiles - 1, 0, last=True)


def running_sum(x, level, upward):
    for step in (1, 2, 4):
        if upward:
            x = x + jnp.where(level < LEVELS - step, pltpu.roll(x, LEVELS - step, 0), 0.0)
        else:
            x = x + jnp.where(level >= step, pltpu.roll(x, step, 0), 0.0)
    return x


def finish(t_early, s_early, u_early, v_early, t_part, s_part, u_part, v_part, count, own, lon_b, lon_a, t_out, s_out, u_out, v_out, turned, sides, *buffers_and_done):
    buffers, done = buffers_and_done[:4], buffers_and_done[4]
    lines = t_part.shape[1]
    even_i = lax.axis_index("lon") % 2 == 0

    def part(ref, number):
        return ref[number * LEVELS : (number + 1) * LEVELS, :]

    t_east, s_east, v_east = [jnp.where(even_i, part(lon_a, 4 + n), part(lon_b, n)) for n in range(3)]
    t_west, s_west, u_west, g_west = [jnp.where(even_i, part(lon_b, n), part(lon_a, n)) for n in range(4)]
    shape = (LEVELS, LANES)
    level, lane = lax.broadcasted_iota(jnp.int32, shape, 0), lane_index(shape)
    depth_index = level.astype(jnp.float32)
    thick = 6.0 + 4.0 * depth_index
    depth = 2.0 * depth_index * depth_index + 6.0 * depth_index + 3.0

    def mine(number):
        return own[number * LEVELS : (number + 1) * LEVELS, :]

    def single(number):
        return own[64 + number : 65 + number, :]

    u_last, g_last, t_first, s_first, face_first = mine(2), mine(3), mine(4), mine(5), mine(7)
    turn = (0.25 * TIME_STEP) * single(4)
    push = -TIME_STEP * GRAVITY / REFERENCE_DENSITY
    inverse_x, inverse_y = 1.0 / single(0), 1.0 / single(1)
    back = -(TIME_STEP * inverse_x * inverse_y) * (0.5 * u_last - g_last)
    anom_t, anom_s = t_east - 10.0, s_east - 35.0
    weight = 0.5 * thick * (
        (-0.1655 * (1.0 + 0.0001497 * depth) + (-0.1655 * 0.5 * 0.05952) * anom_t - 0.0024341 * anom_s) * anom_t
        + (0.76554 * (1.0 - 1.109e-05 * depth) - (0.76554 * 0.5 * 0.00054914) * anom_s) * anom_s
    )
    head = 2.0 * running_sum(weight, level, False) - weight
    v_south_east = jnp.where(lane == 0, roll_lanes(v_east, -lines), roll_lanes(v_east, 1))
    u_add = jnp.where(g_last > 0.0, (push * inverse_x) * head + (turn * inverse_x) * (v_east + v_south_east), 0.0)
    turned[...] = jnp.zeros_like(turned)
    turned[pl.ds(0, LEVELS, 2), :] = back * t_east
    turned[pl.ds(16, LEVELS, 2), :] = back * s_east
    turned[pl.ds(32, LEVELS, 2), :] = u_add
    inverse_x, inverse_y = 1.0 / single(2), 1.0 / single(3)
    scale = -(TIME_STEP * inverse_x * inverse_y)
    here, there = 0.5 * u_west + g_west, 0.5 * u_west - g_west
    upward = running_sum(0.5 * thick * u_west, level, True)

    def first_column(q_west, q):
        flux = upward * (q + jnp.where(level == 0, q, pltpu.roll(q, 1, 0)))
        under = jnp.where(level == LEVELS - 1, 0.0, pltpu.roll(flux, LEVELS - 1, 0))
        return scale * ((flux - under) / thick - (here * q_west + there * q))

    turned[pl.ds(1, LEVELS, 2), :] = first_column(t_west, t_first)
    turned[pl.ds(17, LEVELS, 2), :] = first_column(s_west, s_first)
    turned[pl.ds(33, LEVELS, 2), :] = -(turn * inverse_y) * (u_west + roll_lanes(u_west, -1)) * face_first
    sides[...] = turned[...].T

    at_first, at_last = lane == 0, lane == LANES - 1
    at_side = at_first | at_last
    early, parts, outs = (t_early, s_early, u_early, v_early), (t_part, s_part, u_part, v_part), (t_out, s_out, u_out, v_out)
    chunk = lines // CHUNKS
    copies = []
    for c in range(CHUNKS):

        for r in range(c * chunk // TILE, (c + 1) * chunk // TILE):
            rows = pl.ds(r * TILE, TILE)
            side = sides[rows, :]
            levels = jnp.where(at_side, count[rows, :], 0)
            for k in range(LEVELS):
                wet = levels > k
                both = roll_lanes(side, -(2 * k + 33))
                adds = (
                    jnp.where(wet, roll_lanes(side, -(2 * k + 1)), 0.0),
                    jnp.where(wet, roll_lanes(side, -(2 * k + 17)), 0.0),
                    jnp.where(at_last, both, 0.0),
                    jnp.where(at_first, both, 0.0),
                )
                for part, add, buffer in zip(early if 1 <= r < EARLY else parts, adds, buffers):
                    buffer[k, rows, :] = part[k, rows, :] + add
        rows = pl.ds(c * chunk, chunk)
        for n in range(4):
            copy = pltpu.make_async_copy(buffers[n].at[:, rows, :], outs[n].at[:, rows, :], done.at[c * 4 + n])
            copy.start()
            copies.append(copy)
    for copy in copies:
        copy.wait()


def whole(n):
    return [pl.BlockSpec(memory_space=VMEM)] * n


def per_device(
    potential_warmth_degrees,
    dissolved_salt_content,
    zonal_edge_current,
    meridional_edge_current,
    wet_grid_flag,
    zonal_wet_edge_flag,
    meridional_wet_edge_flag,
    bottom_tier_count,
    zonal_grid_spacing,
    meridional_grid_spacing,
):
    t, s, u, v = potential_warmth_degrees, dissolved_salt_content, zonal_edge_current, meridional_edge_current
    zf, mf, e1, e2 = zonal_wet_edge_flag, meridional_wet_edge_flag, zonal_grid_spacing, meridional_grid_spacing
    lines = t.shape[1]
    lons, lats = lax.axis_size("lon"), lax.axis_size("lat")
    f32 = jnp.float32
    params = pltpu.CompilerParams(vmem_limit_bytes=24 * 1024 * 1024)
    packet = jax.ShapeDtypeStruct((PACKET, LANES), f32)
    field = jax.ShapeDtypeStruct(t.shape, f32)

    lat_to_a, lat_to_b, count = pl.pallas_call(
        row_pack,
        in_specs=[pl.BlockSpec(memory_space=pl.ANY)] * 9,
        out_specs=whole(3),
        out_shape=[packet, packet, jax.ShapeDtypeStruct(e1.shape, jnp.int32)],
        scratch_shapes=[
            VMEM((7, LEVELS, TILE, LANES), f32),
            VMEM((3, LEVELS, TILE, LANES), jnp.int32),
            VMEM((3, TILE, LANES), f32),
            pltpu.SemaphoreType.DMA((14,)),
        ],
        compiler_params=pltpu.CompilerParams(vmem_limit_bytes=4 * 1024 * 1024),
        name="row_pack",
    )(*[pltpu.with_memory_space_constraint(x, pltpu.HBM) for x in (t, s, u, v, zf, mf, e1, e2, bottom_tier_count)])

    pairs_a = [(j, j ^ 1) for j in range(lats)]
    pairs_b = []
    for i in range(lons):
        for j in range(1, lats):
            other = (lons - 1 - i) * lats + j if j == lats - 1 else i * lats + (j + 1 if j % 2 else j - 1)
            pairs_b.append((i * lats + j, other))
    lat_a = lax.ppermute(lat_to_a, "lat", pairs_a)
    lat_b = lax.ppermute(lat_to_b, ("lon", "lat"), pairs_b)

    extended = jax.ShapeDtypeStruct((LEVELS, lines + 2 * TILE, LANES), f32)
    square = VMEM((LANES, LANES), f32)
    to_east, to_west, own, coriolis, *parts = pl.pallas_call(
        front,
        in_specs=whole(9),
        out_specs=whole(15),
        out_shape=[packet, packet, jax.ShapeDtypeStruct((72, LANES), f32), jax.ShapeDtypeStruct(e1.shape, f32)] + [extended] * 7 + [field] * 4,
        scratch_shapes=[square],
        compiler_params=params,
        name="front",
    )(t, s, u, v, zf, mf, count, e1, e2)
    parts, early = parts[:7], parts[7:]

    lon_to_a, lon_to_b = pl.pallas_call(
        corner_pack,
        in_specs=whole(4),
        out_specs=whole(2),
        out_shape=[packet, packet],
        compiler_params=params,
        name="corner_pack",
    )(lat_a, lat_b, to_east, to_west)
    lon_b = lax.ppermute(lon_to_b, "lon", [(i, (i + 1 if i % 2 else i - 1) % lons) for i in range(lons)])
    lon_a = lax.all_gather(lon_to_a, "lon", axis_index_groups=[[i, i + 1] for i in range(0, lons, 2)], tiled=True)

    parts = pl.pallas_call(
        middle,
        in_specs=whole(19),
        out_specs=whole(4),
        out_shape=[field] * 4,
        scratch_shapes=[VMEM((8, LEVELS, LANES), f32)],
        compiler_params=params,
        name="middle",
    )(t, s, u, v, zf, mf, count, e1, e2, coriolis, *parts, lat_a, lat_b)

    return pl.pallas_call(
        finish,
        in_specs=whole(12),
        out_specs=[pl.BlockSpec(memory_space=pltpu.MemorySpace.HBM)] * 4,
        out_shape=[field] * 4,
        scratch_shapes=[square] * 2 + [VMEM(t.shape, f32)] * 4 + [pltpu.SemaphoreType.DMA((4 * CHUNKS,))],
        compiler_params=params,
        name="finish",
    )(*early, *parts, count, own, lon_b, lon_a)


def solution(mesh):
    deep, flat = P(None, "lat", "lon"), P("lat", "lon")
    return jax.shard_map(
        per_device,
        mesh=mesh,
        in_specs=(deep,) * 7 + (flat,) * 3,
        out_specs=(deep,) * 4,
        check_vma=False,
    )
```

```python
import functools
import math

import jax
import jax.numpy as jnp
from jax import lax
from jax.experimental import pallas as pl
from jax.experimental.pallas import tpu as pltpu
from jax.sharding import PartitionSpec as P

GRAVITY = 9.81
REFERENCE_DENSITY = 1026.0
TIME_STEP = 360.0
LATERAL = 300.0
VERTICAL = 0.001
ROTATION = 7.292e-05

LEVELS = 8
LANES = 128
TILE = 8
PACKET = 4 * LEVELS
CHUNKS = 4
EARLY = 7
VMEM = pltpu.MemorySpace.VMEM

THICK = [6.0 + 4.0 * k for k in range(LEVELS)]
DEPTH = [2.0 * k * k + 6.0 * k + 3.0 for k in range(LEVELS)]
SPACING = [4.0 * k + 4.0 for k in range(LEVELS)]


def lane_index(shape):
    return lax.broadcasted_iota(jnp.int32, shape, len(shape) - 1)


def roll_lanes(x, shift):
    return pltpu.roll(x, shift % LANES, x.ndim - 1)


def density(heat, salt, k):
    anom_t = heat - 10.0
    anom_s = salt - 35.0
    by_t = -0.1655 * (1.0 + 0.0001497 * DEPTH[k])
    by_s = 0.76554 * (1.0 - 1.109e-05 * DEPTH[k])
    along_t = by_t + (-0.1655 * 0.5 * 0.05952) * anom_t - 0.0024341 * anom_s
    along_s = by_s - (0.76554 * 0.5 * 0.00054914) * anom_s
    return along_t * anom_t + along_s * anom_s


def row_pack(t, s, u, v, zf, mf, e1, e2, bottom, to_a, to_b, count, deep, flags, flat, arrived):
    j = lax.axis_index("lat")
    even = j % 2 == 0
    top = j == lax.axis_size("lat") - 1
    last = TILE - 1
    low, high = pl.ds(0, TILE), pl.ds(t.shape[1] - TILE, TILE)
    wanted = [(t, low), (t, high), (s, low), (s, high), (u, low), (u, high), (v, high)]
    marks = [(zf, low), (zf, high), (mf, high)]
    sizes = [(e1, high), (e2, high), (e2, low)]
    copies = [pltpu.make_async_copy(ref.at[:, rows, :], deep.at[n], arrived.at[n]) for n, (ref, rows) in enumerate(wanted)]
    copies += [pltpu.make_async_copy(ref.at[:, rows, :], flags.at[n], arrived.at[7 + n]) for n, (ref, rows) in enumerate(marks)]
    copies += [pltpu.make_async_copy(ref.at[rows, :], flat.at[n], arrived.at[10 + n]) for n, (ref, rows) in enumerate(sizes)]
    copies.append(pltpu.make_async_copy(bottom, count, arrived.at[13]))
    for copy in copies:
        copy.start()
    for copy in copies:
        copy.wait()

    def put(out, fields):
        for number, field in enumerate(fields):
            out[number * LEVELS : (number + 1) * LEVELS, :] = field

    def upward():
        spacing_x, spacing_y = flat[0, last:, :], flat[1, last:, :]
        face = flags[2, :, last, :].astype(jnp.float32)
        return [
            deep[1, :, last, :],
            deep[3, :, last, :],
            spacing_x * deep[6, :, last, :] * face,
            LATERAL * spacing_x / spacing_y * face,
        ]

    def downward():
        flux = flat[2, :1, :] * deep[4, :, 0, :] * flags[0, :, 0, :].astype(jnp.float32)
        return [deep[0, :, 0, :], deep[2, :, 0, :], flux, jnp.zeros_like(flux)]

    @pl.when(even)
    def _():
        put(to_a, upward())
        put(to_b, downward())

    @pl.when(jnp.logical_not(even))
    def _():
        put(to_a, downward())

    @pl.when(jnp.logical_not(even) & jnp.logical_not(top))
    def _():
        put(to_b, upward())

    @pl.when(top)
    def _():
        flux = flat[1, last:, :] * deep[5, :, last, :] * flags[1, :, last, :].astype(jnp.float32)
        put(to_b, [deep[1, :, last, :], deep[3, :, last, :], -flux, jnp.zeros_like(flux)])


def from_west(x):
    return jnp.where(lane_index(x.shape) == 0, 0.0, roll_lanes(x, 1))


def from_east(x):
    return jnp.where(lane_index(x.shape) == LANES - 1, 0.0, roll_lanes(x, -1))


def tile_update(
    t, s, u, v, zf, mf, count, e1, e2, coriolis, p_ext, a_ext, b_ext, u_ext, v_ext, ft_ext, fs_ext,
    t_out, s_out, u_out, v_out, beyond,
):
    row = lax.broadcasted_iota(jnp.int32, (TILE, LANES), 0)

    def update(r, _, first=False, last=False):
        source = pl.ds(pl.multiple_of(r * TILE, TILE), TILE)
        rows = pl.ds(pl.multiple_of(r * TILE + TILE, TILE), TILE)
        spacing_x, spacing_y = e1[source, :], e2[source, :]
        levels = count[source, :]
        inverse_x, inverse_y = 1.0 / spacing_x, 1.0 / spacing_y
        ratio_x, ratio_y = LATERAL * spacing_y * inverse_x, LATERAL * spacing_x * inverse_y
        area = spacing_x * spacing_y
        per_area = TIME_STEP * inverse_x * inverse_y
        turn = (0.25 * TIME_STEP) * coriolis[source, :]
        turn_x, turn_y = turn * inverse_x, turn * inverse_y
        push = -TIME_STEP * GRAVITY / REFERENCE_DENSITY
        push_x, push_y = push * inverse_x, push * inverse_y
        zero = jnp.zeros((TILE, LANES), jnp.float32)

        def above(ref, k, number, offset=TILE):
            if last:
                return jnp.where(row == TILE - 1, beyond[number, k : k + 1, :], pltpu.roll(ref[k, pl.ds(r * TILE + offset, TILE), :], TILE - 1, 0))
            return ref[k, pl.ds(r * TILE + offset + 1, TILE), :]

        def below(ref, k, number):
            if first:
                return jnp.where(row == 0, beyond[number, k : k + 1, :], pltpu.roll(ref[k, rows, :], 1, 0))
            return ref[k, pl.ds(r * TILE + TILE - 1, TILE), :]

        upward, t_below, s_below, u_below, v_below = zero, zero, zero, zero, zero
        for k in reversed(range(LEVELS)):
            heat, salt = t[k, source, :], s[k, source, :]
            flux_x, flux_y = u_ext[k, rows, :], v_ext[k, rows, :]
            face_x, face_y = zf[k, source, :].astype(jnp.float32), mf[k, source, :].astype(jnp.float32)
            both_x, both_y = a_ext[k, rows, :], b_ext[k, rows, :]
            wet = levels > k
            spread = ratio_x * face_x
            here, there = 0.5 * flux_x + spread, 0.5 * flux_x - spread
            t_east = here * heat + there * from_east(heat)
            s_east = here * salt + there * from_east(salt)
            if last:
                here, there = 0.5 * flux_y + ratio_y * face_y, 0.5 * flux_y - ratio_y * face_y
                t_north, s_north = here * heat + there * above(t, k, 0, 0), here * salt + there * above(s, k, 1, 0)
                under = pl.ds(r * TILE + TILE - 1, 1)
                t_south = jnp.where(row == 0, ft_ext[k, under, :], pltpu.roll(t_north, 1, 0))
                s_south = jnp.where(row == 0, fs_ext[k, under, :], pltpu.roll(s_north, 1, 0))
            else:
                t_north, s_north = ft_ext[k, rows, :], fs_ext[k, rows, :]
                t_south, s_south = below(ft_ext, k, 6), below(fs_ext, k, 7)
            t_net = t_east - from_west(t_east) + t_north - t_south
            s_net = s_east - from_west(s_east) + s_north - s_south
            converge = 2.0 * flux_x - both_x + flux_y - below(v_ext, k, 5)
            upward = upward - THICK[k] * converge
            if k > 0:
                mix = jnp.where(wet, (VERTICAL / SPACING[k]) * area, 0.0)
                upper, lower = 0.5 * upward - mix, 0.5 * upward + mix
                t_above = upper * t[k - 1, source, :] + lower * heat
                s_above = upper * s[k - 1, source, :] + lower * salt
            else:
                t_above, s_above = upward * heat, upward * salt
            t_net = t_net + (t_above - t_below) * (1.0 / THICK[k])
            s_net = s_net + (s_above - s_below) * (1.0 / THICK[k])
            t_below, s_below = t_above, s_above
            t_out[k, source, :] = jnp.where(wet, heat - per_area * t_net, 0.0)
            s_out[k, source, :] = jnp.where(wet, salt - per_area * s_net, 0.0)
            zonal, meridional = u[k, source, :], v[k, source, :]
            if k > 0:
                u_above = (VERTICAL / SPACING[k]) * (u[k - 1, source, :] - zonal) * face_x
                v_above = (VERTICAL / SPACING[k]) * (v[k - 1, source, :] - meridional) * face_y
            else:
                u_above, v_above = zero, zero
            head = p_ext[k, rows, :]
            slope_x = from_east(head) - head
            slope_y = above(p_ext, k, 3) - head
            share = TIME_STEP / THICK[k]
            u_out[k, source, :] = (
                zonal + push_x * slope_x + turn_x * (both_y + below(b_ext, k, 4)) + share * (u_above - u_below)
            ) * face_x
            v_out[k, source, :] = (
                meridional + push_y * slope_y - turn_y * (both_x + above(a_ext, k, 2)) + share * (v_above - v_below)
            ) * face_y
            u_below, v_below = u_above, v_above
        return 0

    return update


def front(
    t, s, u, v, zf, mf, count, e1, e2,
    to_east, to_west, own, coriolis, p_ext, a_ext, b_ext, u_ext, v_ext, ft_ext, fs_ext,
    t_out, s_out, u_out, v_out, packed,
):
    lines = t.shape[1]
    tiles = lines // TILE
    lane = lane_index((TILE, LANES))
    first_row = lax.axis_index("lat") * lines
    total_rows = lines * lax.axis_size("lat")
    packed[pl.ds(lines, LANES - lines), :] = jnp.zeros((LANES - lines, LANES), jnp.float32)

    def pack(r, _):
        rows = pl.ds(pl.multiple_of(r * TILE, TILE), TILE)
        spacing_x, spacing_y = e1[rows, :], e2[rows, :]
        ratio = LATERAL * spacing_y / spacing_x
        row = (first_row + r * TILE + lax.broadcasted_iota(jnp.int32, (TILE, LANES), 0)).astype(jnp.float32)
        latitude = 10.0 + 78.0 * (row + 0.5) / total_rows
        turn = 2.0 * ROTATION * jnp.sin(latitude * (math.pi / 180.0))
        coriolis[rows, :] = turn
        fields = [jnp.zeros((TILE, LANES), jnp.float32) for _ in range(7)]

        def keep(number, k, x, source):
            target = number * LEVELS + k
            fields[number] = jnp.where(lane == target, roll_lanes(x, target - source), fields[number])

        for k in range(LEVELS):
            heat, salt = t[k, rows, :], s[k, rows, :]
            face_x, face_y = zf[k, rows, :].astype(jnp.float32), mf[k, rows, :].astype(jnp.float32)
            keep(0, k, heat, LANES - 1)
            keep(1, k, salt, LANES - 1)
            keep(2, k, spacing_y * u[k, rows, :] * face_x, LANES - 1)
            keep(3, k, ratio * face_x, LANES - 1)
            keep(4, k, heat, 0)
            keep(5, k, salt, 0)
            keep(6, k, spacing_x * v[k, rows, :] * face_y, 0)
        total = jnp.where(lane == 68, turn, 0.0)
        for n, (x, source) in enumerate([(spacing_x, LANES - 1), (spacing_y, LANES - 1), (spacing_x, 0), (spacing_y, 0)]):
            total = jnp.where(lane == 64 + n, roll_lanes(x, 64 + n - source), total)
        for field in fields:
            total = total + field
        packed[rows, :] = total
        return 0

    lax.fori_loop(0, tiles, pack, 0, unroll=True)
    turned = packed[...].T
    to_east[...] = turned[:PACKET]
    to_west[...] = turned[PACKET : 2 * PACKET]
    own[...] = turned[: own.shape[0]]

    def heads(r, _):
        source = pl.ds(pl.multiple_of(r * TILE, TILE), TILE)
        rows = pl.ds(pl.multiple_of(r * TILE + TILE, TILE), TILE)
        head = jnp.zeros((TILE, LANES), jnp.float32)
        for k in range(LEVELS):
            half = (0.5 * THICK[k]) * density(t[k, source, :], s[k, source, :], k)
            p_ext[k, rows, :] = head + half
            head = head + 2.0 * half
        return 0

    lax.fori_loop(0, tiles, heads, 0, unroll=4)

    def faces(r, _, last=False):
        source = pl.ds(pl.multiple_of(r * TILE, TILE), TILE)
        rows = pl.ds(pl.multiple_of(r * TILE + TILE, TILE), TILE)
        above = pl.ds(r * TILE + 1, TILE)
        spacing_x, spacing_y = e1[source, :], e2[source, :]
        ratio = LATERAL * spacing_x / spacing_y
        for k in range(LEVELS):
            flux_x = spacing_y * u[k, source, :] * zf[k, source, :].astype(jnp.float32)
            u_ext[k, rows, :] = flux_x
            a_ext[k, rows, :] = flux_x + from_west(flux_x)
            face = mf[k, source, :].astype(jnp.float32)
            flux_y = spacing_x * v[k, source, :] * face
            v_ext[k, rows, :] = flux_y
            b_ext[k, rows, :] = flux_y + from_east(flux_y)
            if not last:
                here, there = 0.5 * flux_y + ratio * face, 0.5 * flux_y - ratio * face
                ft_ext[k, rows, :] = here * t[k, source, :] + there * t[k, above, :]
                fs_ext[k, rows, :] = here * s[k, source, :] + there * s[k, above, :]
        return 0

    lax.fori_loop(0, tiles - 1, faces, 0, unroll=3)
    faces(tiles - 1, 0, last=True)
    update = tile_update(
        t, s, u, v, zf, mf, count, e1, e2, coriolis, p_ext, a_ext, b_ext, u_ext, v_ext, ft_ext, fs_ext,
        t_out, s_out, u_out, v_out, None,
    )
    lax.fori_loop(1, EARLY, update, 0, unroll=3)


def corner_pack(from_a, from_b, to_east, to_west, to_a, to_b):
    even_j = lax.axis_index("lat") % 2 == 0
    even_i = lax.axis_index("lon") % 2 == 0
    shape = (PACKET, LANES)
    row = lax.broadcasted_iota(jnp.int32, shape, 0)
    corner = (lane_index(shape) == 96) & (row >= 2 * LEVELS) & (row < 3 * LEVELS)
    first, second = from_a[...], from_b[...]
    north = jnp.where(even_j, first, second)
    south = jnp.where(even_j, second, first)
    top = lax.axis_index("lat") == lax.axis_size("lat") - 1
    last_north = jnp.where(top, roll_lanes(north, 96), roll_lanes(north, 96 - (LANES - 1)))
    east = jnp.where(corner, last_north, to_east[...])
    west = jnp.where(corner, roll_lanes(south, 96), to_west[...])
    to_a[...] = jnp.where(even_i, east, west)
    to_b[...] = jnp.where(even_i, west, east)


def middle(
    t, s, u, v, zf, mf, count, e1, e2, coriolis, p_ext, a_ext, b_ext, u_ext, v_ext, ft_ext, fs_ext, lat_a, lat_b,
    t_out, s_out, u_out, v_out, beyond,
):
    lines = t.shape[1]
    tiles = lines // TILE
    even_j = lax.axis_index("lat") % 2 == 0

    def pick(ref_true, ref_false, flag, number):
        rows = slice(number * LEVELS, (number + 1) * LEVELS)
        return jnp.where(flag, ref_true[rows, :], ref_false[rows, :])

    lane = lane_index((LEVELS, LANES))
    source = jnp.where(lax.axis_index("lat") == lax.axis_size("lat") - 1, LANES - 1 - lane, lane)
    north = [jnp.take_along_axis(pick(lat_a, lat_b, even_j, n), source, axis=1) for n in range(3)]
    south = [pick(lat_b, lat_a, even_j, n) for n in range(4)]
    here, there = 0.5 * south[2] + south[3], 0.5 * south[2] - south[3]
    beyond[0] = north[0]
    beyond[1] = north[1]
    beyond[2] = north[2] + from_west(north[2])
    beyond[4] = south[2] + from_east(south[2])
    beyond[5] = south[2]
    beyond[6] = here * south[0] + there * t[:, 0, :]
    beyond[7] = here * south[1] + there * s[:, 0, :]
    head = jnp.zeros((1, LANES), jnp.float32)
    for k in range(LEVELS):
        half = (0.5 * THICK[k]) * density(beyond[0, k : k + 1, :], beyond[1, k : k + 1, :], k)
        beyond[3, k : k + 1, :] = head + half
        head = head + 2.0 * half

    update = tile_update(
        t, s, u, v, zf, mf, count, e1, e2, coriolis, p_ext, a_ext, b_ext, u_ext, v_ext, ft_ext, fs_ext,
        t_out, s_out, u_out, v_out, beyond,
    )
    update(0, 0, first=True)
    lax.fori_loop(EARLY, tiles - 1, update, 0, unroll=2)
    update(tiles - 1, 0, last=True)


def running_sum(x, level, upward):
    for step in (1, 2, 4):
        if upward:
            x = x + jnp.where(level < LEVELS - step, pltpu.roll(x, LEVELS - step, 0), 0.0)
        else:
            x = x + jnp.where(level >= step, pltpu.roll(x, step, 0), 0.0)
    return x


def finish(t_early, s_early, u_early, v_early, t_part, s_part, u_part, v_part, count, mf, own, lon_b, lon_a, t_out, s_out, u_out, v_out, turned, sides, *buffers_and_done):
    buffers, done = buffers_and_done[:4], buffers_and_done[4]
    lines = t_part.shape[1]
    even_i = lax.axis_index("lon") % 2 == 0

    def part(ref, number):
        return ref[number * LEVELS : (number + 1) * LEVELS, :]

    t_east, s_east, v_east = [jnp.where(even_i, part(lon_a, 4 + n), part(lon_b, n)) for n in range(3)]
    t_west, s_west, u_west, g_west = [jnp.where(even_i, part(lon_b, n), part(lon_a, n)) for n in range(4)]
    shape = (LEVELS, LANES)
    level, lane = lax.broadcasted_iota(jnp.int32, shape, 0), lane_index(shape)
    depth_index = level.astype(jnp.float32)
    thick = 6.0 + 4.0 * depth_index
    depth = 2.0 * depth_index * depth_index + 6.0 * depth_index + 3.0

    def mine(number):
        return own[number * LEVELS : (number + 1) * LEVELS, :]

    def single(number):
        return own[64 + number : 65 + number, :]

    u_last, g_last, t_first, s_first = mine(2), mine(3), mine(4), mine(5)
    turn = (0.25 * TIME_STEP) * single(4)
    push = -TIME_STEP * GRAVITY / REFERENCE_DENSITY
    inverse_x, inverse_y = 1.0 / single(0), 1.0 / single(1)
    back = -(TIME_STEP * inverse_x * inverse_y) * (0.5 * u_last - g_last)
    anom_t, anom_s = t_east - 10.0, s_east - 35.0
    weight = 0.5 * thick * (
        (-0.1655 * (1.0 + 0.0001497 * depth) + (-0.1655 * 0.5 * 0.05952) * anom_t - 0.0024341 * anom_s) * anom_t
        + (0.76554 * (1.0 - 1.109e-05 * depth) - (0.76554 * 0.5 * 0.00054914) * anom_s) * anom_s
    )
    head = 2.0 * running_sum(weight, level, False) - weight
    v_south_east = jnp.where(lane == 0, roll_lanes(v_east, -lines), roll_lanes(v_east, 1))
    u_add = jnp.where(g_last > 0.0, (push * inverse_x) * head + (turn * inverse_x) * (v_east + v_south_east), 0.0)
    turned[...] = jnp.zeros_like(turned)
    turned[pl.ds(0, LEVELS, 2), :] = back * t_east
    turned[pl.ds(16, LEVELS, 2), :] = back * s_east
    turned[pl.ds(32, LEVELS, 2), :] = u_add
    inverse_x, inverse_y = 1.0 / single(2), 1.0 / single(3)
    scale = -(TIME_STEP * inverse_x * inverse_y)
    here, there = 0.5 * u_west + g_west, 0.5 * u_west - g_west
    upward = running_sum(0.5 * thick * u_west, level, True)

    def first_column(q_west, q):
        flux = upward * (q + jnp.where(level == 0, q, pltpu.roll(q, 1, 0)))
        under = jnp.where(level == LEVELS - 1, 0.0, pltpu.roll(flux, LEVELS - 1, 0))
        return scale * ((flux - under) / thick - (here * q_west + there * q))

    turned[pl.ds(1, LEVELS, 2), :] = first_column(t_west, t_first)
    turned[pl.ds(17, LEVELS, 2), :] = first_column(s_west, s_first)
    turned[pl.ds(33, LEVELS, 2), :] = -(turn * inverse_y) * (u_west + roll_lanes(u_west, -1))
    sides[...] = turned[...].T

    at_first, at_last = lane == 0, lane == LANES - 1
    at_side = at_first | at_last
    early, parts, outs = (t_early, s_early, u_early, v_early), (t_part, s_part, u_part, v_part), (t_out, s_out, u_out, v_out)
    chunk = lines // CHUNKS
    copies = []
    for c in range(CHUNKS):

        for r in range(c * chunk // TILE, (c + 1) * chunk // TILE):
            rows = pl.ds(r * TILE, TILE)
            side = sides[rows, :]
            levels = jnp.where(at_side, count[rows, :], 0)
            for k in range(LEVELS):
                wet = levels > k
                both = roll_lanes(side, -(2 * k + 33))
                adds = (
                    jnp.where(wet, roll_lanes(side, -(2 * k + 1)), 0.0),
                    jnp.where(wet, roll_lanes(side, -(2 * k + 17)), 0.0),
                    jnp.where(at_last, both, 0.0),
                    jnp.where(at_first & (mf[k, rows, :] > 0), both, 0.0),
                )
                for part, add, buffer in zip(early if 1 <= r < EARLY else parts, adds, buffers):
                    buffer[k, rows, :] = part[k, rows, :] + add
        rows = pl.ds(c * chunk, chunk)
        for n in range(4):
            copy = pltpu.make_async_copy(buffers[n].at[:, rows, :], outs[n].at[:, rows, :], done.at[c * 4 + n])
            copy.start()
            copies.append(copy)
    for copy in copies:
        copy.wait()


def whole(n):
    return [pl.BlockSpec(memory_space=VMEM)] * n


def per_device(
    potential_warmth_degrees,
    dissolved_salt_content,
    zonal_edge_current,
    meridional_edge_current,
    wet_grid_flag,
    zonal_wet_edge_flag,
    meridional_wet_edge_flag,
    bottom_tier_count,
    zonal_grid_spacing,
    meridional_grid_spacing,
):
    t, s, u, v = potential_warmth_degrees, dissolved_salt_content, zonal_edge_current, meridional_edge_current
    zf, mf, e1, e2 = zonal_wet_edge_flag, meridional_wet_edge_flag, zonal_grid_spacing, meridional_grid_spacing
    lines = t.shape[1]
    lons, lats = lax.axis_size("lon"), lax.axis_size("lat")
    f32 = jnp.float32
    params = pltpu.CompilerParams(vmem_limit_bytes=24 * 1024 * 1024)
    packet = jax.ShapeDtypeStruct((PACKET, LANES), f32)
    field = jax.ShapeDtypeStruct(t.shape, f32)

    lat_to_a, lat_to_b, count = pl.pallas_call(
        row_pack,
        in_specs=[pl.BlockSpec(memory_space=pl.ANY)] * 9,
        out_specs=whole(3),
        out_shape=[packet, packet, jax.ShapeDtypeStruct(e1.shape, jnp.int32)],
        scratch_shapes=[
            VMEM((7, LEVELS, TILE, LANES), f32),
            VMEM((3, LEVELS, TILE, LANES), jnp.int32),
            VMEM((3, TILE, LANES), f32),
            pltpu.SemaphoreType.DMA((14,)),
        ],
        compiler_params=pltpu.CompilerParams(vmem_limit_bytes=4 * 1024 * 1024),
        name="row_pack",
    )(*[pltpu.with_memory_space_constraint(x, pltpu.HBM) for x in (t, s, u, v, zf, mf, e1, e2, bottom_tier_count)])

    pairs_a = [(j, j ^ 1) for j in range(lats)]
    pairs_b = []
    for i in range(lons):
        for j in range(1, lats):
            other = (lons - 1 - i) * lats + j if j == lats - 1 else i * lats + (j + 1 if j % 2 else j - 1)
            pairs_b.append((i * lats + j, other))
    lat_a = lax.ppermute(lat_to_a, "lat", pairs_a)
    lat_b = lax.ppermute(lat_to_b, ("lon", "lat"), pairs_b)

    extended = jax.ShapeDtypeStruct((LEVELS, lines + 2 * TILE, LANES), f32)
    square = VMEM((LANES, LANES), f32)
    to_east, to_west, own, coriolis, *parts = pl.pallas_call(
        front,
        in_specs=whole(9),
        out_specs=whole(15),
        out_shape=[packet, packet, jax.ShapeDtypeStruct((72, LANES), f32), jax.ShapeDtypeStruct(e1.shape, f32)] + [extended] * 7 + [field] * 4,
        scratch_shapes=[square],
        compiler_params=params,
        name="front",
    )(t, s, u, v, zf, mf, count, e1, e2)
    parts, early = parts[:7], parts[7:]

    lon_to_a, lon_to_b = pl.pallas_call(
        corner_pack,
        in_specs=whole(4),
        out_specs=whole(2),
        out_shape=[packet, packet],
        compiler_params=params,
        name="corner_pack",
    )(lat_a, lat_b, to_east, to_west)
    lon_b = lax.ppermute(lon_to_b, "lon", [(i, (i + 1 if i % 2 else i - 1) % lons) for i in range(lons)])
    lon_a = lax.all_gather(lon_to_a, "lon", axis_index_groups=[[i, i + 1] for i in range(0, lons, 2)], tiled=True)

    parts = pl.pallas_call(
        middle,
        in_specs=whole(19),
        out_specs=whole(4),
        out_shape=[field] * 4,
        scratch_shapes=[VMEM((8, LEVELS, LANES), f32)],
        compiler_params=params,
        name="middle",
    )(t, s, u, v, zf, mf, count, e1, e2, coriolis, *parts, lat_a, lat_b)

    return pl.pallas_call(
        finish,
        in_specs=whole(13),
        out_specs=[pl.BlockSpec(memory_space=pltpu.MemorySpace.HBM)] * 4,
        out_shape=[field] * 4,
        scratch_shapes=[square] * 2 + [VMEM(t.shape, f32)] * 4 + [pltpu.SemaphoreType.DMA((4 * CHUNKS,))],
        compiler_params=params,
        name="finish",
    )(*early, *parts, count, mf, own, lon_b, lon_a)


def solution(mesh):
    deep, flat = P(None, "lat", "lon"), P("lat", "lon")
    return jax.shard_map(
        per_device,
        mesh=mesh,
        in_specs=(deep,) * 7 + (flat,) * 3,
        out_specs=(deep,) * 4,
        check_vma=False,
    )
```
